32 devices in a mesh: dp: 16 (over z, x, core), tensor: 2 (over y).
Axes of the slice: x: 2, y: 2, z: 4, core: 2. Of those that a mesh axis runs over, the one named last changes fastest.
Arguments:
- block_in: bfloat16 [32, 256, 768], P('dp'), may hold values from -7.2 to 7.2
- out_grad: bfloat16 [32, 256, 768], P('dp'), may hold values from -6 to 6
- segments: int32 [32, 256], P('dp'), may hold values from 0 to 3, never falling along the last dimension, each value on 1 to 128 neighbouring positions
- weights: float32 [2, 2, 3538944], P(None, 'tensor', 'dp'), may hold values from -0.57735027 to 0.57735027
- weights_first: float32 [2, 2, 3538944], P(None, 'tensor', 'dp'), may hold values from -0.00390625 to 0.00390625
- weights_second: float32 [2, 2, 3538944], P(None, 'tensor', 'dp'), may hold values from 7.064254e-08 to 2.8257017e-07
- split_vectors: float32 [2, 2, 2304], P(None, 'tensor', 'dp'), may hold values from -1.2 to 1.2
- split_first: float32 [2, 2, 2304], P(None, 'tensor', 'dp'), may hold values from -0.01171875 to 0.01171875
- split_second: float32 [2, 2, 2304], P(None, 'tensor', 'dp'), may hold values from 6.357829e-07 to 2.5431316e-06
- rep_vectors: float32 [2, 6, 768], P(None, None, 'dp'), may hold values from -0.9 to 2.2
- rep_first: float32 [2, 6, 768], P(None, None, 'dp'), may hold values from -0.01171875 to 0.01171875
- rep_second: float32 [2, 6, 768], P(None, None, 'dp'), may hold values from 6.357829e-07 to 2.5431316e-06
Outputs:
- block_out: bfloat16 [32, 256, 768], P('dp')
- input_grad: float32 [32, 256, 768], P('dp')
- grad_norm: float32 [], replicated
- new_weights: float32 [2, 2, 3538944], P(None, 'tensor', 'dp')
- weights_first_new: float32 [2, 2, 3538944], P(None, 'tensor', 'dp')
- weights_second_new: float32 [2, 2, 3538944], P(None, 'tensor', 'dp')
- weights_low: bfloat16 [2, 2, 3538944], P(None, 'tensor', 'dp')
- new_split: float32 [2, 2, 2304], P(None, 'tensor', 'dp')
- split_first_new: float32 [2, 2, 2304], P(None, 'tensor', 'dp')
- split_second_new: float32 [2, 2, 2304], P(None, 'tensor', 'dp')
- split_low: bfloat16 [2, 2, 2304], P(None, 'tensor', 'dp')
- new_rep: float32 [2, 6, 768], P(None, None, 'dp')
- rep_first_new: float32 [2, 6, 768], P(None, None, 'dp')
- rep_second_new: float32 [2, 6, 768], P(None, None, 'dp')
- rep_low: bfloat16 [2, 6, 768], P(None, None, 'dp')
- output_bias_grad: float32 [2, 768], P(None, 'dp')
The draws below stay inside these ranges and needn't reach their ends.
Inputs may be any that keep to these rules, and one draw needn't show every extreme that they name: `segments`: segment numbers never fall along a row.
All inputs are finite; a program needn't handle non-finite values.
Results may differ from the reference program's by a relative error of at most 0.038.
Values may be sent and summed in bfloat16 or wider, within the bound.
No kernel may reach another device: no remote copies, remote signals or barrier semaphores. Data moves between devices by JAX's collectives and lax.ppermute only.
A program may use at most 192 MiB of HBM per device.

```python
import math
import jax
import jax.numpy as jnp
import numpy as np
from jax import lax

D = 768
HEAD_DIM = 64
FF = 3072
LAYERS = 2
SEQ = 256
DOCS = 4
STEP = 3
ROWS = 32
HD_T = 384
FF_T = 1536
WCOLS_T = 4608
VCOLS_T = 2304
NPARAM = 14155776
N_TENSOR = 2


def draw_block_in(key, part):
    key = jax.random.fold_in(key, 11)
    column = jnp.arange(D, dtype=jnp.float32) / (D - 1)
    base = jax.random.truncated_normal(key, -4.0, 4.0, (ROWS, SEQ, D), jnp.float32)
    rising = 0.6 + 1.2 * column
    return (base * rising).astype(jnp.bfloat16)


def draw_weights(key, part):
    key = jax.random.fold_in(key, 22)
    shape_full = (LAYERS, N_TENSOR, D, WCOLS_T)
    base = jax.random.truncated_normal(key, -4.0, 4.0, shape_full, jnp.float32)
    column = jnp.arange(WCOLS_T)
    width_scale = D ** (-0.5)
    boosted = width_scale * (SEQ // DOCS) ** 0.5 * 0.5
    scale = jnp.where(column < 3 * HD_T, width_scale, jnp.where(column < 4 * HD_T, boosted, jnp.where(column < 4 * HD_T + FF_T, width_scale, FF ** (-0.5))))
    return (base * scale.astype(jnp.float32)).reshape(LAYERS, N_TENSOR, D * WCOLS_T)


def draw_rep_vectors(key, part):
    key = jax.random.fold_in(key, 33)
    noise_key, shift_key = jax.random.split(key)
    column = jnp.arange(D, dtype=jnp.float32) / (D - 1)
    noise = jax.random.uniform(noise_key, (LAYERS, 6, D), jnp.float32, 0.9, 1.1)
    rising = 0.6 + 1.2 * column
    shifts = 0.3 * jax.random.truncated_normal(shift_key, -3.0, 3.0, (LAYERS, 6, D), jnp.float32)
    kinds = jnp.arange(6)[:, None]
    is_gain = (kinds == 1) | (kinds == 4)
    return jnp.where(is_gain, rising * noise, shifts)


def shard_levels(rng, extent, shards, smallest, top_value):
    def one(position, blocks):
        draws = jax.random.uniform(jax.random.fold_in(jax.random.fold_in(rng, 6), position), (blocks,), jnp.float32, smallest / len(shards), top_value / len(shards))
        return jnp.repeat(jnp.exp(draws), extent[position] // blocks).reshape((-1,) + (1,) * (len(extent) - position - 1))

    level = one(*shards[0])
    for cut in shards[1:]:
        level = level * one(*cut)
    return level


def length_profile(amount, total, reach, skew):
    loads = [(1 << 20) // math.isqrt(grade ** skew) + 1 for grade in range(2, amount + 1)]
    spare, holding = total - reach - (amount - 1), [1] * (amount - 1)
    while spare > 0:
        free = [i for i in range(amount - 1) if holding[i] < reach]
        pool, budget = sum([loads[i] for i in free]), spare
        for i in free:
            extra = min(reach - holding[i], max(1, budget * loads[i] // pool), spare)
            holding[i] = holding[i] + extra
            spare = spare - extra
    return np.array([reach] + holding)


def uneven(own_key, number_of, total, limit, slope):
    if number_of == 2:
        one = jax.random.randint(own_key, (), max(1, total - limit), min(limit, total - 1) + 1)
        return jnp.stack([one, total - one])
    tallies = jnp.asarray(length_profile(number_of, total, limit, slope), jnp.int32)
    pairs = (number_of - 1) // 2
    giver, receiver = tallies[1:1 + 2 * pairs:2], tallies[2:2 + 2 * pairs:2]
    room = jnp.minimum(giver - 1, limit - receiver)
    passed = jax.random.randint(jax.random.fold_in(own_key, 1), (pairs,), 0, 1 << 20) % (room + 1)
    tallies = tallies.at[1:1 + 2 * pairs:2].set(giver - passed).at[2:2 + 2 * pairs:2].set(receiver + passed)
    return tallies[jax.random.permutation(jax.random.fold_in(own_key, 2), number_of)]


def gaussian(stream_key, extent, width, bound, cuts=(), kind=jnp.bfloat16):
    drawn = width * jax.random.normal(stream_key, extent, jnp.float32)
    if cuts:
        drawn = drawn * shard_levels(stream_key, extent, cuts, -0.22, 0.18)
    return jnp.clip(drawn, -bound, bound).astype(kind)


def setup_inputs(seed: int = 0) -> dict:
    arg_keys = jax.random.split(jax.random.key(seed), 13)
    block_in = draw_block_in(jax.random.fold_in(arg_keys[12], 71), 0)
    out_grad = gaussian(arg_keys[1], (ROWS, SEQ, D), 1.0, 6.0, ((0, 16),))
    segments = jax.vmap(lambda own: jnp.searchsorted(jnp.cumsum(uneven(own, DOCS, SEQ, SEQ // 2, 2)), jnp.arange(SEQ), side="right"))(jax.random.split(arg_keys[2], ROWS)).reshape((ROWS, SEQ)).astype(jnp.int32)
    weights = draw_weights(jax.random.fold_in(arg_keys[12], 71), 0)
    weights_first = gaussian(arg_keys[4], (LAYERS, N_TENSOR, D * WCOLS_T), (NPARAM ** -0.5), 0.00390625, ((1, 2), (2, 16)), jnp.float32)
    weights_second = jnp.clip(jnp.exp(math.log(2.825701699293859e-07) - 1.3862944 * jax.random.uniform(arg_keys[5], (LAYERS, N_TENSOR, D * WCOLS_T), jnp.float32) ** shard_levels(arg_keys[5], (LAYERS, N_TENSOR, D * WCOLS_T), ((1, 2), (2, 16)), -0.2, 0.2)), 7.064254248234647e-08, 2.825701699293859e-07)
    split_vectors = gaussian(arg_keys[6], (LAYERS, N_TENSOR, VCOLS_T), 0.3, 1.2, ((1, 2), (2, 16)), jnp.float32)
    split_first = gaussian(arg_keys[7], (LAYERS, N_TENSOR, VCOLS_T), (3.0 * NPARAM ** -0.5), 0.01171875, ((1, 2), (2, 16)), jnp.float32)
    split_second = jnp.clip(jnp.exp(math.log(2.543131586207892e-06) - 1.3862944 * jax.random.uniform(arg_keys[8], (LAYERS, N_TENSOR, VCOLS_T), jnp.float32) ** shard_levels(arg_keys[8], (LAYERS, N_TENSOR, VCOLS_T), ((1, 2), (2, 16)), -0.2, 0.2)), 6.35782896551973e-07, 2.543131586207892e-06)
    rep_vectors = draw_rep_vectors(jax.random.fold_in(arg_keys[12], 71), 0)
    rep_first = gaussian(arg_keys[10], (LAYERS, 6, D), (3.0 * NPARAM ** -0.5), 0.01171875, ((2, 16),), jnp.float32)
    rep_second = jnp.clip(jnp.exp(math.log(2.543131586207892e-06) - 1.3862944 * jax.random.uniform(arg_keys[11], (LAYERS, 6, D), jnp.float32) ** shard_levels(arg_keys[11], (LAYERS, 6, D), ((2, 16),), -0.2, 0.2)), 6.35782896551973e-07, 2.543131586207892e-06)
    return {"block_in": block_in, "out_grad": out_grad, "segments": segments, "weights": weights, "weights_first": weights_first, "weights_second": weights_second, "split_vectors": split_vectors, "split_first": split_first, "split_second": split_second, "rep_vectors": rep_vectors, "rep_first": rep_first, "rep_second": rep_second}


@jax.custom_vjp
def low(v):
    return lax.optimization_barrier(v.astype(jnp.bfloat16)).astype(jnp.float32)

@jax.custom_vjp
def low_back(v):
    return v

def low_keep(v):
    return (low(v), None)

def low_pass(kept, grad):
    return (grad,)

def back_keep(v):
    return (v, None)

def back_low(kept, grad):
    return (low(grad),)
low.defvjp(low_keep, low_pass)
low_back.defvjp(back_keep, back_low)
clip_limit = 1.0
weight_rate = 0.03
weight_decay = 0.01
vector_rate = 0.3

def product(left, right):
    return jnp.dot(left, right, precision=lax.Precision.HIGHEST)

def layer_norm(value, gain, shift):
    center = value - lax.optimization_barrier(jnp.mean(value, axis=-1, keepdims=True))
    spread = lax.optimization_barrier(jnp.mean(center * center, axis=-1, keepdims=True))
    return center * lax.rsqrt(spread + 1e-12) * gain + shift

def attend(query, keys_in, values_in, same):
    scores = jnp.einsum('bqhe,bkhe->bhqk', query, keys_in, precision=lax.Precision.HIGHEST) * HEAD_DIM ** (-0.5)
    scores = jnp.where(same, low_back(scores), -1000000000.0)
    probs = jax.nn.softmax(scores, axis=-1)
    return jnp.einsum('bhqk,bkhe->bqhe', low(probs), values_in, precision=lax.Precision.HIGHEST)

def block_layer(hidden, same, matrices, split_rows, rep_rows):
    row_count = hidden.shape[0]
    flat_in = hidden.reshape(row_count * SEQ, D)
    shape_four = (row_count, SEQ, HD_T // HEAD_DIM, HEAD_DIM)
    attn_total = jnp.zeros((row_count * SEQ, D), jnp.float32)
    for shard in range(N_TENSOR):
        matrix = matrices[shard]
        entry = low_back(low(flat_in))
        mixed = product(entry, matrix[:, :3 * HD_T])
        query = low(low_back(mixed[:, :HD_T] + split_rows[shard, :HD_T]))
        keys_in = low(low_back(mixed[:, HD_T:2 * HD_T]))
        values_in = low(low_back(mixed[:, 2 * HD_T:3 * HD_T] + split_rows[shard, HD_T:2 * HD_T]))
        context = jax.checkpoint(attend)(query.reshape(shape_four), keys_in.reshape(shape_four), values_in.reshape(shape_four), same)
        context = low(low_back(context.reshape(row_count * SEQ, HD_T)))
        attn_total = attn_total + low(product(context, matrix[:, 3 * HD_T:4 * HD_T].T))
    attn_out = low_back(attn_total)
    first = layer_norm(flat_in + attn_out + rep_rows[0], rep_rows[1], rep_rows[2])
    ffn_total = jnp.zeros((row_count * SEQ, D), jnp.float32)
    for shard in range(N_TENSOR):
        matrix = matrices[shard]
        entry = low_back(low(first))
        inner = low_back(product(entry, matrix[:, 4 * HD_T:4 * HD_T + FF_T]) + split_rows[shard, 2 * HD_T:])
        active = low(jax.nn.gelu(inner, approximate=False))
        ffn_total = ffn_total + low(product(active, matrix[:, 4 * HD_T + FF_T:].T))
    ffn_out = low_back(ffn_total)
    result = layer_norm(first + ffn_out + rep_rows[3], rep_rows[4], rep_rows[5])
    return result.reshape(row_count, SEQ, D)

def adamw(value, first, second, grad, rate, decay):
    first = 0.5 * first + 0.5 * grad
    second = 0.5 * second + 0.5 * grad * grad
    correct = 1.0 - 0.5 ** STEP
    direction = first / correct / (jnp.sqrt(second / correct) + 1e-08)
    return (value - rate * (direction + decay * value), first, second)

def reference(block_in, out_grad, segments, weights, weights_first, weights_second, split_vectors, split_first, split_second, rep_vectors, rep_first, rep_second):
    params = (low(weights), low(split_vectors), low(rep_vectors))

    def forward(hidden, same, param_set):
        weight_set, split_set, rep_set = param_set
        for layer_index in range(LAYERS):
            matrices = [weight_set[layer_index, shard].reshape(D, WCOLS_T) for shard in range(N_TENSOR)]
            hidden = block_layer(hidden, same, matrices, split_set[layer_index], rep_set[layer_index].reshape(6, D))
        return hidden

    def one_group(carry, pieces):
        group_in, group_grad, group_seg = pieces
        same = (group_seg[:, :, None] == group_seg[:, None, :])[:, None]
        result, pullback = jax.vjp(lambda hidden, param_set: forward(hidden, same, param_set), group_in.astype(jnp.float32), params)
        hidden_grad, param_grads = pullback(group_grad.astype(jnp.float32))
        return (jax.tree.map(jnp.add, carry, param_grads), (result.astype(jnp.bfloat16), hidden_grad))
    group_rows = 8
    groups = block_in.shape[0] // group_rows
    zero_grads = jax.tree.map(jnp.zeros_like, params)
    pieces = (block_in.reshape(groups, group_rows, SEQ, D), out_grad.reshape(groups, group_rows, SEQ, D), segments.reshape(groups, group_rows, SEQ))
    summed, (block_out, input_grad) = lax.scan(one_group, zero_grads, pieces)
    block_out = block_out.reshape(-1, SEQ, D)
    input_grad = input_grad.reshape(-1, SEQ, D)
    grad_weights, grad_split, grad_rep = summed
    grad_norm = jnp.sqrt(jnp.sum(grad_weights * grad_weights) + jnp.sum(grad_split * grad_split) + jnp.sum(grad_rep * grad_rep))
    factor = jnp.minimum(1.0, clip_limit / (grad_norm + 1e-06))
    clipped_rep = grad_rep * factor
    new_weights, weights_first_new, weights_second_new = adamw(weights, weights_first, weights_second, grad_weights * factor, weight_rate, weight_decay)
    new_split, split_first_new, split_second_new = adamw(split_vectors, split_first, split_second, grad_split * factor, vector_rate, 0.0)
    new_rep, rep_first_new, rep_second_new = adamw(rep_vectors, rep_first, rep_second, clipped_rep, vector_rate, 0.0)
    output_bias_grad = clipped_rep[:, 0, :]
    return (block_out, input_grad, grad_norm, new_weights, weights_first_new, weights_second_new, new_weights.astype(jnp.bfloat16), new_split, split_first_new, split_second_new, new_split.astype(jnp.bfloat16), new_rep, rep_first_new, rep_second_new, new_rep.astype(jnp.bfloat16), output_bias_grad)
```

```python
from functools import partial

import jax
import jax.numpy as jnp
from jax import lax
from jax.experimental import pallas as pl
from jax.experimental.pallas import tpu as pltpu
from jax.sharding import PartitionSpec as P

D = 768
HEAD_DIM = 64
LAYERS = 2
SEQ = 256
MICRO = 2
STEP = 3
HD = 384
FFT = 1536
QKV = 3 * HD
ATT = 4 * HD
COLS = ATT + 2 * FFT
VCOL = 2 * HD + FFT
LANES = 128
TILES = COLS // LANES

clip_limit = 1.0
weight_rate = 0.03
weight_decay = 0.01
vector_rate = 0.3
contract_last = (((1,), (1,)), ((), ()))
contract_first = (((0,), (0,)), ((), ()))
f32 = jnp.float32
b16 = jnp.bfloat16
VMEM_LIMIT = 56 * 1024 * 1024
ANY = pl.BlockSpec(memory_space=pl.ANY)
VM = pl.BlockSpec(memory_space=pltpu.VMEM)


def call(body, outs, in_specs, scratch=(), flops=0, moved=0, out_specs=None, trans=0):
    if out_specs is None:
        out_specs = [VM] * len(outs)
    return pl.pallas_call(
        body,
        out_shape=[jax.ShapeDtypeStruct(s, d) for s, d in outs],
        in_specs=in_specs,
        out_specs=out_specs,
        scratch_shapes=list(scratch),
        compiler_params=pltpu.CompilerParams(vmem_limit_bytes=VMEM_LIMIT),
        cost_estimate=pl.CostEstimate(flops=flops, bytes_accessed=moved, transcendentals=trans),
    )


def dot(a, b, dims=(((1,), (0,)), ((), ()))):
    return lax.dot_general(a, b, dims, preferred_element_type=f32)


def norm_rows(value):
    center = value - jnp.mean(value, axis=-1, keepdims=True)
    scale = lax.rsqrt(jnp.mean(center * center, axis=-1, keepdims=True) + 1e-12)
    return center * scale, scale


def norm_back(grad_out, normed, scale, gain):
    inner = grad_out * gain
    back = scale * (
        inner
        - jnp.mean(inner, axis=-1, keepdims=True)
        - normed * jnp.mean(inner * normed, axis=-1, keepdims=True)
    )
    return (
        back,
        jnp.sum(grad_out * normed, axis=0, keepdims=True),
        jnp.sum(grad_out, axis=0, keepdims=True),
    )


def places(ring):
    me = lax.axis_index("dp")
    return lax.div(me, 4), lax.rem(lax.div(me, 2), 2), lax.rem(me, 2)


def pairs_of(ndp, kind):
    if kind == "ring":
        return [(i, (i + 4) % ndp) for i in range(ndp)]
    if kind == "x":
        return [(i, i ^ 2) for i in range(ndp)]
    return [(i, i ^ 1) for i in range(ndp)]


def move(a, kind):
    return lax.ppermute(a, "dp", pairs_of(lax.axis_size("dp"), kind))


def exchange(a):
    return lax.ppermute(a, "tensor", [(0, 1), (1, 0)])


def assemble(parts):
    half = len(parts) // 2

    def body(*refs):
        ins, out, sem = refs[: 2 * half], refs[2 * half], refs[2 * half + 1]
        copies = []
        for i in range(2 * half):
            copies.append(pltpu.make_async_copy(ins[i], out.at[i // half, i % half], sem.at[i]))
            copies[-1].start()
        for cp in copies:
            cp.wait()

    rows, cols = parts[0].shape
    size = len(parts) * rows * cols * 2
    return call(
        body,
        [((2, half, rows, cols), b16)],
        [ANY] * len(parts),
        [pltpu.SemaphoreType.DMA((2 * half,))],
        moved=2 * size,
        out_specs=[ANY],
    )(*parts)[0]


def gather_chunk(own):
    ring = lax.axis_size("dp") // 4
    rounds = [own]
    for _ in range(ring - 1):
        rounds.append(move(rounds[-1], "ring"))
    across = [move(r, "x") for r in rounds]
    mine = assemble(rounds + across)
    return mine, move(mine, "core")


def start_load(pieces, target, sem, first=0, cols=None):
    if len(pieces) == 1:
        width = target.shape[1]
        src = pieces[0].at[:, pl.ds(first, width)]
        copies = [pltpu.make_async_copy(src, target, sem.at[0])]
    else:
        ring, rows = pieces[0].shape[1], pieces[0].shape[2]
        width = target.shape[1]
        z, x, c = places(ring)
        copies = []
        for other in range(2):
            for xo in range(2):
                for k in range(ring):
                    zz = lax.rem(z - k + ring, ring)
                    xx = lax.rem(x + xo, 2)
                    cc = lax.rem(c + other, 2)
                    row = pl.multiple_of(((zz * 2 + xx) * 2 + cc) * rows, 16)
                    copies.append(
                        pltpu.make_async_copy(
                            pieces[other].at[xo, k, :, pl.ds(first, width)],
                            target.at[pl.ds(row, rows), :],
                            sem.at[len(copies)],
                        )
                    )
    for cp in copies:
        cp.start()
    return copies


def load_count(pieces):
    return 1 if len(pieces) == 1 else 4 * pieces[0].shape[1]


def prep(weights_tiled, rep, split):
    tiled_rows = weights_tiled.shape[1]
    rows = tiled_rows // TILES
    per = split.shape[1]

    def body(w_ref, rep_ref, split_ref, a0, f0, a1, f1):
        for layer, (a_ref, f_ref) in enumerate(((a0, f0), (a1, f1))):
            for c in range(TILES):
                piece = w_ref[layer, pl.ds(c, rows, stride=TILES), :].astype(b16)
                if c < ATT // LANES:
                    a_ref[:, c * LANES : (c + 1) * LANES] = piece
                else:
                    at = c * LANES - ATT
                    f_ref[:, at : at + LANES] = piece
        row = lax.broadcasted_iota(jnp.int32, (rows, rows), 0)
        col = lax.broadcasted_iota(jnp.int32, (rows, rows), 1)
        eye = (row == col).astype(b16)
        row3 = lax.broadcasted_iota(jnp.int32, (rows, per), 0)
        col3 = lax.broadcasted_iota(jnp.int32, (rows, per), 1)
        gap = col3 - 3 * row3
        block = jnp.zeros((rows, LANES), f32)
        lane = lax.broadcasted_iota(jnp.int32, (rows, LANES), 1)
        rep_cols = dot(eye, rep_ref[...].astype(b16), contract_last)
        rep_wide = jnp.concatenate(
            [rep_cols, jnp.zeros((rows, LANES - 6 * LAYERS), f32)], axis=1
        )
        block = rep_wide
        low = split_ref[...].astype(b16).astype(f32)
        for layer in range(LAYERS):
            for j in range(3):
                pick = jnp.where(gap == j, jnp.broadcast_to(low[layer : layer + 1], (rows, per)), 0.0)
                value = jnp.sum(pick, axis=1, keepdims=True)
                block = jnp.where(lane == 6 * LAYERS + 3 * layer + j, value, block)
        a0[:, ATT:] = block.astype(b16)

    return call(
        body,
        [
            ((rows, ATT + LANES), b16),
            ((rows, 2 * FFT), b16),
            ((rows, ATT), b16),
            ((rows, 2 * FFT), b16),
        ],
        [VM] * 3,
        moved=weights_tiled.size * 6,
    )(weights_tiled, rep, split)


def spread_mask(first_row, rows, first, cols):
    row = first_row + lax.broadcasted_iota(jnp.int32, (rows, cols), 0)
    col = first + lax.broadcasted_iota(jnp.int32, (rows, cols), 1)
    gap = col - 3 * row
    return jnp.where((gap >= 0) & (gap < 3), 1.0, 0.0).astype(b16)


def unpack(pieces):
    count = load_count(pieces)

    def body(*refs):
        ins, (rep_ref, split_ref, cols_ref, sem) = refs[: len(pieces)], refs[len(pieces) :]
        for cp in start_load(ins, cols_ref, sem, first=ATT):
            cp.wait()
        flat = cols_ref[...]
        turned = flat.astype(f32).T
        rep_ref[...] = turned[:16]
        low = turned[:24].astype(b16)
        step = VCOL // 3
        for i in range(3):
            rows = D // 3
            mask = spread_mask(i * rows, rows, i * step, step)
            spread = dot(low[:, i * rows : (i + 1) * rows], mask)
            phase = lax.rem(lax.broadcasted_iota(jnp.int32, (1, step), 1), 3)
            for layer in range(LAYERS):
                at = 6 * LAYERS + 3 * layer
                value = jnp.where(
                    phase == 0,
                    spread[at : at + 1],
                    jnp.where(phase == 1, spread[at + 1 : at + 2], spread[at + 2 : at + 3]),
                )
                split_ref[layer : layer + 1, i * step : (i + 1) * step] = value

    return call(
        body,
        [((16, D), f32), ((8, VCOL), f32)],
        [ANY] * len(pieces),
        [pltpu.VMEM((D, LANES), b16), pltpu.SemaphoreType.DMA((count,))],
        moved=D * LANES * 2,
        flops=24 * D * VCOL,
    )(*pieces)


def gelu_parts(inner):
    cdf = 0.5 * (1.0 + lax.erf(inner * (0.5**0.5)))
    dens = jnp.exp(-0.5 * inner * inner) * 0.3989422804014327
    return inner * cdf, cdf + inner * dens


def attend(h_low, layer, w_ref, split_ref, seg_ref, part_ref, qkv_ref, probs_ref, ctx_ref):
    mixed = dot(h_low, w_ref[:, :QKV])
    qkv_ref[:, :HD] = (mixed[:, :HD] + split_ref[layer : layer + 1, :HD]).astype(b16)
    qkv_ref[:, HD : 2 * HD] = mixed[:, HD : 2 * HD].astype(b16)
    qkv_ref[:, 2 * HD :] = (
        mixed[:, 2 * HD :] + split_ref[layer : layer + 1, HD : 2 * HD]
    ).astype(b16)
    seg = jnp.broadcast_to(seg_ref[...].astype(f32), (SEQ, SEQ))
    same = seg == seg.T
    low_half = lax.broadcasted_iota(jnp.int32, (1, LANES), 1) < HEAD_DIM
    for pair in range(HD // LANES):
        at = pair * LANES
        query = qkv_ref[:, at : at + LANES].astype(f32) * HEAD_DIM ** (-0.5)
        keys = qkv_ref[:, HD + at : HD + at + LANES]
        values = qkv_ref[:, 2 * HD + at : 2 * HD + at + LANES].astype(f32)
        total = jnp.zeros((SEQ, LANES), f32)
        for half in range(2):
            mine = low_half if half == 0 else ~low_half
            scores = dot(jnp.where(mine, query, 0.0).astype(b16), keys, contract_last)
            scores = jnp.where(same, scores, -1000000000.0)
            raised = jnp.exp(scores - jnp.max(scores, axis=-1, keepdims=True))
            probs = (raised * (1.0 / jnp.sum(raised, axis=-1, keepdims=True))).astype(b16)
            probs_ref[2 * pair + half] = probs
            total = total + dot(probs, jnp.where(mine, values, 0.0).astype(b16))
        ctx_ref[:, at : at + LANES] = total.astype(b16)
    part_ref[...] = dot(ctx_ref[...], w_ref[:, QKV:ATT], contract_last).astype(b16)


ATT_FLOPS = 2 * SEQ * D * ATT + 4 * SEQ * SEQ * HD * 2
FFN_FLOPS = 2 * SEQ * D * 2 * FFT


def weight_scratch(pieces, cols):
    return [pltpu.VMEM((D, cols), b16), pltpu.SemaphoreType.DMA((load_count(pieces),))]


def attention_first(micro, block_in, segments, split, pieces):
    def body(h_ref, seg_ref, split_ref, *refs):
        ins, refs = refs[: len(pieces)], refs[len(pieces) :]
        part_ref, qkv_ref, probs_ref, ctx_ref, w_ref, sem = refs
        for cp in start_load(ins, w_ref, sem):
            cp.wait()
        attend(
            h_ref[micro], 0, w_ref, split_ref, seg_ref[micro], part_ref, qkv_ref, probs_ref, ctx_ref
        )

    return call(
        body,
        [
            ((SEQ, D), b16),
            ((SEQ, QKV), b16),
            ((HD // HEAD_DIM, SEQ, SEQ), b16),
            ((SEQ, HD), b16),
        ],
        [VM] * 3 + [ANY] * len(pieces),
        weight_scratch(pieces, ATT),
        flops=ATT_FLOPS,
        moved=6 << 20,
    )(block_in, segments, split, *pieces)


def attention_next(micro, layer, normed, part_own, part_other, rep, segments, split, pieces):
    base = 6 * (layer - 1)

    def body(n_ref, own_ref, other_ref, rep_ref, seg_ref, split_ref, *refs):
        ins, refs = refs[: len(pieces)], refs[len(pieces) :]
        part_ref, qkv_ref, probs_ref, ctx_ref, n2_ref, s2_ref, low_ref, w_ref, sem = refs
        copies = start_load(ins, w_ref, sem)
        first = n_ref[...] * rep_ref[base + 1 : base + 2] + rep_ref[base + 2 : base + 3]
        added = own_ref[...].astype(f32) + other_ref[...].astype(f32)
        n2, s2 = norm_rows(first + added + rep_ref[base + 3 : base + 4])
        n2_ref[...] = n2
        s2_ref[...] = s2
        low_ref[...] = (n2 * rep_ref[base + 4 : base + 5] + rep_ref[base + 5 : base + 6]).astype(b16)
        for cp in copies:
            cp.wait()
        attend(
            low_ref[...],
            layer,
            w_ref,
            split_ref,
            seg_ref[micro],
            part_ref,
            qkv_ref,
            probs_ref,
            ctx_ref,
        )

    return call(
        body,
        [
            ((SEQ, D), b16),
            ((SEQ, QKV), b16),
            ((HD // HEAD_DIM, SEQ, SEQ), b16),
            ((SEQ, HD), b16),
            ((SEQ, D), f32),
            ((SEQ, 1), f32),
            ((SEQ, D), b16),
        ],
        [VM] * 6 + [ANY] * len(pieces),
        weight_scratch(pieces, ATT),
        flops=ATT_FLOPS,
        moved=8 << 20,
    )(normed, part_own, part_other, rep, segments, split, *pieces)


def feed_forward(micro, layer, hidden, part_own, part_other, rep, split, pieces):
    base = 6 * layer

    def body(h_ref, own_ref, other_ref, rep_ref, split_ref, *refs):
        ins, refs = refs[: len(pieces)], refs[len(pieces) :]
        part_ref, n1_ref, s1_ref, low_ref, act_ref, slope_ref, w_ref, sem = refs
        copies = start_load(ins, w_ref, sem)
        if layer == 0:
            hidden_in = h_ref[micro].astype(f32)
        else:
            hidden_in = h_ref[...] * rep_ref[base - 2 : base - 1] + rep_ref[base - 1 : base]
        added = own_ref[...].astype(f32) + other_ref[...].astype(f32)
        n1, s1 = norm_rows(hidden_in + added + rep_ref[base : base + 1])
        n1_ref[...] = n1
        s1_ref[...] = s1
        low_ref[...] = (n1 * rep_ref[base + 1 : base + 2] + rep_ref[base + 2 : base + 3]).astype(b16)
        for cp in copies:
            cp.wait()
        step = 512
        for at in range(0, FFT, step):
            inner = (
                dot(low_ref[...], w_ref[:, at : at + step])
                + split_ref[layer : layer + 1, 2 * HD + at : 2 * HD + at + step]
            )
            active, slope = gelu_parts(inner)
            act_ref[:, at : at + step] = active.astype(b16)
            slope_ref[:, at : at + step] = slope.astype(b16)
        part_ref[...] = dot(act_ref[...], w_ref[:, FFT:], contract_last).astype(b16)

    return call(
        body,
        [
            ((SEQ, D), b16),
            ((SEQ, D), f32),
            ((SEQ, 1), f32),
            ((SEQ, D), b16),
            ((SEQ, FFT), b16),
            ((SEQ, FFT), b16),
        ],
        [VM] * 5 + [ANY] * len(pieces),
        weight_scratch(pieces, 2 * FFT),
        flops=FFN_FLOPS,
        moved=10 << 20,
    )(hidden, part_own, part_other, rep, split, *pieces)


def feed_back_tail(grad, n2, s2, layer, rep_ref, act_slope, copies, w_ref, outs):
    base = 6 * layer
    part_ref, res_ref, dffn_ref, din_ref, vec_ref = outs
    slope_ref = act_slope
    back, gain, shift = norm_back(grad, n2, s2, rep_ref[base + 4 : base + 5])
    res_ref[...] = back
    dffn_ref[...] = back.astype(b16)
    vec_ref[...] = jnp.zeros_like(vec_ref)
    vec_ref[0:1] = jnp.sum(back, axis=0, keepdims=True)
    vec_ref[1:2] = gain
    vec_ref[2:3] = shift
    for cp in copies:
        cp.wait()
    step = 384
    for at in range(0, FFT, step):
        grad_act = dot(dffn_ref[...], w_ref[:, FFT + at : FFT + at + step])
        grad_in = (slope_ref[:, at : at + step].astype(f32) * grad_act).astype(b16)
        din_ref[:, at : at + step] = grad_in
        row, lane = 3 + at // D, at % D
        vec_ref[row : row + 1, lane : lane + step] = jnp.sum(
            grad_in.astype(f32), axis=0, keepdims=True
        )
    part_ref[...] = dot(din_ref[...], w_ref[:, :FFT], contract_last).astype(b16)


BACK_OUTS = [
    ((SEQ, D), b16),
    ((SEQ, D), f32),
    ((SEQ, D), b16),
    ((SEQ, FFT), b16),
    ((8, D), f32),
]


def feed_back_top(micro, layer, out_grad, n1, part_own, part_other, rep, slope, pieces):
    base = 6 * layer

    def body(g_ref, n_ref, own_ref, other_ref, rep_ref, slope_ref, *refs):
        ins, refs = refs[: len(pieces)], refs[len(pieces) :]
        out_ref, w_ref, sem = refs[5:]
        copies = start_load(ins, w_ref, sem)
        first = n_ref[...] * rep_ref[base + 1 : base + 2] + rep_ref[base + 2 : base + 3]
        added = own_ref[...].astype(f32) + other_ref[...].astype(f32)
        n2, s2 = norm_rows(first + added + rep_ref[base + 3 : base + 4])
        out_ref[...] = (n2 * rep_ref[base + 4 : base + 5] + rep_ref[base + 5 : base + 6]).astype(b16)
        feed_back_tail(
            g_ref[micro].astype(f32), n2, s2, layer, rep_ref, slope_ref, copies, w_ref, refs[:5]
        )

    return call(
        body,
        BACK_OUTS + [((SEQ, D), b16)],
        [VM] * 6 + [ANY] * len(pieces),
        weight_scratch(pieces, 2 * FFT),
        flops=FFN_FLOPS,
        moved=11 << 20,
    )(out_grad, n1, part_own, part_other, rep, slope, *pieces)


def feed_back(layer, mid, part_own, part_other, n2, s2, rep, slope, pieces):
    def body(mid_ref, own_ref, other_ref, n2_ref, s2_ref, rep_ref, slope_ref, *refs):
        ins, refs = refs[: len(pieces)], refs[len(pieces) :]
        w_ref, sem = refs[5:]
        copies = start_load(ins, w_ref, sem)
        added = own_ref[...].astype(f32) + other_ref[...].astype(f32)
        feed_back_tail(
            mid_ref[...] + added,
            n2_ref[...],
            s2_ref[...],
            layer,
            rep_ref,
            slope_ref,
            copies,
            w_ref,
            refs[:5],
        )

    return call(
        body,
        BACK_OUTS,
        [VM] * 7 + [ANY] * len(pieces),
        weight_scratch(pieces, 2 * FFT),
        flops=FFN_FLOPS,
        moved=11 << 20,
    )(mid, part_own, part_other, n2, s2, rep, slope, *pieces)


def attention_back(layer, res, part_own, part_other, n1, s1, rep, qkv, probs, ctx, pieces):
    base = 6 * layer

    def body(
        res_ref, own_ref, other_ref, n1_ref, s1_ref, rep_ref, qkv_ref, probs_ref, ctx_ref, *refs
    ):
        ins, refs = refs[: len(pieces)], refs[len(pieces) :]
        part_ref, mid_ref, datt_ref, dqkv_ref, vec_ref, w_ref, sem = refs
        copies = start_load(ins, w_ref, sem)
        grad = res_ref[...] + (own_ref[...].astype(f32) + other_ref[...].astype(f32))
        back, gain, shift = norm_back(grad, n1_ref[...], s1_ref[...], rep_ref[base + 1 : base + 2])
        mid_ref[...] = back
        datt_ref[...] = back.astype(b16)
        vec_ref[...] = jnp.zeros_like(vec_ref)
        vec_ref[0:1] = jnp.sum(back, axis=0, keepdims=True)
        vec_ref[1:2] = gain
        vec_ref[2:3] = shift
        for cp in copies:
            cp.wait()
        dctx = dot(datt_ref[...], w_ref[:, QKV:ATT]).astype(b16).astype(f32)
        low_half = lax.broadcasted_iota(jnp.int32, (1, LANES), 1) < HEAD_DIM
        factor = HEAD_DIM ** (-0.5)
        for pair in range(HD // LANES):
            at = pair * LANES
            query = qkv_ref[:, at : at + LANES].astype(f32) * factor
            keys = qkv_ref[:, HD + at : HD + at + LANES].astype(f32) * factor
            values = qkv_ref[:, 2 * HD + at : 2 * HD + at + LANES]
            dc = dctx[:, at : at + LANES]
            weighed = dc * ctx_ref[:, at : at + LANES].astype(f32)
            dq = jnp.zeros((SEQ, LANES), f32)
            dk = jnp.zeros((SEQ, LANES), f32)
            dv = jnp.zeros((SEQ, LANES), f32)
            for half in range(2):
                mine = low_half if half == 0 else ~low_half
                dcm = jnp.where(mine, dc, 0.0).astype(b16)
                delta = jnp.sum(jnp.where(mine, weighed, 0.0), axis=-1, keepdims=True)
                probs = probs_ref[2 * pair + half]
                dprobs = dot(dcm, values, contract_last)
                dscores = (probs.astype(f32) * (dprobs - delta)).astype(b16)
                dq = dq + dot(dscores, jnp.where(mine, keys, 0.0).astype(b16))
                dk = dk + dot(dscores, jnp.where(mine, query, 0.0).astype(b16), contract_first)
                dv = dv + dot(probs, dcm, contract_first)
            dqkv_ref[:, at : at + LANES] = dq.astype(b16)
            dqkv_ref[:, HD + at : HD + at + LANES] = dk.astype(b16)
            dqkv_ref[:, 2 * HD + at : 2 * HD + at + LANES] = dv.astype(b16)
        vec_ref[3:4, :HD] = jnp.sum(dqkv_ref[:, :HD].astype(f32), axis=0, keepdims=True)
        vec_ref[3:4, HD:] = jnp.sum(dqkv_ref[:, 2 * HD :].astype(f32), axis=0, keepdims=True)
        part_ref[...] = dot(dqkv_ref[...], w_ref[:, :QKV], contract_last).astype(b16)

    return call(
        body,
        [
            ((SEQ, D), b16),
            ((SEQ, D), f32),
            ((SEQ, D), b16),
            ((SEQ, QKV), b16),
            ((8, D), f32),
        ],
        [VM] * 9 + [ANY] * len(pieces),
        weight_scratch(pieces, ATT),
        flops=2 * ATT_FLOPS,
        moved=9 << 20,
    )(res, part_own, part_other, n1, s1, rep, qkv, probs, ctx, *pieces)


def finish_input(mids, owns, others):
    def body(*refs):
        for micro in range(MICRO):
            m, a, b = refs[3 * micro : 3 * micro + 3]
            refs[-1][micro] = m[...] + (a[...].astype(f32) + b[...].astype(f32))

    args = []
    for micro in range(MICRO):
        args += [mids[micro], owns[micro], others[micro]]
    return call(body, [((MICRO, SEQ, D), f32)], [VM] * len(args), moved=7 << 20)(*args)[0]


def store_slots(product_ref, outs, at, width):
    if len(outs) == 1:
        outs[0][:, at : at + width] = product_ref[:, :width].astype(b16)
        return
    ring, rows = outs[0].shape[1], outs[0].shape[2]
    z, x, c = places(ring)
    for other in range(2):
        for xo in range(2):
            for k in range(ring):
                zz = lax.rem(z + k, ring)
                xx = lax.rem(x + xo, 2)
                cc = lax.rem(c + other, 2)
                row = pl.multiple_of(((zz * 2 + xx) * 2 + cc) * rows, 16)
                outs[other][xo, k, :, at : at + width] = product_ref[
                    pl.ds(row, rows), :width
                ].astype(b16)


def grad_outs(ndp, pieced, cols):
    rows = D // ndp
    if pieced:
        return [((2, ndp // 4, rows, cols), b16)] * 2
    return [((D, cols), b16)]


def matrix_gradient(sets, pieced, ndp, vectors=None):
    widths = [s[2] for s in sets]
    total = sum(widths) + (LANES if vectors is not None else 0)
    outs = grad_outs(ndp, pieced, total)
    args, specs = [], []
    for left, right, _ in sets:
        for micro in range(MICRO):
            specs.append(VM)
            args.append(left[micro])
        for micro in range(MICRO):
            args.append(right[micro])
            specs.append(VM)
    plain = len(args)
    if vectors is not None:
        args += vectors
        specs += [VM] * len(vectors)
    n_in = len(args)
    step = 384

    def body(*refs):
        out_refs = refs[n_in : n_in + len(outs)]
        prod_ref = refs[n_in + len(outs)]
        at = 0
        for index, width in enumerate(widths):
            l0, l1, r0, r1 = refs[4 * index : 4 * index + 4]
            left = [r[m] if len(r.shape) == 3 else r[...] for m, r in enumerate((l0, l1))]
            for col in range(0, width, step):
                prod_ref[...] = dot(left[0], r0[:, col : col + step], contract_first) + dot(
                    left[1], r1[:, col : col + step], contract_first
                )
                store_slots(prod_ref, out_refs, at, step)
                at += step
        if vectors is not None:
            pack_vectors(refs[plain:n_in], prod_ref)
            store_slots(prod_ref, out_refs, at, LANES)

    moved = sum(a.size * 2 for a in args[:plain]) + D * total * 2
    return call(
        body,
        outs,
        specs,
        [pltpu.VMEM((D, step), f32)],
        flops=2 * MICRO * SEQ * D * total,
        moved=moved,
    )(*args)


def pack_vectors(vec_refs, prod_ref):
    sums = []
    for layer in range(LAYERS):
        a0, a1, b0, b1 = vec_refs[4 * layer : 4 * layer + 4]
        sums.append((a0[...] + a1[...], b0[...] + b1[...]))
    rows = []
    for att, ffn in sums:
        rows += [att[0:1], att[1:2], att[2:3], ffn[0:1], ffn[1:2], ffn[2:3]]
    rows.append(jnp.zeros((4, D), f32))
    turned = jnp.concatenate(rows, axis=0)
    turned = jnp.concatenate([turned, jnp.zeros((LANES - 16, D), f32)], axis=0).T
    step = VCOL // 3
    phase = lax.rem(lax.broadcasted_iota(jnp.int32, (1, step), 1), 3)
    lane = lax.broadcasted_iota(jnp.int32, (1, LANES), 1)
    for i in range(3):
        picked = []
        for att, ffn in sums:
            line = (att[3:4], ffn[3:4], ffn[4:5])[i]
            for j in range(3):
                picked.append(jnp.where(phase == j, line, 0.0))
        picked = jnp.concatenate(
            [jnp.zeros((12, step), f32)] + picked + [jnp.zeros((LANES - 18, step), f32)], axis=0
        ).astype(b16)
        n_rows = D // 3
        mask = spread_mask(i * n_rows, n_rows, i * step, step)
        part = dot(mask, picked, contract_last)
        keep = turned[i * n_rows : (i + 1) * n_rows]
        prod_ref[i * n_rows : (i + 1) * n_rows, :LANES] = jnp.where(lane < 12, keep, part)


def reduce_chunk(pieces):
    ndp = lax.axis_size("dp")
    if len(pieces) == 1:
        return lax.psum_scatter(pieces[0], "dp", scatter_dimension=0, tiled=True).astype(f32)
    own, other = pieces
    ring = own.shape[1]
    met = move(other, "core")
    sent = (own[1].astype(f32) + met[1].astype(f32)).astype(b16)
    got = move(sent, "x")
    sums = [
        own[0, k].astype(f32) + met[0, k].astype(f32) + got[k].astype(f32) for k in range(ring)
    ]
    total = sums[ring - 1]
    for k in range(ring - 2, -1, -1):
        total = sums[k] + move(total.astype(b16), "ring").astype(f32)
    return total


def adamw(value, first, second, grad, rate, decay):
    first = 0.5 * first + 0.5 * grad
    second = 0.5 * second + 0.5 * grad * grad
    correct = 1.0 - 0.5**STEP
    direction = first / correct / (jnp.sqrt(second / correct) + 1e-08)
    return (value - rate * (direction + decay * value), first, second)


def update_matrices(tiled, first, second, grads, factor):
    rows = grads[0].shape[0]
    step = 8 if rows % 8 == 0 else rows
    n_steps = rows // step
    block = (1, step * TILES, LANES)

    def body(f_ref, w_ref, m_ref, v_ref, a0, f0, a1, f1, nw, nm, nv, nl):
        scale = f_ref[0, 0]
        layer = pl.program_id(0)
        for c in range(TILES):
            if c < ATT // LANES:
                lo = c * LANES
                grad = jnp.where(layer == 0, a0[:, lo : lo + LANES], a1[:, lo : lo + LANES])
            else:
                lo = c * LANES - ATT
                grad = jnp.where(layer == 0, f0[:, lo : lo + LANES], f1[:, lo : lo + LANES])
            where = (0, pl.ds(c, step, stride=TILES), slice(None))
            new = adamw(
                w_ref[where], m_ref[where], v_ref[where], grad * scale, weight_rate, weight_decay
            )
            nw[where], nm[where], nv[where] = new
        nl[...] = nw[...].astype(b16)

    big = pl.BlockSpec(block, lambda l, i: (l, i, 0))
    shape = tiled.shape
    return pl.pallas_call(
        body,
        grid=(LAYERS, n_steps),
        out_shape=[jax.ShapeDtypeStruct(shape, f32)] * 3 + [jax.ShapeDtypeStruct(shape, b16)],
        in_specs=[pl.BlockSpec(memory_space=pltpu.SMEM), big, big, big]
        + [pl.BlockSpec((step, g.shape[1]), lambda l, i: (i, 0)) for g in grads],
        out_specs=[big] * 4,
        compiler_params=pltpu.CompilerParams(vmem_limit_bytes=VMEM_LIMIT),
        cost_estimate=pl.CostEstimate(
            flops=20 * tiled.size, bytes_accessed=30 * tiled.size, transcendentals=tiled.size
        ),
    )(factor.reshape(1, 1), tiled, first, second, *grads)


def sum_everywhere(value):
    ndp = lax.axis_size("dp")
    if ndp & (ndp - 1):
        return lax.psum(value, ("dp", "tensor"))
    bit = 1
    while bit < ndp:
        value = value + lax.ppermute(value, "dp", [(i, i ^ bit) for i in range(ndp)])
        bit *= 2
    return value + exchange(value)


def per_device(
    block_in,
    out_grad,
    segments,
    weights,
    weights_first,
    weights_second,
    split_vectors,
    split_first,
    split_second,
    rep_vectors,
    rep_first,
    rep_second,
):
    ndp = lax.axis_size("dp")
    rows = D // ndp
    per = split_vectors.shape[2]
    pieced = ndp % 4 == 0 and rows % 16 == 0
    shard_shape = weights.shape
    tiled_shape = (LAYERS, -1, LANES)
    weights_tiled = weights.reshape(tiled_shape)
    rep_flat = rep_vectors.reshape(LAYERS * 6, -1)
    split_flat = split_vectors.reshape(LAYERS, per)
    if pieced:
        a0, f0, a1, f1 = prep(weights_tiled, rep_flat, split_flat)
        att = [gather_chunk(a0), None]
        ffn = [gather_chunk(f0), None]
        att[1] = gather_chunk(a1)
        ffn[1] = gather_chunk(f1)
    else:
        low = weights.astype(b16).reshape(LAYERS, rows, COLS)
        block = jnp.concatenate(
            [
                rep_flat.T,
                split_flat.reshape(LAYERS, rows, 3).transpose(1, 0, 2).reshape(rows, 6),
                jnp.zeros((rows, LANES - 18), f32),
            ],
            axis=1,
        ).astype(b16)
        gather = partial(lax.all_gather, axis_name="dp", axis=0, tiled=True)
        att = [
            (gather(jnp.concatenate([low[0, :, :ATT], block], axis=1)),),
            (gather(low[1, :, :ATT]),),
        ]
        ffn = [(gather(low[layer, :, ATT:]),) for layer in range(LAYERS)]
    rep, split = unpack(att[0])
    both = range(MICRO)
    seg = segments.reshape(MICRO, 1, SEQ)

    out = [attention_first(m, block_in, seg, split, att[0]) for m in both]
    qkv0, probs0, ctx0 = ([o[i] for o in out] for i in (1, 2, 3))
    met = [exchange(o[0]) for o in out]
    out = [
        feed_forward(m, 0, block_in, out[m][0], met[m], rep, split, ffn[0]) for m in both
    ]
    n1_0, s1_0, low1_0, act0, slope0 = ([o[i] for o in out] for i in range(1, 6))
    met = [exchange(o[0]) for o in out]
    out = [
        attention_next(m, 1, n1_0[m], out[m][0], met[m], rep, seg, split, att[1]) for m in both
    ]
    qkv1, probs1, ctx1, n2_0, s2_0, low_h1 = ([o[i] for o in out] for i in range(1, 7))
    met = [exchange(o[0]) for o in out]
    out = [
        feed_forward(m, 1, n2_0[m], out[m][0], met[m], rep, split, ffn[1]) for m in both
    ]
    n1_1, s1_1, low1_1, act1, slope1 = ([o[i] for o in out] for i in range(1, 6))
    met = [exchange(o[0]) for o in out]

    out = [
        feed_back_top(m, 1, out_grad, n1_1[m], out[m][0], met[m], rep, slope1[m], ffn[1])
        for m in both
    ]
    res, dffn, din, vec_f1 = ([o[i] for o in out] for i in range(1, 5))
    block_out = jnp.stack([o[5] for o in out])
    met = [exchange(o[0]) for o in out]
    out = [
        attention_back(
            1, res[m], out[m][0], met[m], n1_1[m], s1_1[m], rep, qkv1[m], probs1[m], ctx1[m], att[1]
        )
        for m in both
    ]
    grad_f1 = reduce_chunk(
        matrix_gradient([(low1_1, din, FFT), (dffn, act1, FFT)], pieced, ndp)
    )
    mid, datt, dqkv, vec_a1 = ([o[i] for o in out] for i in range(1, 5))
    met = [exchange(o[0]) for o in out]
    out = [
        feed_back(0, mid[m], out[m][0], met[m], n2_0[m], s2_0[m], rep, slope0[m], ffn[0])
        for m in both
    ]
    grad_a1 = reduce_chunk(
        matrix_gradient([(low_h1, dqkv, QKV), (datt, ctx1, HD)], pieced, ndp)
    )
    res, dffn, din, vec_f0 = ([o[i] for o in out] for i in range(1, 5))
    met = [exchange(o[0]) for o in out]
    out = [
        attention_back(
            0, res[m], out[m][0], met[m], n1_0[m], s1_0[m], rep, qkv0[m], probs0[m], ctx0[m], att[0]
        )
        for m in both
    ]
    grad_f0 = reduce_chunk(
        matrix_gradient([(low1_0, din, FFT), (dffn, act0, FFT)], pieced, ndp)
    )
    mid, datt, dqkv, vec_a0 = ([o[i] for o in out] for i in range(1, 5))
    met = [exchange(o[0]) for o in out]
    grad_a0 = reduce_chunk(
        matrix_gradient(
            [([block_in] * MICRO, dqkv, QKV), (datt, ctx0, HD)],
            pieced,
            ndp,
            vectors=vec_a0 + vec_f0 + vec_a1 + vec_f1,
        )
    )
    input_grad = finish_input(mid, [o[0] for o in out], met)

    block = grad_a0[:, ATT:]
    grad_rep = block[:, :12].T.reshape(rep_vectors.shape)
    grad_split = (
        block[:, 12:18].reshape(rows, LAYERS, 3).transpose(1, 0, 2).reshape(split_vectors.shape)
    )
    tensor_first = (lax.axis_index("tensor") == 0).astype(f32)
    square = lambda a: jnp.sum(a * a)
    local_squares = (
        square(grad_a0[:, :ATT])
        + square(grad_f0)
        + square(grad_a1)
        + square(grad_f1)
        + square(block[:, 12:18])
        + tensor_first * square(block[:, :12])
    )
    total = sum_everywhere(jnp.full((8, LANES), local_squares, f32))[0, 0]
    grad_norm = jnp.sqrt(total)
    factor = jnp.minimum(1.0, clip_limit / (grad_norm + 1e-06))
    clipped_rep = grad_rep * factor
    masters = [a.reshape(tiled_shape) for a in (weights, weights_first, weights_second)]
    if pieced:
        new = update_matrices(*masters, [grad_a0, grad_f0, grad_a1, grad_f1], factor)
    else:
        grad = jnp.stack(
            [
                jnp.concatenate([grad_a0[:, :ATT], grad_f0], axis=1),
                jnp.concatenate([grad_a1, grad_f1], axis=1),
            ]
        ).reshape(tiled_shape)
        new = adamw(*masters, grad * factor, weight_rate, weight_decay)
        new = (*new, new[0].astype(b16))
    new_weights, weights_first_new, weights_second_new, weights_low = (
        a.reshape(shard_shape) for a in new
    )
    new_split, split_first_new, split_second_new = adamw(
        split_vectors, split_first, split_second, grad_split * factor, vector_rate, 0.0
    )
    new_rep, rep_first_new, rep_second_new = adamw(
        rep_vectors, rep_first, rep_second, clipped_rep, vector_rate, 0.0
    )
    return (
        block_out,
        input_grad,
        grad_norm,
        new_weights,
        weights_first_new,
        weights_second_new,
        weights_low,
        new_split,
        split_first_new,
        split_second_new,
        new_split.astype(b16),
        new_rep,
        rep_first_new,
        rep_second_new,
        new_rep.astype(b16),
        clipped_rep[:, 0, :],
    )


def solution(mesh):
    rows, packed, vector = P("dp", None, None), P(None, "tensor", "dp"), P(None, None, "dp")
    return jax.shard_map(
        per_device,
        mesh=mesh,
        in_specs=(rows, rows, P("dp", None)) + (packed,) * 6 + (vector,) * 3,
        out_specs=(rows, rows, P()) + (packed,) * 8 + (vector,) * 4 + (P(None, "dp"),),
        check_vma=False,
    )
```

```python
from functools import partial

import jax
import jax.numpy as jnp
from jax import lax
from jax.experimental import pallas as pl
from jax.experimental.pallas import tpu as pltpu
from jax.sharding import PartitionSpec as P

D = 768
HEAD_DIM = 64
LAYERS = 2
SEQ = 256
MICRO = 2
STEP = 3
HD = 384
FFT = 1536
QKV = 3 * HD
ATT = 4 * HD
COLS = ATT + 2 * FFT
VCOL = 2 * HD + FFT
LANES = 128
TILES = COLS // LANES

clip_limit = 1.0
weight_rate = 0.03
weight_decay = 0.01
vector_rate = 0.3
contract_last = (((1,), (1,)), ((), ()))
contract_first = (((0,), (0,)), ((), ()))
f32 = jnp.float32
b16 = jnp.bfloat16
VMEM_LIMIT = 13 * 1024 * 1024
VM = pl.BlockSpec(memory_space=pltpu.VMEM)


def call(body, outs, in_specs, scratch=(), flops=0, moved=0, out_specs=None, trans=0, limit=13):
    if out_specs is None:
        out_specs = [VM] * len(outs)
    return pl.pallas_call(
        body,
        out_shape=[jax.ShapeDtypeStruct(s, d) for s, d in outs],
        in_specs=in_specs,
        out_specs=out_specs,
        scratch_shapes=list(scratch),
        compiler_params=pltpu.CompilerParams(vmem_limit_bytes=limit * 1024 * 1024),
        cost_estimate=pl.CostEstimate(flops=flops, bytes_accessed=moved, transcendentals=trans),
    )


def dot(a, b, dims=(((1,), (0,)), ((), ()))):
    return lax.dot_general(a, b, dims, preferred_element_type=f32)


def norm_rows(value):
    center = value - jnp.mean(value, axis=-1, keepdims=True)
    scale = lax.rsqrt(jnp.mean(center * center, axis=-1, keepdims=True) + 1e-12)
    return center * scale, scale


def norm_back(grad_out, normed, scale, gain):
    inner = grad_out * gain
    back = scale * (
        inner
        - jnp.mean(inner, axis=-1, keepdims=True)
        - normed * jnp.mean(inner * normed, axis=-1, keepdims=True)
    )
    return (
        back,
        jnp.sum(grad_out * normed, axis=0, keepdims=True),
        jnp.sum(grad_out, axis=0, keepdims=True),
    )


def places(ring):
    me = lax.axis_index("dp")
    return lax.div(me, 4), lax.rem(lax.div(me, 2), 2), lax.rem(me, 2)


def pairs_of(ndp, kind):
    if kind in (1, 2, 3):
        return [(i, (i + 4 * kind) % ndp) for i in range(ndp)]
    if kind == "x":
        return [(i, i ^ 2) for i in range(ndp)]
    return [(i, i ^ 1) for i in range(ndp)]


def move(a, kind):
    return lax.ppermute(a, "dp", pairs_of(lax.axis_size("dp"), kind))


def exchange(a):
    return lax.ppermute(a, "tensor", [(0, 1), (1, 0)])


def after(value, *others):
    return lax.optimization_barrier((value,) + others)[0]


def tie(*arrays):
    return lax.optimization_barrier(arrays)


def unique(entries):
    entries = [e if isinstance(e, tuple) else (e, Ellipsis) for e in entries]
    arrays, at = [], []
    for array, _ in entries:
        found = [i for i, a in enumerate(arrays) if a is array]
        if not found:
            found = [len(arrays)]
            arrays.append(array)
        at.append(found[0])
    return arrays, at, [where for _, where in entries]


def stack(entries, rows, cols, lead=None):
    arrays, at, where = unique(entries)
    lead = (len(entries),) if lead is None else lead

    def body(*refs):
        for i in range(len(entries)):
            place = (i,) if len(lead) == 1 else (i // lead[1], i % lead[1])
            refs[-1][place] = refs[at[i]][where[i]]

    size = len(entries) * rows * cols
    return call(body, [(lead + (rows, cols), b16)], [VM] * len(arrays), moved=4 * size)(*arrays)[0]


def settle(mine, met):
    _, ring, rows, cols = mine.shape

    def body(mine_ref, met_ref, out_ref):
        z, x, c = places(ring)
        for other in range(2):
            source = (mine_ref, met_ref)[other]
            for xo in range(2):
                for k in range(ring):
                    zz = lax.rem(z - k + ring, ring)
                    xx = lax.rem(x + xo, 2)
                    cc = lax.rem(c + other, 2)
                    row = pl.multiple_of(((zz * 2 + xx) * 2 + cc) * rows, 16)
                    out_ref[pl.ds(row, rows), :] = source[xo, k]

    return call(
        body, [((4 * ring * rows, cols), b16)], [VM] * 2, moved=16 * ring * rows * cols
    )(mine, met)[0]


def prep(weights_tiled, rep, split):
    tiled_rows = weights_tiled.shape[1]
    rows = tiled_rows // TILES
    per = split.shape[1]

    def body(w_ref, rep_ref, split_ref, a0, f0, l1, every):
        a1, f1 = l1.at[:, :ATT], l1.at[:, ATT:]
        for layer, (a_ref, f_ref) in enumerate(((a0, f0), (a1, f1))):
            for c in range(TILES):
                piece = w_ref[layer, pl.ds(c, rows, stride=TILES), :].astype(b16)
                if c < ATT // LANES:
                    a_ref[:, c * LANES : (c + 1) * LANES] = piece
                else:
                    at = c * LANES - ATT
                    f_ref[:, at : at + LANES] = piece
        row = lax.broadcasted_iota(jnp.int32, (rows, rows), 0)
        col = lax.broadcasted_iota(jnp.int32, (rows, rows), 1)
        eye = (row == col).astype(b16)
        row3 = lax.broadcasted_iota(jnp.int32, (rows, per), 0)
        col3 = lax.broadcasted_iota(jnp.int32, (rows, per), 1)
        gap = col3 - 3 * row3
        block = jnp.zeros((rows, LANES), f32)
        lane = lax.broadcasted_iota(jnp.int32, (rows, LANES), 1)
        rep_cols = dot(eye, rep_ref[...].astype(b16), contract_last)
        rep_wide = jnp.concatenate(
            [rep_cols, jnp.zeros((rows, LANES - 6 * LAYERS), f32)], axis=1
        )
        block = rep_wide
        low = split_ref[...].astype(b16).astype(f32)
        for layer in range(LAYERS):
            for j in range(3):
                pick = jnp.where(gap == j, jnp.broadcast_to(low[layer : layer + 1], (rows, per)), 0.0)
                value = jnp.sum(pick, axis=1, keepdims=True)
                block = jnp.where(lane == 6 * LAYERS + 3 * layer + j, value, block)
        a0[:, ATT:] = block.astype(b16)
        every[:, : ATT + LANES] = a0[...]
        every[:, ATT + LANES : COLS + LANES] = f0[...]
        every[:, COLS + LANES :] = l1[...]

    return call(
        body,
        [
            ((rows, ATT + LANES), b16),
            ((rows, 2 * FFT), b16),
            ((rows, COLS), b16),
            ((rows, 2 * COLS + LANES), b16),
        ],
        [VM] * 3,
        moved=weights_tiled.size * 6,
    )(weights_tiled, rep, split)


def spread_mask(first_row, rows, first, cols):
    row = first_row + lax.broadcasted_iota(jnp.int32, (rows, cols), 0)
    col = first + lax.broadcasted_iota(jnp.int32, (rows, cols), 1)
    gap = col - 3 * row
    return jnp.where((gap >= 0) & (gap < 3), 1.0, 0.0).astype(b16)


def unpack(gathered):
    def body(w_ref, rep_ref, split_ref):
        flat = w_ref[:, ATT:]
        turned = flat.astype(f32).T
        rep_ref[...] = turned[:16]
        low = turned[:24].astype(b16)
        step = VCOL // 3
        for i in range(3):
            rows = D // 3
            mask = spread_mask(i * rows, rows, i * step, step)
            spread = dot(low[:, i * rows : (i + 1) * rows], mask)
            phase = lax.rem(lax.broadcasted_iota(jnp.int32, (1, step), 1), 3)
            for layer in range(LAYERS):
                at = 6 * LAYERS + 3 * layer
                value = jnp.where(
                    phase == 0,
                    spread[at : at + 1],
                    jnp.where(phase == 1, spread[at + 1 : at + 2], spread[at + 2 : at + 3]),
                )
                split_ref[layer : layer + 1, i * step : (i + 1) * step] = value

    return call(
        body,
        [((16, D), f32), ((8, VCOL), f32)],
        [VM],
        moved=D * LANES * 2,
        flops=24 * D * VCOL,
    )(gathered)


def gelu_parts(inner):
    cdf = 0.5 * (1.0 + lax.erf(inner * (0.5**0.5)))
    dens = jnp.exp(-0.5 * inner * inner) * 0.3989422804014327
    return inner * cdf, cdf + inner * dens


def attend(h_low, layer, w_ref, split_ref, seg_ref, part_ref, qkv_ref, probs_ref, ctx_ref):
    mixed = dot(h_low, w_ref[:, :QKV])
    qkv_ref[:, :HD] = (mixed[:, :HD] + split_ref[layer : layer + 1, :HD]).astype(b16)
    qkv_ref[:, HD : 2 * HD] = mixed[:, HD : 2 * HD].astype(b16)
    qkv_ref[:, 2 * HD :] = (
        mixed[:, 2 * HD :] + split_ref[layer : layer + 1, HD : 2 * HD]
    ).astype(b16)
    seg = jnp.broadcast_to(seg_ref[...].astype(f32), (SEQ, SEQ))
    same = seg == seg.T
    low_half = lax.broadcasted_iota(jnp.int32, (1, LANES), 1) < HEAD_DIM
    for pair in range(HD // LANES):
        at = pair * LANES
        query = qkv_ref[:, at : at + LANES].astype(f32) * HEAD_DIM ** (-0.5)
        keys = qkv_ref[:, HD + at : HD + at + LANES]
        values = qkv_ref[:, 2 * HD + at : 2 * HD + at + LANES].astype(f32)
        total = jnp.zeros((SEQ, LANES), f32)
        for half in range(2):
            mine = low_half if half == 0 else ~low_half
            scores = dot(jnp.where(mine, query, 0.0).astype(b16), keys, contract_last)
            scores = jnp.where(same, scores, -1000000000.0)
            raised = jnp.exp(scores - jnp.max(scores, axis=-1, keepdims=True))
            probs = (raised * (1.0 / jnp.sum(raised, axis=-1, keepdims=True))).astype(b16)
            probs_ref[2 * pair + half] = probs
            total = total + dot(probs, jnp.where(mine, values, 0.0).astype(b16))
        ctx_ref[:, at : at + LANES] = total.astype(b16)
    part_ref[...] = dot(ctx_ref[...], w_ref[:, QKV:ATT], contract_last).astype(b16)


ATT_FLOPS = 2 * SEQ * D * ATT + 4 * SEQ * SEQ * HD * 2
FFN_FLOPS = 2 * SEQ * D * 2 * FFT


ATT_OUTS = [((MICRO, SEQ, QKV), b16), ((MICRO, HD // HEAD_DIM, SEQ, SEQ), b16), ((MICRO, SEQ, HD), b16)]


def attention_first(block_in, segments, split, matrix):
    def body(h_ref, seg_ref, split_ref, w_ref, part_ref, qkv_ref, probs_ref, ctx_ref):
        for m in range(MICRO):
            views = [r.at[m] for r in (part_ref, qkv_ref, probs_ref, ctx_ref)]
            attend(h_ref[m], 0, w_ref, split_ref, seg_ref[m], *views)

    return call(
        body,
        [((MICRO, SEQ, D), b16)] + ATT_OUTS,
        [VM] * 4,
        flops=2 * ATT_FLOPS,
        moved=12 << 20,
        limit=16,
    )(block_in, segments, split, matrix)


def attention_next(layer, normed, part_own, part_other, rep, segments, split, matrix):
    base = 6 * (layer - 1)

    def body(n_ref, own_ref, other_ref, rep_ref, seg_ref, split_ref, w_ref, *refs):
        parts, (qkv_ref, probs_ref, ctx_ref, n2_ref, s2_ref, low_ref) = refs[:MICRO], refs[MICRO:]
        for m in range(MICRO):
            first = n_ref[m] * rep_ref[base + 1 : base + 2] + rep_ref[base + 2 : base + 3]
            added = own_ref[m].astype(f32) + other_ref[m].astype(f32)
            n2, s2 = norm_rows(first + added + rep_ref[base + 3 : base + 4])
            n2_ref[m] = n2
            s2_ref[m] = s2
            low = (n2 * rep_ref[base + 4 : base + 5] + rep_ref[base + 5 : base + 6]).astype(b16)
            low_ref[m] = low
            views = [r.at[m] for r in (qkv_ref, probs_ref, ctx_ref)]
            attend(low, layer, w_ref, split_ref, seg_ref[m], parts[m], *views)

    return call(
        body,
        [((SEQ, D), b16)] * MICRO
        + ATT_OUTS
        + [((MICRO, SEQ, D), f32), ((MICRO, SEQ, 1), f32), ((MICRO, SEQ, D), b16)],
        [VM] * 7,
        flops=2 * ATT_FLOPS,
        moved=16 << 20,
        limit=22,
    )(normed, part_own, part_other, rep, segments, split, matrix)


def feed_step(hidden_in, added, layer, rep_ref, split_ref, w_ref, outs):
    base = 6 * layer
    part_ref, n1_ref, s1_ref, low_ref, act_ref, slope_ref = outs
    n1, s1 = norm_rows(hidden_in + added + rep_ref[base : base + 1])
    n1_ref[...] = n1
    s1_ref[...] = s1
    low_ref[...] = (n1 * rep_ref[base + 1 : base + 2] + rep_ref[base + 2 : base + 3]).astype(b16)
    step = 512
    for at in range(0, FFT, step):
        inner = (
            dot(low_ref[...], w_ref[:, at : at + step])
            + split_ref[layer : layer + 1, 2 * HD + at : 2 * HD + at + step]
        )
        active, slope = gelu_parts(inner)
        act_ref[:, at : at + step] = active.astype(b16)
        slope_ref[:, at : at + step] = slope.astype(b16)
    part_ref[...] = dot(act_ref[...], w_ref[:, FFT:], contract_last).astype(b16)


FEED_OUTS = [
    ((SEQ, D), b16),
    ((SEQ, D), f32),
    ((SEQ, 1), f32),
    ((SEQ, D), b16),
    ((SEQ, FFT), b16),
    ((SEQ, FFT), b16),
]


def feed_first(hidden, part_own, part_other, rep, split, matrix):
    def body(h_ref, own_ref, other_ref, rep_ref, split_ref, w_ref, *outs):
        for m in range(MICRO):
            added = own_ref[m].astype(f32) + other_ref[m].astype(f32)
            views = [r.at[m] for r in outs]
            feed_step(h_ref[m].astype(f32), added, 0, rep_ref, split_ref, w_ref, views)

    return call(
        body,
        [((MICRO,) + shape, kind) for shape, kind in FEED_OUTS],
        [VM] * 6,
        flops=2 * FFN_FLOPS,
        moved=20 << 20,
        limit=22,
    )(hidden, part_own, part_other, rep, split, matrix)


def feed_forward(micro, layer, hidden, part_own, part_other, rep, split, matrix):
    base = 6 * layer

    def body(h_ref, own_ref, other_ref, rep_ref, split_ref, w_ref, *outs):
        hidden_in = h_ref[micro] * rep_ref[base - 2 : base - 1] + rep_ref[base - 1 : base]
        added = own_ref[...].astype(f32) + other_ref[...].astype(f32)
        feed_step(hidden_in, added, layer, rep_ref, split_ref, w_ref, outs)

    return call(
        body,
        FEED_OUTS,
        [VM] * 6,
        flops=FFN_FLOPS,
        moved=10 << 20,
    )(hidden, part_own, part_other, rep, split, matrix)


def view(ref, micro):
    return ref.at[micro] if ref.shape[0] == MICRO else ref


def feed_back_tail(grad, n2, s2, layer, rep_ref, slope_ref, w_ref, outs):
    base = 6 * layer
    part_ref, res_ref, dffn_ref, din_ref, vec_ref = outs
    back, gain, shift = norm_back(grad, n2, s2, rep_ref[base + 4 : base + 5])
    res_ref[...] = back
    dffn_ref[...] = back.astype(b16)
    vec_ref[...] = jnp.zeros_like(vec_ref)
    vec_ref[0:1] = jnp.sum(back, axis=0, keepdims=True)
    vec_ref[1:2] = gain
    vec_ref[2:3] = shift
    step = 384
    for at in range(0, FFT, step):
        grad_act = dot(dffn_ref[...], w_ref[:, FFT + at : FFT + at + step])
        grad_in = (slope_ref[:, at : at + step].astype(f32) * grad_act).astype(b16)
        din_ref[:, at : at + step] = grad_in
        row, lane = 3 + at // D, at % D
        vec_ref[row : row + 1, lane : lane + step] = jnp.sum(
            grad_in.astype(f32), axis=0, keepdims=True
        )
    part_ref[...] = dot(din_ref[...], w_ref[:, :FFT], contract_last).astype(b16)


BACK_OUTS = [
    ((SEQ, D), b16),
    ((SEQ, D), f32),
    ((SEQ, D), b16),
    ((SEQ, FFT), b16),
    ((8, D), f32),
]


def feed_back_top(micro, layer, out_grad, n1, part_own, part_other, rep, slope, matrix):
    base = 6 * layer

    def body(g_ref, n_ref, own_ref, other_ref, rep_ref, slope_ref, w_ref, *refs):
        out_ref = refs[5]
        first = n_ref[...] * rep_ref[base + 1 : base + 2] + rep_ref[base + 2 : base + 3]
        added = own_ref[...].astype(f32) + other_ref[...].astype(f32)
        n2, s2 = norm_rows(first + added + rep_ref[base + 3 : base + 4])
        out_ref[...] = (n2 * rep_ref[base + 4 : base + 5] + rep_ref[base + 5 : base + 6]).astype(b16)
        feed_back_tail(
            g_ref[micro].astype(f32), n2, s2, layer, rep_ref, slope_ref, w_ref, refs[:5]
        )

    return call(
        body,
        BACK_OUTS + [((SEQ, D), b16)],
        [VM] * 6 + [VM],
        flops=FFN_FLOPS,
        moved=11 << 20,
    )(out_grad, n1, part_own, part_other, rep, slope, matrix)


def feed_back(micro, layer, mid, part_own, part_other, n2, s2, rep, slope, matrix):
    def body(mid_ref, own_ref, other_ref, n2_ref, s2_ref, rep_ref, slope_ref, w_ref, *refs):
        added = own_ref[...].astype(f32) + other_ref[...].astype(f32)
        feed_back_tail(
            mid_ref[...] + added,
            view(n2_ref, micro)[...],
            view(s2_ref, micro)[...],
            layer,
            rep_ref,
            view(slope_ref, micro),
            w_ref,
            refs[:5],
        )

    return call(
        body,
        BACK_OUTS,
        [VM] * 7 + [VM],
        flops=FFN_FLOPS,
        moved=11 << 20,
    )(mid, part_own, part_other, n2, s2, rep, slope, matrix)


def attention_back(micro, layer, res, part_own, part_other, n1, s1, rep, qkv, probs, ctx, matrix):
    base = 6 * layer

    def body(
        res_ref, own_ref, other_ref, n1_ref, s1_ref, rep_ref, qkv_ref, probs_ref, ctx_ref, w_ref, *refs
    ):
        part_ref, mid_ref, datt_ref, dqkv_ref, vec_ref = refs
        n1_ref, s1_ref, qkv_ref, probs_ref, ctx_ref = (
            view(r, micro) for r in (n1_ref, s1_ref, qkv_ref, probs_ref, ctx_ref)
        )
        grad = res_ref[...] + (own_ref[...].astype(f32) + other_ref[...].astype(f32))
        back, gain, shift = norm_back(grad, n1_ref[...], s1_ref[...], rep_ref[base + 1 : base + 2])
        mid_ref[...] = back
        datt_ref[...] = back.astype(b16)
        vec_ref[...] = jnp.zeros_like(vec_ref)
        vec_ref[0:1] = jnp.sum(back, axis=0, keepdims=True)
        vec_ref[1:2] = gain
        vec_ref[2:3] = shift
        dctx = dot(datt_ref[...], w_ref[:, QKV:ATT]).astype(b16).astype(f32)
        low_half = lax.broadcasted_iota(jnp.int32, (1, LANES), 1) < HEAD_DIM
        factor = HEAD_DIM ** (-0.5)
        for pair in range(HD // LANES):
            at = pair * LANES
            query = qkv_ref[:, at : at + LANES].astype(f32) * factor
            keys = qkv_ref[:, HD + at : HD + at + LANES].astype(f32) * factor
            values = qkv_ref[:, 2 * HD + at : 2 * HD + at + LANES]
            dc = dctx[:, at : at + LANES]
            weighed = dc * ctx_ref[:, at : at + LANES].astype(f32)
            dq = jnp.zeros((SEQ, LANES), f32)
            dk = jnp.zeros((SEQ, LANES), f32)
            dv = jnp.zeros((SEQ, LANES), f32)
            for half in range(2):
                mine = low_half if half == 0 else ~low_half
                dcm = jnp.where(mine, dc, 0.0).astype(b16)
                delta = jnp.sum(jnp.where(mine, weighed, 0.0), axis=-1, keepdims=True)
                probs = probs_ref[2 * pair + half]
                dprobs = dot(dcm, values, contract_last)
                dscores = (probs.astype(f32) * (dprobs - delta)).astype(b16)
                dq = dq + dot(dscores, jnp.where(mine, keys, 0.0).astype(b16))
                dk = dk + dot(dscores, jnp.where(mine, query, 0.0).astype(b16), contract_first)
                dv = dv + dot(probs, dcm, contract_first)
            dqkv_ref[:, at : at + LANES] = dq.astype(b16)
            dqkv_ref[:, HD + at : HD + at + LANES] = dk.astype(b16)
            dqkv_ref[:, 2 * HD + at : 2 * HD + at + LANES] = dv.astype(b16)
        vec_ref[3:4, :HD] = jnp.sum(dqkv_ref[:, :HD].astype(f32), axis=0, keepdims=True)
        vec_ref[3:4, HD:] = jnp.sum(dqkv_ref[:, 2 * HD :].astype(f32), axis=0, keepdims=True)
        part_ref[...] = dot(dqkv_ref[...], w_ref[:, :QKV], contract_last).astype(b16)

    return call(
        body,
        [
            ((SEQ, D), b16),
            ((SEQ, D), f32),
            ((SEQ, D), b16),
            ((SEQ, QKV), b16),
            ((8, D), f32),
        ],
        [VM] * 9 + [VM],
        flops=2 * ATT_FLOPS,
        moved=9 << 20,
    )(res, part_own, part_other, n1, s1, rep, qkv, probs, ctx, matrix)


def finish_input(mids, owns, others):
    def body(*refs):
        for micro in range(MICRO):
            m, a, b = refs[3 * micro : 3 * micro + 3]
            refs[-1][micro] = m[...] + (a[...].astype(f32) + b[...].astype(f32))

    args = []
    for micro in range(MICRO):
        args += [mids[micro], owns[micro], others[micro]]
    return call(body, [((MICRO, SEQ, D), f32)], [VM] * len(args), moved=7 << 20)(*args)[0]


def store_slots(product_ref, outs, at, width):
    if len(outs) == 1:
        outs[0][:, at : at + width] = product_ref[:, :width].astype(b16)
        return
    ring, rows = outs[0].shape[1], outs[0].shape[2]
    z, x, c = places(ring)
    for other in range(2):
        for xo in range(2):
            for k in range(ring):
                zz = lax.rem(z + k, ring)
                xx = lax.rem(x + xo, 2)
                cc = lax.rem(c + other, 2)
                row = pl.multiple_of(((zz * 2 + xx) * 2 + cc) * rows, 16)
                outs[other][xo, k, :, at : at + width] = product_ref[
                    pl.ds(row, rows), :width
                ].astype(b16)


def grad_outs(ndp, pieced, cols):
    rows = D // ndp
    if pieced:
        return [((2, ndp // 4, rows, cols), b16)] * 2
    return [((D, cols), b16)]


def matrix_gradient(sets, pieced, ndp, vectors=None):
    widths = [s[2] for s in sets]
    total = sum(widths) + (LANES if vectors is not None else 0)
    outs = grad_outs(ndp, pieced, total)
    args, specs = [], []
    for left, right, _ in sets:
        for micro in range(MICRO):
            specs.append(VM)
            args.append(left[micro])
        for micro in range(MICRO):
            args.append(right[micro])
            specs.append(VM)
    plain = len(args)
    if vectors is not None:
        args += vectors
        specs += [VM] * len(vectors)
    n_in = len(args)
    step = 384

    def body(*refs):
        out_refs = refs[n_in : n_in + len(outs)]
        prod_ref = refs[n_in + len(outs)]
        at = 0
        for index, width in enumerate(widths):
            l0, l1, r0, r1 = refs[4 * index : 4 * index + 4]
            left = [r[m] if len(r.shape) == 3 else r[...] for m, r in enumerate((l0, l1))]
            r0, r1 = (r.at[m] if len(r.shape) == 3 else r for m, r in enumerate((r0, r1)))
            for col in range(0, width, step):
                prod_ref[...] = dot(left[0], r0[:, col : col + step], contract_first) + dot(
                    left[1], r1[:, col : col + step], contract_first
                )
                store_slots(prod_ref, out_refs, at, step)
                at += step
        if vectors is not None:
            pack_vectors(refs[plain:n_in], prod_ref)
            store_slots(prod_ref, out_refs, at, LANES)

    moved = sum(a.size * 2 for a in args[:plain]) + D * total * 2
    return call(
        body,
        outs,
        specs,
        [pltpu.VMEM((D, step), f32)],
        flops=2 * MICRO * SEQ * D * total,
        moved=moved,
    )(*args)


def pack_vectors(vec_refs, prod_ref):
    sums = []
    for layer in range(LAYERS):
        a0, a1, b0, b1 = vec_refs[4 * layer : 4 * layer + 4]
        sums.append((a0[...] + a1[...], b0[...] + b1[...]))
    rows = []
    for att, ffn in sums:
        rows += [att[0:1], att[1:2], att[2:3], ffn[0:1], ffn[1:2], ffn[2:3]]
    rows.append(jnp.zeros((4, D), f32))
    turned = jnp.concatenate(rows, axis=0)
    turned = jnp.concatenate([turned, jnp.zeros((LANES - 16, D), f32)], axis=0).T
    step = VCOL // 3
    phase = lax.rem(lax.broadcasted_iota(jnp.int32, (1, step), 1), 3)
    lane = lax.broadcasted_iota(jnp.int32, (1, LANES), 1)
    for i in range(3):
        picked = []
        for att, ffn in sums:
            line = (att[3:4], ffn[3:4], ffn[4:5])[i]
            for j in range(3):
                picked.append(jnp.where(phase == j, line, 0.0))
        picked = jnp.concatenate(
            [jnp.zeros((12, step), f32)] + picked + [jnp.zeros((LANES - 18, step), f32)], axis=0
        ).astype(b16)
        n_rows = D // 3
        mask = spread_mask(i * n_rows, n_rows, i * step, step)
        part = dot(mask, picked, contract_last)
        keep = turned[i * n_rows : (i + 1) * n_rows]
        prod_ref[i * n_rows : (i + 1) * n_rows, :LANES] = jnp.where(lane < 12, keep, part)


def meet(own, met, places):
    lo, hi = places[0], places[-1] + 1
    return (own[1, lo:hi].astype(f32) + met[1, lo:hi].astype(f32)).astype(b16)


def pass_on(own, met, got, places):
    lo, hi = places[0], places[-1] + 1
    total = own[0, lo:hi].astype(f32) + met[0, lo:hi].astype(f32) + got.astype(f32)
    return [total[i].astype(b16) for i in range(hi - lo)]


def pass_both(own, met, k, received=None):
    total = own[:, k].astype(f32) + met[:, k].astype(f32)
    if received is not None:
        total = total + received.astype(f32)
    return total.astype(b16)


def close(own, met, parts, vectors=False):
    _, _, rows, cols = own.shape
    mats = cols - LANES if vectors else cols
    parts = [p if isinstance(p, tuple) else (p, None) for p in parts]
    n = len(parts)

    def body(own_ref, met_ref, *refs):
        out_ref, sq_ref = refs[n:]
        total = jnp.zeros((rows, LANES), f32)
        for at in range(0, cols, LANES):
            s = slice(at, at + LANES)
            value = own_ref[0, 0, :, s].astype(f32) + met_ref[0, 0, :, s].astype(f32)
            for (_, index), ref in zip(parts, refs[:n]):
                value = value + (ref[:, s] if index is None else ref[index, :, s]).astype(f32)
            out_ref[:, s] = value
            square = value * value
            if at >= mats:
                lane = lax.broadcasted_iota(jnp.int32, (rows, LANES), 1)
                twice = (lane < 6 * LAYERS) & (lax.axis_index("tensor") != 0)
                square = jnp.where(twice, 0.0, square)
            total = total + square
        part = total[:8]
        for i in range(8, rows, 8):
            part = part + total[i : i + 8]
        sq_ref[...] = part

    return call(
        body,
        [((rows, cols), f32), ((8, LANES), f32)],
        [VM] * (2 + n),
        moved=rows * cols * 14,
    )(own, met, *[p[0] for p in parts])


def adamw(value, first, second, grad, rate, decay):
    first = 0.5 * first + 0.5 * grad
    second = 0.5 * second + 0.5 * grad * grad
    correct = 1.0 - 0.5**STEP
    direction = first / correct / (jnp.sqrt(second / correct) + 1e-08)
    return (value - rate * (direction + decay * value), first, second)


def clip_factor(squares):
    norm = jnp.sqrt(jnp.sum(squares, keepdims=True))
    return norm, jnp.minimum(1.0, clip_limit / (norm + 1e-06))


def ready(tiled, first, second):
    def body(w_ref, m_ref, v_ref, w_out, m_out, v_out):
        w_out[...] = w_ref[...] * (1.0 - weight_rate * weight_decay)
        m_out[...] = 0.5 * m_ref[...]
        v_out[...] = 0.5 * v_ref[...]

    return call(body, [(tiled.shape, f32)] * 3, [VM] * 3, moved=24 * tiled.size)(tiled, first, second)


def stepped(decayed, half_first, half_second, grad, rate):
    first = half_first + 0.5 * grad
    second = half_second + 0.5 * grad * grad
    correct = 1.0 - 0.5**STEP
    direction = first / correct / (jnp.sqrt(second / correct) + 1e-08)
    return decayed - rate * direction, first, second


def update_vectors(block, squares, reps, splits):
    rows = block.shape[0]
    per = splits[0].shape[2]

    def body(b_ref, q_ref, rw, rm, rv, sw, sm, sv, norm_ref, rwo, rmo, rvo, rlo, go, swo, smo, svo, slo):
        norm, scale = clip_factor(q_ref[...])
        norm_ref[...] = norm
        turned = jnp.concatenate([b_ref[...], jnp.zeros((LANES - rows, LANES), f32)], axis=0).T
        for layer in range(LAYERS):
            at = slice(layer, layer + 1)
            for kind in range(6):
                grad = turned[6 * layer + kind : 6 * layer + kind + 1, :rows] * scale
                new = adamw(rw[kind, at], rm[kind, at], rv[kind, at], grad, vector_rate, 0.0)
                rwo[kind, at], rmo[kind, at], rvo[kind, at] = new
                rlo[kind, at] = new[0].astype(b16)
                if kind == 0:
                    go[at] = grad
        row = lax.broadcasted_iota(jnp.int32, (rows, per), 0)
        col = lax.broadcasted_iota(jnp.int32, (rows, per), 1)
        gap = col - 3 * row
        mask = jnp.where((gap >= 0) & (gap < 3), 1.0, 0.0)
        wide = lax.dot_general(
            turned[6 * LAYERS : 6 * LAYERS + 8, :rows],
            mask,
            (((1,), (0,)), ((), ())),
            preferred_element_type=f32,
            precision=lax.Precision.HIGHEST,
        )
        phase = lax.rem(lax.broadcasted_iota(jnp.int32, (1, per), 1), 3)
        for layer in range(LAYERS):
            one, two, three = (wide[3 * layer + j : 3 * layer + j + 1] for j in range(3))
            grad = jnp.where(phase == 0, one, jnp.where(phase == 1, two, three)) * scale
            new = adamw(sw[layer], sm[layer], sv[layer], grad, vector_rate, 0.0)
            swo[layer], smo[layer], svo[layer] = new
            slo[layer] = new[0].astype(b16)

    rep, split = reps[0].shape, splits[0].shape
    return call(
        body,
        [((1, 1), f32)]
        + [(rep, f32)] * 3
        + [(rep, b16), ((LAYERS, rows), f32)]
        + [(split, f32)] * 3
        + [(split, b16)],
        [VM] * 8,
        moved=1 << 18,
    )(block, squares, *reps, *splits)


def update_matrices(decayed, first, second, grads, squares):
    rows = grads[0].shape[0]
    tiled = decayed
    step = 8 if rows % 8 == 0 else rows
    n_steps = rows // step
    block = (1, step * TILES, LANES)

    def body(f_ref, w_ref, m_ref, v_ref, a0, f0, a1, f1, nw, nm, nv, nl):
        scale = clip_factor(f_ref[...])[1]
        layer = pl.program_id(0)
        for c in range(TILES):
            if c < ATT // LANES:
                lo = c * LANES
                grad = jnp.where(layer == 0, a0[:, lo : lo + LANES], a1[:, lo : lo + LANES])
            else:
                lo = c * LANES - ATT
                grad = jnp.where(layer == 0, f0[:, lo : lo + LANES], f1[:, lo : lo + LANES])
            where = (0, pl.ds(c, step, stride=TILES), slice(None))
            new = stepped(w_ref[where], m_ref[where], v_ref[where], grad * scale, weight_rate)
            nw[where], nm[where], nv[where] = new
        nl[...] = nw[...].astype(b16)

    big = pl.BlockSpec(block, lambda l, i: (l, i, 0))
    shape = tiled.shape
    return pl.pallas_call(
        body,
        grid=(LAYERS, n_steps),
        out_shape=[jax.ShapeDtypeStruct(shape, f32)] * 3 + [jax.ShapeDtypeStruct(shape, b16)],
        in_specs=[pl.BlockSpec((8, LANES), lambda l, i: (0, 0)), big, big, big]
        + [pl.BlockSpec((step, g.shape[1]), lambda l, i: (i, 0)) for g in grads],
        out_specs=[big] * 4,
        compiler_params=pltpu.CompilerParams(vmem_limit_bytes=VMEM_LIMIT),
        cost_estimate=pl.CostEstimate(
            flops=20 * tiled.size, bytes_accessed=30 * tiled.size, transcendentals=tiled.size
        ),
    )(squares, tiled, first, second, *grads)


def sum_everywhere(value):
    ndp = lax.axis_size("dp")
    if ndp & (ndp - 1) or ndp < 4:
        return lax.psum(value, ("dp", "tensor"))

    def level(a, first, second):
        one, two, both = ppermute_bits(a, first), ppermute_bits(a, second), ppermute_bits(a, first | second)
        return (a + one) + (two + both)

    value = value + ppermute_bits(value, 2)
    value = level(value, 4, 1)
    bit = 8
    while bit < 2 * ndp:
        if 2 * bit < 2 * ndp:
            value = level(value, bit, 2 * bit)
        else:
            value = value + ppermute_bits(value, bit)
        bit *= 4
    return value


def ppermute_bits(value, bits):
    n = 2 * lax.axis_size("dp")
    return lax.ppermute(value, ("dp", "tensor"), [(i, i ^ bits) for i in range(n)])


def per_device(
    block_in,
    out_grad,
    segments,
    weights,
    weights_first,
    weights_second,
    split_vectors,
    split_first,
    split_second,
    rep_vectors,
    rep_first,
    rep_second,
):
    ndp = lax.axis_size("dp")
    rows = D // ndp
    per = split_vectors.shape[2]
    pieced = ndp == 16 and rows % 16 == 0
    shard_shape = weights.shape
    tiled_shape = (LAYERS, -1, LANES)
    masters = [a.reshape(tiled_shape) for a in (weights, weights_first, weights_second)]
    weights_tiled = masters[0]
    rep_flat = rep_vectors.reshape(LAYERS * 6, -1)
    split_flat = split_vectors.reshape(LAYERS, per)
    both = range(MICRO)
    seg = segments.reshape(MICRO, 1, SEQ)
    if pieced:
        a0, f0, l1, every = prep(weights_tiled, rep_flat, split_flat)
        across = partial(move, kind="x")
        third = slice(COLS + LANES, COLS + LANES + ATT)
        fourth = slice(COLS + LANES + ATT, None)

        def finish(slots, cols):
            mine = stack(slots, rows, cols, (2, 4))
            return settle(mine, move(mine, "core"))

        def cut(array, cols):
            return (array, (slice(None), cols))

        x0 = across(every)
        a0_r1, a0_r2, a0_r3, f0 = tie(move(a0, 1), move(a0, 2), move(a0, 3), f0)
        a0_x = across(stack([a0_r1, a0_r2, a0_r3], rows, ATT + LANES))
        f0_r1, f0_r3 = move(f0, 1), move(f0, 3)
        mine0 = stack(
            [a0, a0_r1, a0_r2, a0_r3, cut(x0, slice(0, ATT + LANES)), (a0_x, 0), (a0_x, 1), (a0_x, 2)],
            rows,
            ATT + LANES,
            (2, 4),
        )
        mine0, f0_r1, f0_r3, l1 = tie(mine0, f0_r1, f0_r3, l1)
        watt0 = settle(mine0, move(mine0, "core"))
        f0_x13 = across(stack([f0_r1, f0_r3], rows, 2 * FFT))
        f0_r2 = move(f0_r1, 1)
        l1_r1, l1_r3 = move(l1, 1), move(l1, 3)
        f0_x2 = across(f0_r2)
    else:
        low = weights.astype(b16).reshape(LAYERS, rows, COLS)
        block = jnp.concatenate(
            [
                rep_flat.T,
                split_flat.reshape(LAYERS, rows, 3).transpose(1, 0, 2).reshape(rows, 6),
                jnp.zeros((rows, LANES - 18), f32),
            ],
            axis=1,
        ).astype(b16)
        gather = partial(lax.all_gather, axis_name="dp", axis=0, tiled=True)
        watt0 = gather(jnp.concatenate([low[0, :, :ATT], block], axis=1))
        watt1 = gather(low[1, :, :ATT])
        wffn0, wffn1 = (gather(low[layer, :, ATT:]) for layer in range(LAYERS))
    rep, split = unpack(watt0)

    done, qkv0, probs0, ctx0 = attention_first(block_in, seg, split, watt0)
    met = exchange(done)
    if pieced:
        f0_x13, f0_x2, l1_r1, l1_r3, met = tie(f0_x13, f0_x2, l1_r1, l1_r3, met)
        a1_x13 = across(stack([cut(l1_r1, slice(0, ATT)), cut(l1_r3, slice(0, ATT))], rows, ATT))
        l1_r2 = move(l1_r1, 1)
        wffn0 = finish(
            [f0, f0_r1, f0_r2, f0_r3]
            + [cut(x0, slice(ATT + LANES, COLS + LANES)), (f0_x13, 0), f0_x2, (f0_x13, 1)],
            2 * FFT,
        )
    done, n1_0, s1_0, low1_0, act0, slope0 = feed_first(block_in, done, met, rep, split, wffn0)
    if pieced:
        a1_x13, l1_r2, done = tie(a1_x13, l1_r2, done)
        head, tail = slice(0, ATT), slice(ATT, None)
        a1_x2 = across(stack([cut(l1_r2, head)], rows, ATT))
        f1_x13 = across(stack([cut(l1_r1, tail), cut(l1_r3, tail)], rows, 2 * FFT))
        watt1 = finish(
            [cut(r, head) for r in (l1, l1_r1, l1_r2, l1_r3)]
            + [cut(x0, third), (a1_x13, 0), (a1_x2, 0), (a1_x13, 1)],
            ATT,
        )
    met = exchange(done)
    if pieced:
        f1_x13, met = tie(f1_x13, met)
    out = attention_next(1, n1_0, done, met, rep, seg, split, watt1)
    done, (qkv1, probs1, ctx1, n2_0, s2_0, low_h1) = list(out[:MICRO]), out[MICRO:]
    if pieced:
        f1_x2 = across(stack([cut(l1_r2, tail)], rows, 2 * FFT))
        wffn1 = finish(
            [cut(r, tail) for r in (l1, l1_r1, l1_r2, l1_r3)]
            + [cut(x0, fourth), (f1_x13, 0), (f1_x2, 0), (f1_x13, 1)],
            2 * FFT,
        )
    met = [exchange(a) for a in done]
    out = [feed_forward(m, 1, n2_0, done[m], met[m], rep, split, wffn1) for m in both]
    n1_1, s1_1, low1_1, act1, slope1 = ([o[i] for o in out] for i in range(1, 6))
    met = [exchange(o[0]) for o in out]

    out = [
        feed_back_top(m, 1, out_grad, n1_1[m], out[m][0], met[m], rep, slope1[m], wffn1)
        for m in both
    ]
    res, dffn, din, vec_f1 = ([o[i] for o in out] for i in range(1, 5))
    block_out = jnp.stack([o[5] for o in out])
    done = [o[0] for o in out]
    met = [exchange(o[0]) for o in out]
    g_f1 = matrix_gradient([(low1_1, din, FFT), (dffn, act1, FFT)], pieced, ndp)
    res[0] = after(res[0], g_f1[0])

    def back_1(m):
        return attention_back(
            m, 1, res[m], done[m], met[m], n1_1[m], s1_1[m], rep, qkv1, probs1, ctx1, watt1
        )

    out = [back_1(0)]
    if pieced:
        f1_own, f1_met = g_f1[0], move(g_f1[1], "core")
        f1_t = pass_both(f1_own, after(f1_met, out[0][0]), 3)
        f1_rec = move(f1_t, 1)
        res[1] = after(res[1], f1_t)
    out += [back_1(1)]
    mid, datt, dqkv, vec_a1 = ([o[i] for o in out] for i in range(1, 5))
    done = [o[0] for o in out]
    met = [exchange(o[0]) for o in out]
    g_a1 = matrix_gradient([([low_h1] * 2, dqkv, QKV), (datt, [ctx1] * 2, HD)], pieced, ndp)
    mid[0] = after(mid[0], g_a1[0])
    def back_2(m):
        return feed_back(m, 0, mid[m], done[m], met[m], n2_0, s2_0, rep, slope0, wffn0)

    out = [back_2(0)]
    if pieced:
        a1_own, a1_met = g_a1[0], move(g_a1[1], "core")
        a1_s = meet(a1_own, after(a1_met, out[0][0]), (0, 1, 2, 3))
        a1_got = across(a1_s)
        f1_t = pass_both(f1_own, f1_met, 2, after(f1_rec, out[0][0]))
        f1_rec = move(f1_t, 1)
        mid[1] = after(mid[1], a1_s, f1_t)
    out += [back_2(1)]
    res, dffn, din, vec_f0 = ([o[i] for o in out] for i in range(1, 5))
    done = [o[0] for o in out]
    met = [exchange(o[0]) for o in out]
    g_f0 = matrix_gradient([([low1_0] * 2, din, FFT), (dffn, [act0] * 2, FFT)], pieced, ndp)
    res[0] = after(res[0], g_f0[0])
    if pieced:
        f1_t = pass_both(f1_own, f1_met, 1, after(f1_rec, g_f0[0]))
        f1_rec = move(f1_t, 1)
        res[0] = after(res[0], f1_t)

    def back_3(m):
        return attention_back(
            m, 0, res[m], done[m], met[m], n1_0, s1_0, rep, qkv0, probs0, ctx0, watt0
        )

    out = [back_3(0)]
    if pieced:
        f0_own, f0_met = g_f0[0], move(g_f0[1], "core")
        f0_s = meet(f0_own, after(f0_met, out[0][0]), (2, 3))
        f0_got_hi = across(f0_s)
        a1_t1, a1_t2, a1_t3 = pass_on(a1_own, a1_met, after(a1_got, out[0][0])[1:], (1, 2, 3))
        a1_r = [move(t, k) for k, t in ((1, a1_t1), (2, a1_t2), (3, a1_t3))]
        res[1] = after(res[1], f0_s, a1_t3)
    out += [back_3(1)]
    mid, datt, dqkv, vec_a0 = ([o[i] for o in out] for i in range(1, 5))
    done = [o[0] for o in out]
    met = [exchange(o[0]) for o in out]
    g_a0 = matrix_gradient(
        [([block_in] * MICRO, dqkv, QKV), (datt, [ctx0] * 2, HD)],
        pieced,
        ndp,
        vectors=vec_a0 + vec_f0 + vec_a1 + vec_f1,
    )
    if pieced:
        masters = ready(*(after(a, g_a0[0]) for a in masters))
        input_grad = finish_input(mid, done, met)
        a0_own, a0_met = g_a0[0], move(g_a0[1], "core")
        a0_s, f0_got_hi, f1_rec = tie(meet(a0_own, a0_met, (0, 1, 2, 3)), f0_got_hi, f1_rec)
        a0_got = across(a0_s)
        f1_last = pass_both(f1_own, f1_met, 0, f1_rec)
        f1_got = across(f1_last[1])
        f0_t2, f0_t3 = pass_on(f0_own, f0_met, f0_got_hi, (2, 3))
        f0_r3, f0_r2 = move(f0_t3, 3), move(f0_t2, 2)
        a0_got, f0_r3, f0_r2, *a1_r = tie(a0_got, f0_r3, f0_r2, *a1_r)
        f0_got_lo = across(meet(f0_own, f0_met, (0, 1)))
        a0_t = pass_on(a0_own, a0_met, a0_got[1:], (1, 2, 3))
        a0_r = [move(t, k + 1) for k, t in enumerate(a0_t)]
        grad_a1, sq_a1 = close(a1_own, a1_met, [(a1_got, 0)] + a1_r)
        grad_f1, sq_f1 = close(f1_own, f1_met, [f1_got, (f1_rec, 0)])
        f0_got_lo, grad_f1, grad_a1, block_out, input_grad, *rest = tie(
            f0_got_lo, grad_f1, grad_a1, block_out, input_grad, *a0_r, *masters
        )
        a0_r, masters = rest[:3], rest[3:]
        f0_r1 = move(pass_on(f0_own, f0_met, f0_got_lo[1:], (1,))[0], 1)
        grad_a0, sq_a0 = close(a0_own, a0_met, [(a0_got, 0)] + a0_r, vectors=True)
        grad_f0, sq_f0 = close(f0_own, f0_met, [(f0_got_lo, 0), f0_r1, f0_r2, f0_r3])
        squares = (sq_f1 + sq_a1) + (sq_f0 + sq_a0)
    else:
        input_grad = finish_input(mid, done, met)
        scatter = lambda g: lax.psum_scatter(g[0], "dp", scatter_dimension=0, tiled=True).astype(f32)
        grad_f1, grad_a1, grad_f0, grad_a0 = (scatter(g) for g in (g_f1, g_a1, g_f0, g_a0))
        once = jnp.where(lax.axis_index("tensor") == 0, 1.0, 0.0).astype(f32)
        square = lambda a: jnp.sum(a * a)
        squares = (
            square(grad_a0[:, :ATT])
            + square(grad_f0)
            + square(grad_a1)
            + square(grad_f1)
            + square(grad_a0[:, ATT + 12 :])
            + once * square(grad_a0[:, ATT : ATT + 12])
        )
        squares = jnp.full((8, LANES), squares / (8 * LANES), f32)

    squares = sum_everywhere(squares)
    if pieced:
        new = update_matrices(*masters, [grad_a0, grad_f0, grad_a1, grad_f1], squares)
        turn = lambda a: jnp.transpose(a, (1, 0, 2))
        vectors = update_vectors(
            grad_a0[:, ATT:],
            squares,
            [turn(a) for a in (rep_vectors, rep_first, rep_second)],
            (split_vectors, split_first, split_second),
        )
        grad_norm = vectors[0][0, 0]
        new_rep, rep_first_new, rep_second_new, rep_low = (turn(a) for a in vectors[1:5])
        bias_grad = vectors[5]
        new_split, split_first_new, split_second_new, split_low = vectors[6:]
    else:
        block = grad_a0[:, ATT:]
        grad_rep = block[:, :12].T.reshape(rep_vectors.shape)
        grad_split = (
            block[:, 12:18].reshape(rows, LAYERS, 3).transpose(1, 0, 2).reshape(split_vectors.shape)
        )
        grad_norm, factor = (a[0, 0] for a in clip_factor(squares))
        clipped_rep = grad_rep * factor
        grad = jnp.stack(
            [
                jnp.concatenate([grad_a0[:, :ATT], grad_f0], axis=1),
                jnp.concatenate([grad_a1, grad_f1], axis=1),
            ]
        ).reshape(tiled_shape)
        new = adamw(*masters, grad * factor, weight_rate, weight_decay)
        new = (*new, new[0].astype(b16))
        new_split, split_first_new, split_second_new = adamw(
            split_vectors, split_first, split_second, grad_split * factor, vector_rate, 0.0
        )
        new_rep, rep_first_new, rep_second_new = adamw(
            rep_vectors, rep_first, rep_second, clipped_rep, vector_rate, 0.0
        )
        split_low, rep_low = new_split.astype(b16), new_rep.astype(b16)
        bias_grad = clipped_rep[:, 0, :]
    new_weights, weights_first_new, weights_second_new, weights_low = (
        a.reshape(shard_shape) for a in new
    )
    return (
        block_out,
        input_grad,
        grad_norm,
        new_weights,
        weights_first_new,
        weights_second_new,
        weights_low,
        new_split,
        split_first_new,
        split_second_new,
        split_low,
        new_rep,
        rep_first_new,
        rep_second_new,
        rep_low,
        bias_grad,
    )


def solution(mesh):
    rows, packed, vector = P("dp", None, None), P(None, "tensor", "dp"), P(None, None, "dp")
    return jax.shard_map(
        per_device,
        mesh=mesh,
        in_specs=(rows, rows, P("dp", None)) + (packed,) * 6 + (vector,) * 3,
        out_specs=(rows, rows, P()) + (packed,) * 8 + (vector,) * 4 + (P(None, "dp"),),
        check_vma=False,
    )
```

```python
from functools import partial

import jax
import jax.numpy as jnp
from jax import lax
from jax.experimental import pallas as pl
from jax.experimental.pallas import tpu as pltpu
from jax.sharding import PartitionSpec as P

D = 768
HEAD_DIM = 64
LAYERS = 2
SEQ = 256
MICRO = 2
STEP = 3
HD = 384
FFT = 1536
QKV = 3 * HD
ATT = 4 * HD
COLS = ATT + 2 * FFT
VCOL = 2 * HD + FFT
LANES = 128
TILES = COLS // LANES

clip_limit = 1.0
weight_rate = 0.03
weight_decay = 0.01
vector_rate = 0.3
contract_last = (((1,), (1,)), ((), ()))
contract_first = (((0,), (0,)), ((), ()))
f32 = jnp.float32
b16 = jnp.bfloat16
VMEM_LIMIT = 13 * 1024 * 1024
VM = pl.BlockSpec(memory_space=pltpu.VMEM)


def call(body, outs, in_specs, scratch=(), flops=0, moved=0, out_specs=None, trans=0, limit=13):
    weight = 16 if scratch else 16 if flops else 1
    if out_specs is None:
        out_specs = [VM] * len(outs)
    return pl.pallas_call(
        body,
        out_shape=[jax.ShapeDtypeStruct(s, d) for s, d in outs],
        in_specs=in_specs,
        out_specs=out_specs,
        scratch_shapes=list(scratch),
        compiler_params=pltpu.CompilerParams(vmem_limit_bytes=limit * 1024 * 1024),
        cost_estimate=pl.CostEstimate(
            flops=int(flops * weight), bytes_accessed=int(moved * weight), transcendentals=trans
        ),
    )


def dot(a, b, dims=(((1,), (0,)), ((), ()))):
    return lax.dot_general(a, b, dims, preferred_element_type=f32)


def norm_rows(value):
    center = value - jnp.mean(value, axis=-1, keepdims=True)
    scale = lax.rsqrt(jnp.mean(center * center, axis=-1, keepdims=True) + 1e-12)
    return center * scale, scale


def norm_back(grad_out, normed, scale, gain):
    inner = grad_out * gain
    back = scale * (
        inner
        - jnp.mean(inner, axis=-1, keepdims=True)
        - normed * jnp.mean(inner * normed, axis=-1, keepdims=True)
    )
    return (
        back,
        jnp.sum(grad_out * normed, axis=0, keepdims=True),
        jnp.sum(grad_out, axis=0, keepdims=True),
    )


def places(ring):
    me = lax.axis_index("dp")
    return lax.div(me, 4), lax.rem(lax.div(me, 2), 2), lax.rem(me, 2)


def pairs_of(ndp, kind):
    if kind in (1, 2, 3):
        return [(i, (i + 4 * kind) % ndp) for i in range(ndp)]
    if kind == "x":
        return [(i, i ^ 2) for i in range(ndp)]
    return [(i, i ^ 1) for i in range(ndp)]


def move(a, kind):
    return lax.ppermute(a, "dp", pairs_of(lax.axis_size("dp"), kind))


def exchange(a):
    return lax.ppermute(a, "tensor", [(0, 1), (1, 0)])


def after(value, *others):
    return lax.optimization_barrier((value,) + others)[0]


def tie(*arrays):
    return lax.optimization_barrier(arrays)


def unique(entries):
    entries = [e if isinstance(e, tuple) else (e, Ellipsis) for e in entries]
    arrays, at = [], []
    for array, _ in entries:
        found = [i for i, a in enumerate(arrays) if a is array]
        if not found:
            found = [len(arrays)]
            arrays.append(array)
        at.append(found[0])
    return arrays, at, [where for _, where in entries]


def stack(entries, rows, cols, lead=None):
    arrays, at, where = unique(entries)
    lead = (len(entries),) if lead is None else lead

    def body(*refs):
        for i in range(len(entries)):
            place = (i,) if len(lead) == 1 else (i // lead[1], i % lead[1])
            refs[-1][place] = refs[at[i]][where[i]]

    size = len(entries) * rows * cols
    return call(body, [(lead + (rows, cols), b16)], [VM] * len(arrays), moved=4 * size)(*arrays)[0]


def settle(mine, met):
    _, ring, rows, cols = mine.shape

    def body(mine_ref, met_ref, out_ref):
        z, x, c = places(ring)
        for other in range(2):
            source = (mine_ref, met_ref)[other]
            for xo in range(2):
                for k in range(ring):
                    zz = lax.rem(z - k + ring, ring)
                    xx = lax.rem(x + xo, 2)
                    cc = lax.rem(c + other, 2)
                    row = pl.multiple_of(((zz * 2 + xx) * 2 + cc) * rows, 16)
                    out_ref[pl.ds(row, rows), :] = source[xo, k]

    return call(
        body, [((4 * ring * rows, cols), b16)], [VM] * 2, moved=16 * ring * rows * cols
    )(mine, met)[0]


def prep(weights_tiled, rep, split):
    tiled_rows = weights_tiled.shape[1]
    rows = tiled_rows // TILES
    per = split.shape[1]

    def body(w_ref, rep_ref, split_ref, a0, f0, l1, every):
        a1, f1 = l1.at[:, :ATT], l1.at[:, ATT:]
        for layer, (a_ref, f_ref) in enumerate(((a0, f0), (a1, f1))):
            for c in range(TILES):
                piece = w_ref[layer, pl.ds(c, rows, stride=TILES), :].astype(b16)
                if c < ATT // LANES:
                    a_ref[:, c * LANES : (c + 1) * LANES] = piece
                else:
                    at = c * LANES - ATT
                    f_ref[:, at : at + LANES] = piece
        row = lax.broadcasted_iota(jnp.int32, (rows, rows), 0)
        col = lax.broadcasted_iota(jnp.int32, (rows, rows), 1)
        eye = (row == col).astype(b16)
        row3 = lax.broadcasted_iota(jnp.int32, (rows, per), 0)
        col3 = lax.broadcasted_iota(jnp.int32, (rows, per), 1)
        gap = col3 - 3 * row3
        block = jnp.zeros((rows, LANES), f32)
        lane = lax.broadcasted_iota(jnp.int32, (rows, LANES), 1)
        rep_cols = dot(eye, rep_ref[...].astype(b16), contract_last)
        rep_wide = jnp.concatenate(
            [rep_cols, jnp.zeros((rows, LANES - 6 * LAYERS), f32)], axis=1
        )
        block = rep_wide
        low = split_ref[...].astype(b16).astype(f32)
        for layer in range(LAYERS):
            for j in range(3):
                pick = jnp.where(gap == j, jnp.broadcast_to(low[layer : layer + 1], (rows, per)), 0.0)
                value = jnp.sum(pick, axis=1, keepdims=True)
                block = jnp.where(lane == 6 * LAYERS + 3 * layer + j, value, block)
        a0[:, ATT:] = block.astype(b16)
        every[:, : ATT + LANES] = a0[...]
        every[:, ATT + LANES : COLS + LANES] = f0[...]
        every[:, COLS + LANES :] = l1[...]

    return call(
        body,
        [
            ((rows, ATT + LANES), b16),
            ((rows, 2 * FFT), b16),
            ((rows, COLS), b16),
            ((rows, 2 * COLS + LANES), b16),
        ],
        [VM] * 3,
        moved=weights_tiled.size * 6,
    )(weights_tiled, rep, split)


def spread_mask(first_row, rows, first, cols):
    row = first_row + lax.broadcasted_iota(jnp.int32, (rows, cols), 0)
    col = first + lax.broadcasted_iota(jnp.int32, (rows, cols), 1)
    gap = col - 3 * row
    return jnp.where((gap >= 0) & (gap < 3), 1.0, 0.0).astype(b16)


def unpack(gathered):
    def body(w_ref, rep_ref, split_ref):
        flat = w_ref[:, ATT:]
        turned = flat.astype(f32).T
        rep_ref[...] = turned[:16]
        low = turned[:24].astype(b16)
        step = VCOL // 3
        for i in range(3):
            rows = D // 3
            mask = spread_mask(i * rows, rows, i * step, step)
            spread = dot(low[:, i * rows : (i + 1) * rows], mask)
            phase = lax.rem(lax.broadcasted_iota(jnp.int32, (1, step), 1), 3)
            for layer in range(LAYERS):
                at = 6 * LAYERS + 3 * layer
                value = jnp.where(
                    phase == 0,
                    spread[at : at + 1],
                    jnp.where(phase == 1, spread[at + 1 : at + 2], spread[at + 2 : at + 3]),
                )
                split_ref[layer : layer + 1, i * step : (i + 1) * step] = value

    return call(
        body,
        [((16, D), f32), ((8, VCOL), f32)],
        [VM],
        moved=D * LANES * 2,
        flops=24 * D * VCOL,
    )(gathered)


def gelu_parts(inner):
    cdf = 0.5 * (1.0 + lax.erf(inner * (0.5**0.5)))
    dens = jnp.exp(-0.5 * inner * inner) * 0.3989422804014327
    return inner * cdf, cdf + inner * dens


def attend(h_low, layer, w_ref, split_ref, seg_ref, part_ref, qkv_ref, probs_ref, ctx_ref):
    mixed = dot(h_low, w_ref[:, :QKV])
    qkv_ref[:, :HD] = (mixed[:, :HD] + split_ref[layer : layer + 1, :HD]).astype(b16)
    qkv_ref[:, HD : 2 * HD] = mixed[:, HD : 2 * HD].astype(b16)
    qkv_ref[:, 2 * HD :] = (
        mixed[:, 2 * HD :] + split_ref[layer : layer + 1, HD : 2 * HD]
    ).astype(b16)
    seg = jnp.broadcast_to(seg_ref[...].astype(f32), (SEQ, SEQ))
    same = seg == seg.T
    low_half = lax.broadcasted_iota(jnp.int32, (1, LANES), 1) < HEAD_DIM
    for pair in range(HD // LANES):
        at = pair * LANES
        query = qkv_ref[:, at : at + LANES].astype(f32) * HEAD_DIM ** (-0.5)
        keys = qkv_ref[:, HD + at : HD + at + LANES]
        values = qkv_ref[:, 2 * HD + at : 2 * HD + at + LANES].astype(f32)
        total = jnp.zeros((SEQ, LANES), f32)
        for half in range(2):
            mine = low_half if half == 0 else ~low_half
            scores = dot(jnp.where(mine, query, 0.0).astype(b16), keys, contract_last)
            scores = jnp.where(same, scores, -1000000000.0)
            raised = jnp.exp(scores - jnp.max(scores, axis=-1, keepdims=True))
            probs = (raised * (1.0 / jnp.sum(raised, axis=-1, keepdims=True))).astype(b16)
            probs_ref[2 * pair + half] = probs
            total = total + dot(probs, jnp.where(mine, values, 0.0).astype(b16))
        ctx_ref[:, at : at + LANES] = total.astype(b16)
    part_ref[...] = dot(ctx_ref[...], w_ref[:, QKV:ATT], contract_last).astype(b16)


ATT_FLOPS = 2 * SEQ * D * ATT + 4 * SEQ * SEQ * HD * 2
FFN_FLOPS = 2 * SEQ * D * 2 * FFT


ATT_OUTS = [((MICRO, SEQ, QKV), b16), ((MICRO, HD // HEAD_DIM, SEQ, SEQ), b16), ((MICRO, SEQ, HD), b16)]


def attention_first(block_in, segments, split, matrix):
    def body(h_ref, seg_ref, split_ref, w_ref, part_ref, qkv_ref, probs_ref, ctx_ref):
        for m in range(MICRO):
            views = [r.at[m] for r in (part_ref, qkv_ref, probs_ref, ctx_ref)]
            attend(h_ref[m], 0, w_ref, split_ref, seg_ref[m], *views)

    return call(
        body,
        [((MICRO, SEQ, D), b16)] + ATT_OUTS,
        [VM] * 4,
        flops=2 * ATT_FLOPS,
        moved=12 << 20,
        limit=16,
    )(block_in, segments, split, matrix)


def attention_next(layer, normed, part_own, part_other, rep, segments, split, matrix):
    base = 6 * (layer - 1)

    def body(n_ref, own_ref, other_ref, rep_ref, seg_ref, split_ref, w_ref, *refs):
        parts, (qkv_ref, probs_ref, ctx_ref, n2_ref, s2_ref, low_ref) = refs[:MICRO], refs[MICRO:]
        for m in range(MICRO):
            first = n_ref[m] * rep_ref[base + 1 : base + 2] + rep_ref[base + 2 : base + 3]
            added = own_ref[m].astype(f32) + other_ref[m].astype(f32)
            n2, s2 = norm_rows(first + added + rep_ref[base + 3 : base + 4])
            n2_ref[m] = n2
            s2_ref[m] = s2
            low = (n2 * rep_ref[base + 4 : base + 5] + rep_ref[base + 5 : base + 6]).astype(b16)
            low_ref[m] = low
            views = [r.at[m] for r in (qkv_ref, probs_ref, ctx_ref)]
            attend(low, layer, w_ref, split_ref, seg_ref[m], parts[m], *views)

    return call(
        body,
        [((SEQ, D), b16)] * MICRO
        + ATT_OUTS
        + [((MICRO, SEQ, D), f32), ((MICRO, SEQ, 1), f32), ((MICRO, SEQ, D), b16)],
        [VM] * 7,
        flops=2 * ATT_FLOPS,
        moved=16 << 20,
        limit=22,
    )(normed, part_own, part_other, rep, segments, split, matrix)


def feed_step(hidden_in, added, layer, rep_ref, split_ref, w_ref, outs):
    base = 6 * layer
    part_ref, n1_ref, s1_ref, low_ref, act_ref, slope_ref = outs
    n1, s1 = norm_rows(hidden_in + added + rep_ref[base : base + 1])
    n1_ref[...] = n1
    s1_ref[...] = s1
    low_ref[...] = (n1 * rep_ref[base + 1 : base + 2] + rep_ref[base + 2 : base + 3]).astype(b16)
    step = 512
    for at in range(0, FFT, step):
        inner = (
            dot(low_ref[...], w_ref[:, at : at + step])
            + split_ref[layer : layer + 1, 2 * HD + at : 2 * HD + at + step]
        )
        active, slope = gelu_parts(inner)
        act_ref[:, at : at + step] = active.astype(b16)
        slope_ref[:, at : at + step] = slope.astype(b16)
    part_ref[...] = dot(act_ref[...], w_ref[:, FFT:], contract_last).astype(b16)


FEED_OUTS = [
    ((SEQ, D), b16),
    ((SEQ, D), f32),
    ((SEQ, 1), f32),
    ((SEQ, D), b16),
    ((SEQ, FFT), b16),
    ((SEQ, FFT), b16),
]


def feed_first(hidden, part_own, part_other, rep, split, matrix):
    def body(h_ref, own_ref, other_ref, rep_ref, split_ref, w_ref, *outs):
        for m in range(MICRO):
            added = own_ref[m].astype(f32) + other_ref[m].astype(f32)
            views = [r.at[m] for r in outs]
            feed_step(h_ref[m].astype(f32), added, 0, rep_ref, split_ref, w_ref, views)

    return call(
        body,
        [((MICRO,) + shape, kind) for shape, kind in FEED_OUTS],
        [VM] * 6,
        flops=2 * FFN_FLOPS,
        moved=20 << 20,
        limit=22,
    )(hidden, part_own, part_other, rep, split, matrix)


def feed_forward(micro, layer, hidden, part_own, part_other, rep, split, matrix):
    base = 6 * layer

    def body(h_ref, own_ref, other_ref, rep_ref, split_ref, w_ref, *outs):
        hidden_in = h_ref[micro] * rep_ref[base - 2 : base - 1] + rep_ref[base - 1 : base]
        added = own_ref[...].astype(f32) + other_ref[...].astype(f32)
        feed_step(hidden_in, added, layer, rep_ref, split_ref, w_ref, outs)

    return call(
        body,
        FEED_OUTS,
        [VM] * 6,
        flops=FFN_FLOPS,
        moved=10 << 20,
    )(hidden, part_own, part_other, rep, split, matrix)


def view(ref, micro):
    return ref.at[micro] if ref.shape[0] == MICRO else ref


def feed_back_tail(grad, n2, s2, layer, rep_ref, slope_ref, w_ref, outs):
    base = 6 * layer
    part_ref, res_ref, dffn_ref, din_ref, vec_ref = outs
    back, gain, shift = norm_back(grad, n2, s2, rep_ref[base + 4 : base + 5])
    res_ref[...] = back
    dffn_ref[...] = back.astype(b16)
    vec_ref[...] = jnp.zeros_like(vec_ref)
    vec_ref[0:1] = jnp.sum(back, axis=0, keepdims=True)
    vec_ref[1:2] = gain
    vec_ref[2:3] = shift
    step = 384
    for at in range(0, FFT, step):
        grad_act = dot(dffn_ref[...], w_ref[:, FFT + at : FFT + at + step])
        grad_in = (slope_ref[:, at : at + step].astype(f32) * grad_act).astype(b16)
        din_ref[:, at : at + step] = grad_in
        row, lane = 3 + at // D, at % D
        vec_ref[row : row + 1, lane : lane + step] = jnp.sum(
            grad_in.astype(f32), axis=0, keepdims=True
        )
    part_ref[...] = dot(din_ref[...], w_ref[:, :FFT], contract_last).astype(b16)


BACK_OUTS = [
    ((SEQ, D), b16),
    ((SEQ, D), f32),
    ((SEQ, D), b16),
    ((SEQ, FFT), b16),
    ((8, D), f32),
]


def feed_back_top(micro, layer, out_grad, n1, part_own, part_other, rep, slope, matrix):
    base = 6 * layer

    def body(g_ref, n_ref, own_ref, other_ref, rep_ref, slope_ref, w_ref, *refs):
        out_ref = refs[5]
        first = n_ref[...] * rep_ref[base + 1 : base + 2] + rep_ref[base + 2 : base + 3]
        added = own_ref[...].astype(f32) + other_ref[...].astype(f32)
        n2, s2 = norm_rows(first + added + rep_ref[base + 3 : base + 4])
        out_ref[...] = (n2 * rep_ref[base + 4 : base + 5] + rep_ref[base + 5 : base + 6]).astype(b16)
        feed_back_tail(
            g_ref[micro].astype(f32), n2, s2, layer, rep_ref, slope_ref, w_ref, refs[:5]
        )

    return call(
        body,
        BACK_OUTS + [((SEQ, D), b16)],
        [VM] * 6 + [VM],
        flops=FFN_FLOPS,
        moved=11 << 20,
    )(out_grad, n1, part_own, part_other, rep, slope, matrix)


def feed_back(micro, layer, mid, part_own, part_other, n2, s2, rep, slope, matrix):
    def body(mid_ref, own_ref, other_ref, n2_ref, s2_ref, rep_ref, slope_ref, w_ref, *refs):
        added = own_ref[...].astype(f32) + other_ref[...].astype(f32)
        feed_back_tail(
            mid_ref[...] + added,
            view(n2_ref, micro)[...],
            view(s2_ref, micro)[...],
            layer,
            rep_ref,
            view(slope_ref, micro),
            w_ref,
            refs[:5],
        )

    return call(
        body,
        BACK_OUTS,
        [VM] * 7 + [VM],
        flops=FFN_FLOPS,
        moved=11 << 20,
    )(mid, part_own, part_other, n2, s2, rep, slope, matrix)


def attention_back(micro, layer, res, part_own, part_other, n1, s1, rep, qkv, probs, ctx, matrix):
    base = 6 * layer

    def body(
        res_ref, own_ref, other_ref, n1_ref, s1_ref, rep_ref, qkv_ref, probs_ref, ctx_ref, w_ref, *refs
    ):
        part_ref, mid_ref, datt_ref, dqkv_ref, vec_ref = refs
        n1_ref, s1_ref, qkv_ref, probs_ref, ctx_ref = (
            view(r, micro) for r in (n1_ref, s1_ref, qkv_ref, probs_ref, ctx_ref)
        )
        grad = res_ref[...] + (own_ref[...].astype(f32) + other_ref[...].astype(f32))
        back, gain, shift = norm_back(grad, n1_ref[...], s1_ref[...], rep_ref[base + 1 : base + 2])
        mid_ref[...] = back
        datt_ref[...] = back.astype(b16)
        vec_ref[...] = jnp.zeros_like(vec_ref)
        vec_ref[0:1] = jnp.sum(back, axis=0, keepdims=True)
        vec_ref[1:2] = gain
        vec_ref[2:3] = shift
        dctx = dot(datt_ref[...], w_ref[:, QKV:ATT]).astype(b16).astype(f32)
        low_half = lax.broadcasted_iota(jnp.int32, (1, LANES), 1) < HEAD_DIM
        factor = HEAD_DIM ** (-0.5)
        for pair in range(HD // LANES):
            at = pair * LANES
            query = qkv_ref[:, at : at + LANES].astype(f32) * factor
            keys = qkv_ref[:, HD + at : HD + at + LANES].astype(f32) * factor
            values = qkv_ref[:, 2 * HD + at : 2 * HD + at + LANES]
            dc = dctx[:, at : at + LANES]
            weighed = dc * ctx_ref[:, at : at + LANES].astype(f32)
            dq = jnp.zeros((SEQ, LANES), f32)
            dk = jnp.zeros((SEQ, LANES), f32)
            dv = jnp.zeros((SEQ, LANES), f32)
            for half in range(2):
                mine = low_half if half == 0 else ~low_half
                dcm = jnp.where(mine, dc, 0.0).astype(b16)
                delta = jnp.sum(jnp.where(mine, weighed, 0.0), axis=-1, keepdims=True)
                probs = probs_ref[2 * pair + half]
                dprobs = dot(dcm, values, contract_last)
                dscores = (probs.astype(f32) * (dprobs - delta)).astype(b16)
                dq = dq + dot(dscores, jnp.where(mine, keys, 0.0).astype(b16))
                dk = dk + dot(dscores, jnp.where(mine, query, 0.0).astype(b16), contract_first)
                dv = dv + dot(probs, dcm, contract_first)
            dqkv_ref[:, at : at + LANES] = dq.astype(b16)
            dqkv_ref[:, HD + at : HD + at + LANES] = dk.astype(b16)
            dqkv_ref[:, 2 * HD + at : 2 * HD + at + LANES] = dv.astype(b16)
        vec_ref[3:4, :HD] = jnp.sum(dqkv_ref[:, :HD].astype(f32), axis=0, keepdims=True)
        vec_ref[3:4, HD:] = jnp.sum(dqkv_ref[:, 2 * HD :].astype(f32), axis=0, keepdims=True)
        part_ref[...] = dot(dqkv_ref[...], w_ref[:, :QKV], contract_last).astype(b16)

    return call(
        body,
        [
            ((SEQ, D), b16),
            ((SEQ, D), f32),
            ((SEQ, D), b16),
            ((SEQ, QKV), b16),
            ((8, D), f32),
        ],
        [VM] * 9 + [VM],
        flops=2 * ATT_FLOPS,
        moved=9 << 20,
    )(res, part_own, part_other, n1, s1, rep, qkv, probs, ctx, matrix)


def finish_input(mids, owns, others):
    def body(*refs):
        for micro in range(MICRO):
            m, a, b = refs[3 * micro : 3 * micro + 3]
            refs[-1][micro] = m[...] + (a[...].astype(f32) + b[...].astype(f32))

    args = []
    for micro in range(MICRO):
        args += [mids[micro], owns[micro], others[micro]]
    return call(body, [((MICRO, SEQ, D), f32)], [VM] * len(args), moved=7 << 20)(*args)[0]


def store_slots(product_ref, outs, at, width):
    if len(outs) == 1:
        outs[0][:, at : at + width] = product_ref[:, :width].astype(b16)
        return
    ring, rows = outs[0].shape[1], outs[0].shape[2]
    z, x, c = places(ring)
    for other in range(2):
        for xo in range(2):
            for k in range(ring):
                zz = lax.rem(z + k, ring)
                xx = lax.rem(x + xo, 2)
                cc = lax.rem(c + other, 2)
                row = pl.multiple_of(((zz * 2 + xx) * 2 + cc) * rows, 16)
                outs[other][xo, k, :, at : at + width] = product_ref[
                    pl.ds(row, rows), :width
                ].astype(b16)


def grad_outs(ndp, pieced, cols):
    rows = D // ndp
    if pieced:
        return [((2, ndp // 4, rows, cols), b16)] * 2
    return [((D, cols), b16)]


def matrix_gradient(sets, pieced, ndp, vectors=None):
    widths = [s[2] for s in sets]
    total = sum(widths) + (LANES if vectors is not None else 0)
    outs = grad_outs(ndp, pieced, total)
    args, specs = [], []
    for left, right, _ in sets:
        for micro in range(MICRO):
            specs.append(VM)
            args.append(left[micro])
        for micro in range(MICRO):
            args.append(right[micro])
            specs.append(VM)
    plain = len(args)
    if vectors is not None:
        args += vectors
        specs += [VM] * len(vectors)
    n_in = len(args)
    step = 384

    def body(*refs):
        out_refs = refs[n_in : n_in + len(outs)]
        prod_ref = refs[n_in + len(outs)]
        at = 0
        for index, width in enumerate(widths):
            l0, l1, r0, r1 = refs[4 * index : 4 * index + 4]
            left = [r[m] if len(r.shape) == 3 else r[...] for m, r in enumerate((l0, l1))]
            r0, r1 = (r.at[m] if len(r.shape) == 3 else r for m, r in enumerate((r0, r1)))
            for col in range(0, width, step):
                prod_ref[...] = dot(left[0], r0[:, col : col + step], contract_first) + dot(
                    left[1], r1[:, col : col + step], contract_first
                )
                store_slots(prod_ref, out_refs, at, step)
                at += step
        if vectors is not None:
            pack_vectors(refs[plain:n_in], prod_ref)
            store_slots(prod_ref, out_refs, at, LANES)

    moved = sum(a.size * 2 for a in args[:plain]) + D * total * 2
    return call(
        body,
        outs,
        specs,
        [pltpu.VMEM((D, step), f32)],
        flops=2 * MICRO * SEQ * D * total,
        moved=moved,
    )(*args)


def pack_vectors(vec_refs, prod_ref):
    sums = []
    for layer in range(LAYERS):
        a0, a1, b0, b1 = vec_refs[4 * layer : 4 * layer + 4]
        sums.append((a0[...] + a1[...], b0[...] + b1[...]))
    rows = []
    for att, ffn in sums:
        rows += [att[0:1], att[1:2], att[2:3], ffn[0:1], ffn[1:2], ffn[2:3]]
    rows.append(jnp.zeros((4, D), f32))
    turned = jnp.concatenate(rows, axis=0)
    turned = jnp.concatenate([turned, jnp.zeros((LANES - 16, D), f32)], axis=0).T
    step = VCOL // 3
    phase = lax.rem(lax.broadcasted_iota(jnp.int32, (1, step), 1), 3)
    lane = lax.broadcasted_iota(jnp.int32, (1, LANES), 1)
    for i in range(3):
        picked = []
        for att, ffn in sums:
            line = (att[3:4], ffn[3:4], ffn[4:5])[i]
            for j in range(3):
                picked.append(jnp.where(phase == j, line, 0.0))
        picked = jnp.concatenate(
            [jnp.zeros((12, step), f32)] + picked + [jnp.zeros((LANES - 18, step), f32)], axis=0
        ).astype(b16)
        n_rows = D // 3
        mask = spread_mask(i * n_rows, n_rows, i * step, step)
        part = dot(mask, picked, contract_last)
        keep = turned[i * n_rows : (i + 1) * n_rows]
        prod_ref[i * n_rows : (i + 1) * n_rows, :LANES] = jnp.where(lane < 12, keep, part)


def meet(own, met, places):
    lo, hi = places[0], places[-1] + 1
    return (own[1, lo:hi].astype(f32) + met[1, lo:hi].astype(f32)).astype(b16)


def pass_on(own, met, got, places):
    lo, hi = places[0], places[-1] + 1
    total = own[0, lo:hi].astype(f32) + met[0, lo:hi].astype(f32) + got.astype(f32)
    return [total[i].astype(b16) for i in range(hi - lo)]


def pass_both(own, met, k, received=None):
    total = own[:, k].astype(f32) + met[:, k].astype(f32)
    if received is not None:
        total = total + received.astype(f32)
    return total.astype(b16)


def close(own, met, parts, vectors=False):
    _, _, rows, cols = own.shape
    mats = cols - LANES if vectors else cols
    parts = [p if isinstance(p, tuple) else (p, None) for p in parts]
    n = len(parts)

    def body(own_ref, met_ref, *refs):
        out_ref, sq_ref = refs[n:]
        total = jnp.zeros((rows, LANES), f32)
        for at in range(0, cols, LANES):
            s = slice(at, at + LANES)
            value = own_ref[0, 0, :, s].astype(f32) + met_ref[0, 0, :, s].astype(f32)
            for (_, index), ref in zip(parts, refs[:n]):
                value = value + (ref[:, s] if index is None else ref[index, :, s]).astype(f32)
            out_ref[:, s] = value
            square = value * value
            if at >= mats:
                lane = lax.broadcasted_iota(jnp.int32, (rows, LANES), 1)
                twice = (lane < 6 * LAYERS) & (lax.axis_index("tensor") != 0)
                square = jnp.where(twice, 0.0, square)
            total = total + square
        part = total[:8]
        for i in range(8, rows, 8):
            part = part + total[i : i + 8]
        sq_ref[...] = part

    return call(
        body,
        [((rows, cols), f32), ((8, LANES), f32)],
        [VM] * (2 + n),
        moved=rows * cols * 14,
    )(own, met, *[p[0] for p in parts])


def adamw(value, first, second, grad, rate, decay):
    first = 0.5 * first + 0.5 * grad
    second = 0.5 * second + 0.5 * grad * grad
    correct = 1.0 - 0.5**STEP
    direction = first / correct / (jnp.sqrt(second / correct) + 1e-08)
    return (value - rate * (direction + decay * value), first, second)


def clip_factor(squares):
    norm = jnp.sqrt(jnp.sum(squares, keepdims=True))
    return norm, jnp.minimum(1.0, clip_limit / (norm + 1e-06))


def ready(tiled, first, second):
    def body(w_ref, m_ref, v_ref, w_out, m_out, v_out):
        w_out[...] = w_ref[...] * (1.0 - weight_rate * weight_decay)
        m_out[...] = 0.5 * m_ref[...]
        v_out[...] = 0.5 * v_ref[...]

    return call(body, [(tiled.shape, f32)] * 3, [VM] * 3, moved=24 * tiled.size)(tiled, first, second)


def stepped(decayed, half_first, half_second, grad, rate):
    first = half_first + 0.5 * grad
    second = half_second + 0.5 * grad * grad
    correct = 1.0 - 0.5**STEP
    direction = first / correct / (jnp.sqrt(second / correct) + 1e-08)
    return decayed - rate * direction, first, second


def update_vectors(block, squares, reps, splits):
    rows = block.shape[0]
    per = splits[0].shape[2]

    def body(b_ref, q_ref, rw, rm, rv, sw, sm, sv, norm_ref, rwo, rmo, rvo, rlo, go, swo, smo, svo, slo):
        norm, scale = clip_factor(q_ref[...])
        norm_ref[...] = norm
        turned = jnp.concatenate([b_ref[...], jnp.zeros((LANES - rows, LANES), f32)], axis=0).T
        for layer in range(LAYERS):
            at = slice(layer, layer + 1)
            for kind in range(6):
                grad = turned[6 * layer + kind : 6 * layer + kind + 1, :rows] * scale
                new = adamw(rw[kind, at], rm[kind, at], rv[kind, at], grad, vector_rate, 0.0)
                rwo[kind, at], rmo[kind, at], rvo[kind, at] = new
                rlo[kind, at] = new[0].astype(b16)
                if kind == 0:
                    go[at] = grad
        row = lax.broadcasted_iota(jnp.int32, (rows, per), 0)
        col = lax.broadcasted_iota(jnp.int32, (rows, per), 1)
        gap = col - 3 * row
        mask = jnp.where((gap >= 0) & (gap < 3), 1.0, 0.0)
        wide = lax.dot_general(
            turned[6 * LAYERS : 6 * LAYERS + 8, :rows],
            mask,
            (((1,), (0,)), ((), ())),
            preferred_element_type=f32,
            precision=lax.Precision.HIGHEST,
        )
        phase = lax.rem(lax.broadcasted_iota(jnp.int32, (1, per), 1), 3)
        for layer in range(LAYERS):
            one, two, three = (wide[3 * layer + j : 3 * layer + j + 1] for j in range(3))
            grad = jnp.where(phase == 0, one, jnp.where(phase == 1, two, three)) * scale
            new = adamw(sw[layer], sm[layer], sv[layer], grad, vector_rate, 0.0)
            swo[layer], smo[layer], svo[layer] = new
            slo[layer] = new[0].astype(b16)

    rep, split = reps[0].shape, splits[0].shape
    return call(
        body,
        [((1, 1), f32)]
        + [(rep, f32)] * 3
        + [(rep, b16), ((LAYERS, rows), f32)]
        + [(split, f32)] * 3
        + [(split, b16)],
        [VM] * 8,
        moved=1 << 18,
    )(block, squares, *reps, *splits)


def update_matrices(decayed, first, second, grads, squares):
    rows = grads[0].shape[0]
    tiled = decayed
    step = 8 if rows % 8 == 0 else rows
    n_steps = rows // step
    block = (1, step * TILES, LANES)

    def body(f_ref, w_ref, m_ref, v_ref, a0, f0, a1, f1, nw, nm, nv, nl):
        scale = clip_factor(f_ref[...])[1]
        layer = pl.program_id(0)
        for c in range(TILES):
            if c < ATT // LANES:
                lo = c * LANES
                grad = jnp.where(layer == 0, a0[:, lo : lo + LANES], a1[:, lo : lo + LANES])
            else:
                lo = c * LANES - ATT
                grad = jnp.where(layer == 0, f0[:, lo : lo + LANES], f1[:, lo : lo + LANES])
            where = (0, pl.ds(c, step, stride=TILES), slice(None))
            new = stepped(w_ref[where], m_ref[where], v_ref[where], grad * scale, weight_rate)
            nw[where], nm[where], nv[where] = new
        nl[...] = nw[...].astype(b16)

    big = pl.BlockSpec(block, lambda l, i: (l, i, 0))
    shape = tiled.shape
    return pl.pallas_call(
        body,
        grid=(LAYERS, n_steps),
        out_shape=[jax.ShapeDtypeStruct(shape, f32)] * 3 + [jax.ShapeDtypeStruct(shape, b16)],
        in_specs=[pl.BlockSpec((8, LANES), lambda l, i: (0, 0)), big, big, big]
        + [pl.BlockSpec((step, g.shape[1]), lambda l, i: (i, 0)) for g in grads],
        out_specs=[big] * 4,
        compiler_params=pltpu.CompilerParams(vmem_limit_bytes=VMEM_LIMIT),
        cost_estimate=pl.CostEstimate(
            flops=20 * tiled.size, bytes_accessed=30 * tiled.size, transcendentals=tiled.size
        ),
    )(squares, tiled, first, second, *grads)


def sum_everywhere(value):
    ndp = lax.axis_size("dp")
    if ndp & (ndp - 1) or ndp < 4:
        return lax.psum(value, ("dp", "tensor"))

    def level(a, first, second):
        one, two, both = ppermute_bits(a, first), ppermute_bits(a, second), ppermute_bits(a, first | second)
        return (a + one) + (two + both)

    value = value + ppermute_bits(value, 2)
    value = level(value, 4, 1)
    bit = 8
    while bit < 2 * ndp:
        if 2 * bit < 2 * ndp:
            value = level(value, bit, 2 * bit)
        else:
            value = value + ppermute_bits(value, bit)
        bit *= 4
    return value


def ppermute_bits(value, bits):
    n = 2 * lax.axis_size("dp")
    return lax.ppermute(value, ("dp", "tensor"), [(i, i ^ bits) for i in range(n)])


def per_device(
    block_in,
    out_grad,
    segments,
    weights,
    weights_first,
    weights_second,
    split_vectors,
    split_first,
    split_second,
    rep_vectors,
    rep_first,
    rep_second,
):
    ndp = lax.axis_size("dp")
    rows = D // ndp
    per = split_vectors.shape[2]
    pieced = ndp == 16 and rows % 16 == 0
    shard_shape = weights.shape
    tiled_shape = (LAYERS, -1, LANES)
    masters = [a.reshape(tiled_shape) for a in (weights, weights_first, weights_second)]
    weights_tiled = masters[0]
    rep_flat = rep_vectors.reshape(LAYERS * 6, -1)
    split_flat = split_vectors.reshape(LAYERS, per)
    both = range(MICRO)
    seg = segments.reshape(MICRO, 1, SEQ)
    if pieced:
        a0, f0, l1, every = prep(weights_tiled, rep_flat, split_flat)
        across = partial(move, kind="x")
        third = slice(COLS + LANES, COLS + LANES + ATT)
        fourth = slice(COLS + LANES + ATT, None)

        def finish(slots, cols):
            mine = stack(slots, rows, cols, (2, 4))
            return settle(mine, move(mine, "core"))

        def cut(array, cols):
            return (array, (slice(None), cols))

        x0 = across(every)
        a0_r1, a0_r2, a0_r3, f0 = tie(move(a0, 1), move(a0, 2), move(a0, 3), f0)
        a0_x = across(stack([a0_r1, a0_r2, a0_r3], rows, ATT + LANES))
        f0_r1, f0_r3 = move(f0, 1), move(f0, 3)
        mine0 = stack(
            [a0, a0_r1, a0_r2, a0_r3, cut(x0, slice(0, ATT + LANES)), (a0_x, 0), (a0_x, 1), (a0_x, 2)],
            rows,
            ATT + LANES,
            (2, 4),
        )
        mine0, f0_r1, f0_r3, l1 = tie(mine0, f0_r1, f0_r3, l1)
        watt0 = settle(mine0, move(mine0, "core"))
        f0_x13 = across(stack([f0_r1, f0_r3], rows, 2 * FFT))
        f0_r2 = move(f0_r1, 1)
        l1_r1, l1_r3 = move(l1, 1), move(l1, 3)
        f0_x2 = across(f0_r2)
    else:
        low = weights.astype(b16).reshape(LAYERS, rows, COLS)
        block = jnp.concatenate(
            [
                rep_flat.T,
                split_flat.reshape(LAYERS, rows, 3).transpose(1, 0, 2).reshape(rows, 6),
                jnp.zeros((rows, LANES - 18), f32),
            ],
            axis=1,
        ).astype(b16)
        gather = partial(lax.all_gather, axis_name="dp", axis=0, tiled=True)
        watt0 = gather(jnp.concatenate([low[0, :, :ATT], block], axis=1))
        watt1 = gather(low[1, :, :ATT])
        wffn0, wffn1 = (gather(low[layer, :, ATT:]) for layer in range(LAYERS))
    rep, split = unpack(watt0)

    done, qkv0, probs0, ctx0 = attention_first(block_in, seg, split, watt0)
    met = exchange(done)
    if pieced:
        f0_x13, f0_x2, l1_r1, l1_r3, met = tie(f0_x13, f0_x2, l1_r1, l1_r3, met)
        a1_x13 = across(stack([cut(l1_r1, slice(0, ATT)), cut(l1_r3, slice(0, ATT))], rows, ATT))
        l1_r2 = move(l1_r1, 1)
        wffn0 = finish(
            [f0, f0_r1, f0_r2, f0_r3]
            + [cut(x0, slice(ATT + LANES, COLS + LANES)), (f0_x13, 0), f0_x2, (f0_x13, 1)],
            2 * FFT,
        )
    done, n1_0, s1_0, low1_0, act0, slope0 = feed_first(block_in, done, met, rep, split, wffn0)
    if pieced:
        a1_x13, l1_r2, done = tie(a1_x13, l1_r2, done)
        head, tail = slice(0, ATT), slice(ATT, None)
        a1_x2 = across(stack([cut(l1_r2, head)], rows, ATT))
        f1_x13 = across(stack([cut(l1_r1, tail), cut(l1_r3, tail)], rows, 2 * FFT))
        watt1 = finish(
            [cut(r, head) for r in (l1, l1_r1, l1_r2, l1_r3)]
            + [cut(x0, third), (a1_x13, 0), (a1_x2, 0), (a1_x13, 1)],
            ATT,
        )
    met = exchange(done)
    if pieced:
        f1_x13, met = tie(f1_x13, met)
    out = attention_next(1, n1_0, done, met, rep, seg, split, watt1)
    done, (qkv1, probs1, ctx1, n2_0, s2_0, low_h1) = list(out[:MICRO]), out[MICRO:]
    if pieced:
        f1_x2 = across(stack([cut(l1_r2, tail)], rows, 2 * FFT))
        wffn1 = finish(
            [cut(r, tail) for r in (l1, l1_r1, l1_r2, l1_r3)]
            + [cut(x0, fourth), (f1_x13, 0), (f1_x2, 0), (f1_x13, 1)],
            2 * FFT,
        )
    met = [exchange(a) for a in done]
    out = [feed_forward(m, 1, n2_0, done[m], met[m], rep, split, wffn1) for m in both]
    n1_1, s1_1, low1_1, act1, slope1 = ([o[i] for o in out] for i in range(1, 6))
    met = [exchange(o[0]) for o in out]

    out = [
        feed_back_top(m, 1, out_grad, n1_1[m], out[m][0], met[m], rep, slope1[m], wffn1)
        for m in both
    ]
    res, dffn, din, vec_f1 = ([o[i] for o in out] for i in range(1, 5))
    block_out = jnp.stack([o[5] for o in out])
    done = [o[0] for o in out]
    met = [exchange(o[0]) for o in out]
    plan = {"w_f1": 0, "f1_3": 1, "w_a1": 2, "f1_2": 3, "a1_s": 3, "w_f0": 4, "f1_1": 4, "a1_t": 5, "f0_s": 5}
    held, ends = {}, []

    def make(name):
        gate = ends[-1:] if 1 else []
        if name == "w_f1":
            g = matrix_gradient([(low1_1, din_1, FFT), (dffn_1, act1, FFT)], pieced, ndp)
        elif name == "w_a1":
            g = matrix_gradient(
                [([low_h1] * 2, dqkv_1, QKV), (datt_1, [ctx1] * 2, HD)], pieced, ndp
            )
        elif name == "w_f0":
            g = matrix_gradient(
                [([low1_0] * 2, din_0, FFT), (dffn_0, [act0] * 2, FFT)], pieced, ndp
            )
        elif not pieced:
            return []
        if name.startswith("w_"):
            held[name[2:]] = g if not pieced else (g[0], move(g[1], "core"))
            return [g[0]]
        own, across_core = held[name[:2]]
        if name[:3] == "f1_":
            k = int(name[3])
            if k == 3:
                total = pass_both(own, after(across_core, *gate), k)
            else:
                total = pass_both(own, across_core, k, after(held["f1_rec"], *gate))
            held["f1_rec"] = move(total, 1)
            return [total]
        if name == "a1_t":
            parts = pass_on(own, across_core, after(held["a1_got"], *gate)[1:], (1, 2, 3))
            held["a1_r"] = [move(t, k + 1) for k, t in enumerate(parts)]
            return [parts[2]]
        places = (0, 1, 2, 3) if name == "a1_s" else (2, 3)
        total = meet(own, after(across_core, *gate), places)
        held[name[:2] + "_got"] = move(total, "x")
        return [total]

    def before(stage, value):
        needed = [a for name in plan if plan[name] == stage for a in make(name)]
        return after(value, *needed) if needed else value

    din_1, dffn_1 = din, dffn
    out = []
    for m in both:
        value = before(m, res[m])
        out.append(
            attention_back(
                m, 1, value, done[m], met[m], n1_1[m], s1_1[m], rep, qkv1, probs1, ctx1, watt1
            )
        )
        ends.append(out[m][0])
    mid, datt_1, dqkv_1, vec_a1 = ([o[i] for o in out] for i in range(1, 5))
    done = [o[0] for o in out]
    met = [exchange(o[0]) for o in out]
    out = []
    for m in both:
        value = before(2 + m, mid[m])
        out.append(feed_back(m, 0, value, done[m], met[m], n2_0, s2_0, rep, slope0, wffn0))
        ends.append(out[m][0])
    res, dffn_0, din_0, vec_f0 = ([o[i] for o in out] for i in range(1, 5))
    done = [o[0] for o in out]
    met = [exchange(o[0]) for o in out]
    out = []
    for m in both:
        value = before(4 + m, res[m])
        out.append(
            attention_back(
                m, 0, value, done[m], met[m], n1_0, s1_0, rep, qkv0, probs0, ctx0, watt0
            )
        )
        ends.append(out[m][0])
    mid, datt, dqkv, vec_a0 = ([o[i] for o in out] for i in range(1, 5))
    done = [o[0] for o in out]
    met = [exchange(o[0]) for o in out]
    dqkv[0] = before(6, dqkv[0])
    g_a0 = matrix_gradient(
        [([block_in] * MICRO, dqkv, QKV), (datt, [ctx0] * 2, HD)],
        pieced,
        ndp,
        vectors=vec_a0 + vec_f0 + vec_a1 + vec_f1,
    )
    ends.append(g_a0[0])
    before(7, g_a0[0])
    if pieced:
        (f1_own, f1_met), (a1_own, a1_met), (f0_own, f0_met) = (held[c] for c in ("f1", "a1", "f0"))
        f1_rec, a1_got, a1_r, f0_got_hi = (held[c] for c in ("f1_rec", "a1_got", "a1_r", "f0_got"))
    else:
        g_f1, g_a1, g_f0 = (held[c] for c in ("f1", "a1", "f0"))
    if pieced:
        masters = ready(*(after(a, g_a0[0]) for a in masters))
        input_grad = finish_input(mid, done, met)
        a0_own, a0_met = g_a0[0], move(g_a0[1], "core")
        a0_got = across(meet(a0_own, a0_met, (0, 1, 2, 3)))
        f1_last = pass_both(f1_own, f1_met, 0, f1_rec)
        f1_got = across(f1_last[1])
        f0_t2, f0_t3 = pass_on(f0_own, f0_met, f0_got_hi, (2, 3))
        f0_r3, f0_r2 = move(f0_t3, 3), move(f0_t2, 2)
        a0_got, f0_r3, f0_r2, *a1_r = tie(a0_got, f0_r3, f0_r2, *a1_r)
        f0_got_lo = across(meet(f0_own, f0_met, (0, 1)))
        a0_t = pass_on(a0_own, a0_met, a0_got[1:], (1, 2, 3))
        a0_r = [move(t, k + 1) for k, t in enumerate(a0_t)]
        grad_a1, sq_a1 = close(a1_own, a1_met, [(a1_got, 0)] + a1_r)
        grad_f1, sq_f1 = close(f1_own, f1_met, [f1_got, (f1_rec, 0)])
        f0_got_lo, grad_f1, grad_a1, block_out, input_grad, *rest = tie(
            f0_got_lo, grad_f1, grad_a1, block_out, input_grad, *a0_r, *masters
        )
        a0_r, masters = rest[:3], rest[3:]
        f0_r1 = move(pass_on(f0_own, f0_met, f0_got_lo[1:], (1,))[0], 1)
        grad_a0, sq_a0 = close(a0_own, a0_met, [(a0_got, 0)] + a0_r, vectors=True)
        grad_f0, sq_f0 = close(f0_own, f0_met, [(f0_got_lo, 0), f0_r1, f0_r2, f0_r3])
        squares = (sq_f1 + sq_a1) + (sq_f0 + sq_a0)
    else:
        input_grad = finish_input(mid, done, met)
        scatter = lambda g: lax.psum_scatter(g[0], "dp", scatter_dimension=0, tiled=True).astype(f32)
        grad_f1, grad_a1, grad_f0, grad_a0 = (scatter(g) for g in (g_f1, g_a1, g_f0, g_a0))
        once = jnp.where(lax.axis_index("tensor") == 0, 1.0, 0.0).astype(f32)
        square = lambda a: jnp.sum(a * a)
        squares = (
            square(grad_a0[:, :ATT])
            + square(grad_f0)
            + square(grad_a1)
            + square(grad_f1)
            + square(grad_a0[:, ATT + 12 :])
            + once * square(grad_a0[:, ATT : ATT + 12])
        )
        squares = jnp.full((8, LANES), squares / (8 * LANES), f32)

    squares = sum_everywhere(squares)
    if pieced:
        new = update_matrices(*masters, [grad_a0, grad_f0, grad_a1, grad_f1], squares)
        turn = lambda a: jnp.transpose(a, (1, 0, 2))
        vectors = update_vectors(
            grad_a0[:, ATT:],
            squares,
            [turn(a) for a in (rep_vectors, rep_first, rep_second)],
            (split_vectors, split_first, split_second),
        )
        grad_norm = vectors[0][0, 0]
        new_rep, rep_first_new, rep_second_new, rep_low = (turn(a) for a in vectors[1:5])
        bias_grad = vectors[5]
        new_split, split_first_new, split_second_new, split_low = vectors[6:]
    else:
        block = grad_a0[:, ATT:]
        grad_rep = block[:, :12].T.reshape(rep_vectors.shape)
        grad_split = (
            block[:, 12:18].reshape(rows, LAYERS, 3).transpose(1, 0, 2).reshape(split_vectors.shape)
        )
        grad_norm, factor = (a[0, 0] for a in clip_factor(squares))
        clipped_rep = grad_rep * factor
        grad = jnp.stack(
            [
                jnp.concatenate([grad_a0[:, :ATT], grad_f0], axis=1),
                jnp.concatenate([grad_a1, grad_f1], axis=1),
            ]
        ).reshape(tiled_shape)
        new = adamw(*masters, grad * factor, weight_rate, weight_decay)
        new = (*new, new[0].astype(b16))
        new_split, split_first_new, split_second_new = adamw(
            split_vectors, split_first, split_second, grad_split * factor, vector_rate, 0.0
        )
        new_rep, rep_first_new, rep_second_new = adamw(
            rep_vectors, rep_first, rep_second, clipped_rep, vector_rate, 0.0
        )
        split_low, rep_low = new_split.astype(b16), new_rep.astype(b16)
        bias_grad = clipped_rep[:, 0, :]
    new_weights, weights_first_new, weights_second_new, weights_low = (
        a.reshape(shard_shape) for a in new
    )
    return (
        block_out,
        input_grad,
        grad_norm,
        new_weights,
        weights_first_new,
        weights_second_new,
        weights_low,
        new_split,
        split_first_new,
        split_second_new,
        split_low,
        new_rep,
        rep_first_new,
        rep_second_new,
        rep_low,
        bias_grad,
    )


def solution(mesh):
    rows, packed, vector = P("dp", None, None), P(None, "tensor", "dp"), P(None, None, "dp")
    return jax.shard_map(
        per_device,
        mesh=mesh,
        in_specs=(rows, rows, P("dp", None)) + (packed,) * 6 + (vector,) * 3,
        out_specs=(rows, rows, P()) + (packed,) * 8 + (vector,) * 4 + (P(None, "dp"),),
        check_vma=False,
    )
```

```python
from functools import partial

import jax
import jax.numpy as jnp
from jax import lax
from jax.experimental import pallas as pl
from jax.experimental.pallas import tpu as pltpu
from jax.sharding import PartitionSpec as P

D = 768
HEAD_DIM = 64
LAYERS = 2
SEQ = 256
MICRO = 2
STEP = 3
HD = 384
FFT = 1536
QKV = 3 * HD
ATT = 4 * HD
COLS = ATT + 2 * FFT
VCOL = 2 * HD + FFT
LANES = 128
TILES = COLS // LANES

clip_limit = 1.0
weight_rate = 0.03
weight_decay = 0.01
vector_rate = 0.3
contract_last = (((1,), (1,)), ((), ()))
contract_first = (((0,), (0,)), ((), ()))
f32 = jnp.float32
b16 = jnp.bfloat16
VM = pl.BlockSpec(memory_space=pltpu.VMEM)


def call(body, outs, in_specs, scratch=(), flops=0, moved=0, out_specs=None, trans=0, limit=13):
    weight = 16 if flops else 1
    if out_specs is None:
        out_specs = [VM] * len(outs)
    return pl.pallas_call(
        body,
        out_shape=[jax.ShapeDtypeStruct(s, d) for s, d in outs],
        in_specs=in_specs,
        out_specs=out_specs,
        scratch_shapes=list(scratch),
        compiler_params=pltpu.CompilerParams(vmem_limit_bytes=limit * 1024 * 1024),
        cost_estimate=pl.CostEstimate(
            flops=int(flops * weight), bytes_accessed=int(moved * weight), transcendentals=trans
        ),
    )


def dot(a, b, dims=(((1,), (0,)), ((), ()))):
    return lax.dot_general(a, b, dims, preferred_element_type=f32)


def norm_rows(value):
    center = value - jnp.mean(value, axis=-1, keepdims=True)
    scale = lax.rsqrt(jnp.mean(center * center, axis=-1, keepdims=True) + 1e-12)
    return center * scale, scale


def norm_back(grad_out, normed, scale, gain):
    inner = grad_out * gain
    back = scale * (
        inner
        - jnp.mean(inner, axis=-1, keepdims=True)
        - normed * jnp.mean(inner * normed, axis=-1, keepdims=True)
    )
    return (
        back,
        jnp.sum(grad_out * normed, axis=0, keepdims=True),
        jnp.sum(grad_out, axis=0, keepdims=True),
    )


def places(ring):
    me = lax.axis_index("dp")
    return lax.div(me, 4), lax.rem(lax.div(me, 2), 2), lax.rem(me, 2)


def pairs_of(ndp, kind):
    if kind in (1, 2, 3):
        return [(i, (i + 4 * kind) % ndp) for i in range(ndp)]
    if kind == "x":
        return [(i, i ^ 2) for i in range(ndp)]
    return [(i, i ^ 1) for i in range(ndp)]


def move(a, kind):
    return lax.ppermute(a, "dp", pairs_of(lax.axis_size("dp"), kind))


def exchange(a):
    return lax.ppermute(a, "tensor", [(0, 1), (1, 0)])


def after(value, *others):
    return lax.optimization_barrier((value,) + others)[0]


def tie(*arrays):
    return lax.optimization_barrier(arrays)


def unique(entries):
    entries = [e if isinstance(e, tuple) else (e, Ellipsis) for e in entries]
    arrays, at = [], []
    for array, _ in entries:
        found = [i for i, a in enumerate(arrays) if a is array]
        if not found:
            found = [len(arrays)]
            arrays.append(array)
        at.append(found[0])
    return arrays, at, [where for _, where in entries]


def stack(entries, rows, cols, lead=None):
    arrays, at, where = unique(entries)
    lead = (len(entries),) if lead is None else lead

    def body(*refs):
        for i in range(len(entries)):
            place = (i,) if len(lead) == 1 else (i // lead[1], i % lead[1])
            refs[-1][place] = refs[at[i]][where[i]]

    size = len(entries) * rows * cols
    return call(body, [(lead + (rows, cols), b16)], [VM] * len(arrays), moved=4 * size)(*arrays)[0]


def settle(mine, met):
    ring, rows, cols = mine[0].shape

    def body(*refs):
        z, x, c = places(ring)
        for other in range(2):
            for xo in range(2):
                for k in range(ring):
                    zz = lax.rem(z - k + ring, ring)
                    xx = lax.rem(x + xo, 2)
                    cc = lax.rem(c + other, 2)
                    row = pl.multiple_of(((zz * 2 + xx) * 2 + cc) * rows, 16)
                    refs[4][pl.ds(row, rows), :] = refs[2 * other + xo][k]

    return call(
        body, [((4 * ring * rows, cols), b16)], [VM] * 4, moved=16 * ring * rows * cols
    )(*mine, *met)[0]


def prep(weights_tiled, rep, split):
    tiled_rows = weights_tiled.shape[1]
    rows = tiled_rows // TILES
    per = split.shape[1]

    def body(w_ref, rep_ref, split_ref, a0, f0, l1, every):
        a1, f1 = l1.at[:, :ATT], l1.at[:, ATT:]
        for layer, (a_ref, f_ref) in enumerate(((a0, f0), (a1, f1))):
            for c in range(TILES):
                piece = w_ref[layer, pl.ds(c, rows, stride=TILES), :].astype(b16)
                if c < ATT // LANES:
                    a_ref[:, c * LANES : (c + 1) * LANES] = piece
                else:
                    at = c * LANES - ATT
                    f_ref[:, at : at + LANES] = piece
        row = lax.broadcasted_iota(jnp.int32, (rows, rows), 0)
        col = lax.broadcasted_iota(jnp.int32, (rows, rows), 1)
        eye = (row == col).astype(b16)
        row3 = lax.broadcasted_iota(jnp.int32, (rows, per), 0)
        col3 = lax.broadcasted_iota(jnp.int32, (rows, per), 1)
        gap = col3 - 3 * row3
        block = jnp.zeros((rows, LANES), f32)
        lane = lax.broadcasted_iota(jnp.int32, (rows, LANES), 1)
        rep_cols = dot(eye, rep_ref[...].astype(b16), contract_last)
        rep_wide = jnp.concatenate(
            [rep_cols, jnp.zeros((rows, LANES - 6 * LAYERS), f32)], axis=1
        )
        block = rep_wide
        low = split_ref[...].astype(b16).astype(f32)
        for layer in range(LAYERS):
            for j in range(3):
                pick = jnp.where(gap == j, jnp.broadcast_to(low[layer : layer + 1], (rows, per)), 0.0)
                value = jnp.sum(pick, axis=1, keepdims=True)
                block = jnp.where(lane == 6 * LAYERS + 3 * layer + j, value, block)
        a0[:, ATT:] = block.astype(b16)
        every[:, : ATT + LANES] = a0[...]
        every[:, ATT + LANES : COLS + LANES] = f0[...]
        every[:, COLS + LANES :] = l1[...]

    return call(
        body,
        [
            ((rows, ATT + LANES), b16),
            ((rows, 2 * FFT), b16),
            ((rows, COLS), b16),
            ((rows, 2 * COLS + LANES), b16),
        ],
        [VM] * 3,
        moved=weights_tiled.size * 6,
    )(weights_tiled, rep, split)


def spread_mask(first_row, rows, first, cols):
    row = first_row + lax.broadcasted_iota(jnp.int32, (rows, cols), 0)
    col = first + lax.broadcasted_iota(jnp.int32, (rows, cols), 1)
    gap = col - 3 * row
    return jnp.where((gap >= 0) & (gap < 3), 1.0, 0.0).astype(b16)


def unpack(gathered):
    def body(w_ref, rep_ref, split_ref):
        flat = w_ref[:, ATT:]
        turned = flat.astype(f32).T
        rep_ref[...] = turned[:16]
        low = turned[:24].astype(b16)
        step = VCOL // 3
        for i in range(3):
            rows = D // 3
            mask = spread_mask(i * rows, rows, i * step, step)
            spread = dot(low[:, i * rows : (i + 1) * rows], mask)
            phase = lax.rem(lax.broadcasted_iota(jnp.int32, (1, step), 1), 3)
            for layer in range(LAYERS):
                at = 6 * LAYERS + 3 * layer
                value = jnp.where(
                    phase == 0,
                    spread[at : at + 1],
                    jnp.where(phase == 1, spread[at + 1 : at + 2], spread[at + 2 : at + 3]),
                )
                split_ref[layer : layer + 1, i * step : (i + 1) * step] = value

    return call(
        body,
        [((16, D), f32), ((8, VCOL), f32)],
        [VM],
        moved=D * LANES * 2,
        flops=24 * D * VCOL,
    )(gathered)


def gelu_parts(inner):
    cdf = 0.5 * (1.0 + lax.erf(inner * (0.5**0.5)))
    dens = jnp.exp(-0.5 * inner * inner) * 0.3989422804014327
    return inner * cdf, cdf + inner * dens


def attend(h_low, layer, w_ref, split_ref, seg_ref, part_ref, qkv_ref, probs_ref, ctx_ref):
    mixed = dot(h_low, w_ref[:, :QKV])
    qkv_ref[:, :HD] = (mixed[:, :HD] + split_ref[layer : layer + 1, :HD]).astype(b16)
    qkv_ref[:, HD : 2 * HD] = mixed[:, HD : 2 * HD].astype(b16)
    qkv_ref[:, 2 * HD :] = (
        mixed[:, 2 * HD :] + split_ref[layer : layer + 1, HD : 2 * HD]
    ).astype(b16)
    seg = jnp.broadcast_to(seg_ref[...].astype(f32), (SEQ, SEQ))
    same = seg == seg.T
    low_half = lax.broadcasted_iota(jnp.int32, (1, LANES), 1) < HEAD_DIM
    for pair in range(HD // LANES):
        at = pair * LANES
        query = qkv_ref[:, at : at + LANES].astype(f32) * HEAD_DIM ** (-0.5)
        keys = qkv_ref[:, HD + at : HD + at + LANES]
        values = qkv_ref[:, 2 * HD + at : 2 * HD + at + LANES].astype(f32)
        total = jnp.zeros((SEQ, LANES), f32)
        for half in range(2):
            mine = low_half if half == 0 else ~low_half
            scores = dot(jnp.where(mine, query, 0.0).astype(b16), keys, contract_last)
            scores = jnp.where(same, scores, -1000000000.0)
            raised = jnp.exp(scores - jnp.max(scores, axis=-1, keepdims=True))
            probs = (raised * (1.0 / jnp.sum(raised, axis=-1, keepdims=True))).astype(b16)
            probs_ref[2 * pair + half] = probs
            total = total + dot(probs, jnp.where(mine, values, 0.0).astype(b16))
        ctx_ref[:, at : at + LANES] = total.astype(b16)
    part_ref[...] = dot(ctx_ref[...], w_ref[:, QKV:ATT], contract_last).astype(b16)


ATT_FLOPS = 2 * SEQ * D * ATT + 4 * SEQ * SEQ * HD * 2
FFN_FLOPS = 2 * SEQ * D * 2 * FFT


ATT_OUTS = [((MICRO, SEQ, QKV), b16), ((MICRO, HD // HEAD_DIM, SEQ, SEQ), b16), ((MICRO, SEQ, HD), b16)]


def attention_first(block_in, segments, split, matrix):
    def body(h_ref, seg_ref, split_ref, w_ref, part_ref, qkv_ref, probs_ref, ctx_ref):
        for m in range(MICRO):
            views = [r.at[m] for r in (part_ref, qkv_ref, probs_ref, ctx_ref)]
            attend(h_ref[m], 0, w_ref, split_ref, seg_ref[m], *views)

    return call(
        body,
        [((MICRO, SEQ, D), b16)] + ATT_OUTS,
        [VM] * 4,
        flops=2 * ATT_FLOPS,
        moved=12 << 20,
        limit=16,
    )(block_in, segments, split, matrix)


def attention_next(micro, layer, normed, part_own, part_other, rep, segments, split, matrix):
    base = 6 * (layer - 1)

    def body(n_ref, own_ref, other_ref, rep_ref, seg_ref, split_ref, w_ref, *refs):
        part_ref, qkv_ref, probs_ref, ctx_ref, n2_ref, s2_ref, low_ref = refs
        first = n_ref[micro] * rep_ref[base + 1 : base + 2] + rep_ref[base + 2 : base + 3]
        added = own_ref[...].astype(f32) + other_ref[...].astype(f32)
        n2, s2 = norm_rows(first + added + rep_ref[base + 3 : base + 4])
        n2_ref[...] = n2
        s2_ref[...] = s2
        low = (n2 * rep_ref[base + 4 : base + 5] + rep_ref[base + 5 : base + 6]).astype(b16)
        low_ref[...] = low
        attend(
            low, layer, w_ref, split_ref, seg_ref[micro], part_ref, qkv_ref, probs_ref, ctx_ref
        )

    return call(
        body,
        [((SEQ, D), b16)]
        + [(shape[1:], kind) for shape, kind in ATT_OUTS]
        + [((SEQ, D), f32), ((SEQ, 1), f32), ((SEQ, D), b16)],
        [VM] * 7,
        flops=ATT_FLOPS,
        moved=8 << 20,
    )(normed, part_own, part_other, rep, segments, split, matrix)


def feed_step(hidden_in, added, layer, rep_ref, split_ref, w_ref, outs):
    base = 6 * layer
    part_ref, n1_ref, s1_ref, low_ref, act_ref, slope_ref = outs
    n1, s1 = norm_rows(hidden_in + added + rep_ref[base : base + 1])
    n1_ref[...] = n1
    s1_ref[...] = s1
    low_ref[...] = (n1 * rep_ref[base + 1 : base + 2] + rep_ref[base + 2 : base + 3]).astype(b16)
    step = 512
    for at in range(0, FFT, step):
        inner = (
            dot(low_ref[...], w_ref[:, at : at + step])
            + split_ref[layer : layer + 1, 2 * HD + at : 2 * HD + at + step]
        )
        active, slope = gelu_parts(inner)
        act_ref[:, at : at + step] = active.astype(b16)
        slope_ref[:, at : at + step] = slope.astype(b16)
    part_ref[...] = dot(act_ref[...], w_ref[:, FFT:], contract_last).astype(b16)


FEED_OUTS = [
    ((SEQ, D), b16),
    ((SEQ, D), f32),
    ((SEQ, 1), f32),
    ((SEQ, D), b16),
    ((SEQ, FFT), b16),
    ((SEQ, FFT), b16),
]


def feed_first(hidden, part_own, part_other, rep, split, matrix):
    def body(h_ref, own_ref, other_ref, rep_ref, split_ref, w_ref, *refs):
        parts, outs = refs[:MICRO], refs[MICRO:]
        for m in range(MICRO):
            added = own_ref[m].astype(f32) + other_ref[m].astype(f32)
            views = [parts[m]] + [r.at[m] for r in outs]
            feed_step(h_ref[m].astype(f32), added, 0, rep_ref, split_ref, w_ref, views)

    return call(
        body,
        [((SEQ, D), b16)] * MICRO + [((MICRO,) + shape, kind) for shape, kind in FEED_OUTS[1:]],
        [VM] * 6,
        flops=2 * FFN_FLOPS,
        moved=20 << 20,
        limit=22,
    )(hidden, part_own, part_other, rep, split, matrix)


def feed_forward(micro, layer, hidden, part_own, part_other, rep, split, matrix):
    base = 6 * layer

    def body(h_ref, own_ref, other_ref, rep_ref, split_ref, w_ref, *outs):
        hidden_in = h_ref[...] * rep_ref[base - 2 : base - 1] + rep_ref[base - 1 : base]
        added = own_ref[...].astype(f32) + other_ref[...].astype(f32)
        feed_step(hidden_in, added, layer, rep_ref, split_ref, w_ref, outs)

    return call(
        body,
        FEED_OUTS,
        [VM] * 6,
        flops=FFN_FLOPS,
        moved=10 << 20,
    )(hidden, part_own, part_other, rep, split, matrix)


def view(ref, micro):
    return ref.at[micro] if ref.shape[0] == MICRO else ref


def feed_back_tail(grad, n2, s2, layer, rep_ref, slope_ref, w_ref, outs):
    base = 6 * layer
    part_ref, res_ref, dffn_ref, din_ref, vec_ref = outs
    back, gain, shift = norm_back(grad, n2, s2, rep_ref[base + 4 : base + 5])
    res_ref[...] = back
    dffn_ref[...] = back.astype(b16)
    vec_ref[...] = jnp.zeros_like(vec_ref)
    vec_ref[0:1] = jnp.sum(back, axis=0, keepdims=True)
    vec_ref[1:2] = gain
    vec_ref[2:3] = shift
    step = 384
    for at in range(0, FFT, step):
        grad_act = dot(dffn_ref[...], w_ref[:, FFT + at : FFT + at + step])
        grad_in = (slope_ref[:, at : at + step].astype(f32) * grad_act).astype(b16)
        din_ref[:, at : at + step] = grad_in
        row, lane = 3 + at // D, at % D
        vec_ref[row : row + 1, lane : lane + step] = jnp.sum(
            grad_in.astype(f32), axis=0, keepdims=True
        )
    part_ref[...] = dot(din_ref[...], w_ref[:, :FFT], contract_last).astype(b16)


BACK_OUTS = [
    ((SEQ, D), b16),
    ((SEQ, D), f32),
    ((SEQ, D), b16),
    ((SEQ, FFT), b16),
    ((8, D), f32),
]


def feed_back_top(micro, layer, out_grad, n1, part_own, part_other, rep, slope, matrix):
    base = 6 * layer

    def body(g_ref, n_ref, own_ref, other_ref, rep_ref, slope_ref, w_ref, *refs):
        out_ref = refs[5]
        first = n_ref[...] * rep_ref[base + 1 : base + 2] + rep_ref[base + 2 : base + 3]
        added = own_ref[...].astype(f32) + other_ref[...].astype(f32)
        n2, s2 = norm_rows(first + added + rep_ref[base + 3 : base + 4])
        out_ref[...] = (n2 * rep_ref[base + 4 : base + 5] + rep_ref[base + 5 : base + 6]).astype(b16)
        feed_back_tail(
            g_ref[micro].astype(f32), n2, s2, layer, rep_ref, slope_ref, w_ref, refs[:5]
        )

    return call(
        body,
        BACK_OUTS + [((SEQ, D), b16)],
        [VM] * 6 + [VM],
        flops=FFN_FLOPS,
        moved=11 << 20,
    )(out_grad, n1, part_own, part_other, rep, slope, matrix)


def feed_back(micro, layer, mid, part_own, part_other, n2, s2, rep, slope, matrix):
    def body(mid_ref, own_ref, other_ref, n2_ref, s2_ref, rep_ref, slope_ref, w_ref, *refs):
        added = own_ref[...].astype(f32) + other_ref[...].astype(f32)
        feed_back_tail(
            mid_ref[...] + added,
            view(n2_ref, micro)[...],
            view(s2_ref, micro)[...],
            layer,
            rep_ref,
            view(slope_ref, micro),
            w_ref,
            refs[:5],
        )

    return call(
        body,
        BACK_OUTS,
        [VM] * 7 + [VM],
        flops=FFN_FLOPS,
        moved=11 << 20,
    )(mid, part_own, part_other, n2, s2, rep, slope, matrix)


def attention_back(micro, layer, res, part_own, part_other, n1, s1, rep, qkv, probs, ctx, matrix):
    base = 6 * layer

    def body(
        res_ref, own_ref, other_ref, n1_ref, s1_ref, rep_ref, qkv_ref, probs_ref, ctx_ref, w_ref, *refs
    ):
        part_ref, mid_ref, datt_ref, dqkv_ref, vec_ref = refs
        n1_ref, s1_ref, qkv_ref, probs_ref, ctx_ref = (
            view(r, micro) for r in (n1_ref, s1_ref, qkv_ref, probs_ref, ctx_ref)
        )
        grad = res_ref[...] + (own_ref[...].astype(f32) + other_ref[...].astype(f32))
        back, gain, shift = norm_back(grad, n1_ref[...], s1_ref[...], rep_ref[base + 1 : base + 2])
        mid_ref[...] = back
        datt_ref[...] = back.astype(b16)
        vec_ref[...] = jnp.zeros_like(vec_ref)
        vec_ref[0:1] = jnp.sum(back, axis=0, keepdims=True)
        vec_ref[1:2] = gain
        vec_ref[2:3] = shift
        dctx = dot(datt_ref[...], w_ref[:, QKV:ATT]).astype(b16).astype(f32)
        low_half = lax.broadcasted_iota(jnp.int32, (1, LANES), 1) < HEAD_DIM
        factor = HEAD_DIM ** (-0.5)
        for pair in range(HD // LANES):
            at = pair * LANES
            query = qkv_ref[:, at : at + LANES].astype(f32) * factor
            keys = qkv_ref[:, HD + at : HD + at + LANES].astype(f32) * factor
            values = qkv_ref[:, 2 * HD + at : 2 * HD + at + LANES]
            dc = dctx[:, at : at + LANES]
            weighed = dc * ctx_ref[:, at : at + LANES].astype(f32)
            dq = jnp.zeros((SEQ, LANES), f32)
            dk = jnp.zeros((SEQ, LANES), f32)
            dv = jnp.zeros((SEQ, LANES), f32)
            for half in range(2):
                mine = low_half if half == 0 else ~low_half
                dcm = jnp.where(mine, dc, 0.0).astype(b16)
                delta = jnp.sum(jnp.where(mine, weighed, 0.0), axis=-1, keepdims=True)
                probs = probs_ref[2 * pair + half]
                dprobs = dot(dcm, values, contract_last)
                dscores = (probs.astype(f32) * (dprobs - delta)).astype(b16)
                dq = dq + dot(dscores, jnp.where(mine, keys, 0.0).astype(b16))
                dk = dk + dot(dscores, jnp.where(mine, query, 0.0).astype(b16), contract_first)
                dv = dv + dot(probs, dcm, contract_first)
            dqkv_ref[:, at : at + LANES] = dq.astype(b16)
            dqkv_ref[:, HD + at : HD + at + LANES] = dk.astype(b16)
            dqkv_ref[:, 2 * HD + at : 2 * HD + at + LANES] = dv.astype(b16)
        vec_ref[3:4, :HD] = jnp.sum(dqkv_ref[:, :HD].astype(f32), axis=0, keepdims=True)
        vec_ref[3:4, HD:] = jnp.sum(dqkv_ref[:, 2 * HD :].astype(f32), axis=0, keepdims=True)
        part_ref[...] = dot(dqkv_ref[...], w_ref[:, :QKV], contract_last).astype(b16)

    return call(
        body,
        [
            ((SEQ, D), b16),
            ((SEQ, D), f32),
            ((SEQ, D), b16),
            ((SEQ, QKV), b16),
            ((8, D), f32),
        ],
        [VM] * 9 + [VM],
        flops=2 * ATT_FLOPS,
        moved=9 << 20,
    )(res, part_own, part_other, n1, s1, rep, qkv, probs, ctx, matrix)


def finish_input(mids, owns, others):
    def body(*refs):
        for micro in range(MICRO):
            m, a, b = refs[3 * micro : 3 * micro + 3]
            refs[-1][micro] = m[...] + (a[...].astype(f32) + b[...].astype(f32))

    args = []
    for micro in range(MICRO):
        args += [mids[micro], owns[micro], others[micro]]
    return call(body, [((MICRO, SEQ, D), f32)], [VM] * len(args), moved=7 << 20)(*args)[0]


def store_slots(product_ref, outs, at, width):
    if len(outs) == 1:
        outs[0][:, at : at + width] = product_ref[:, :width].astype(b16)
        return
    ring, rows = outs[0].shape[1], outs[0].shape[2]
    z, x, c = places(ring)
    for other in range(2):
        for xo in range(2):
            for k in range(ring):
                zz = lax.rem(z + k, ring)
                xx = lax.rem(x + xo, 2)
                cc = lax.rem(c + other, 2)
                row = pl.multiple_of(((zz * 2 + xx) * 2 + cc) * rows, 16)
                outs[other][xo, k, :, at : at + width] = product_ref[
                    pl.ds(row, rows), :width
                ].astype(b16)


def grad_outs(ndp, pieced, cols):
    rows = D // ndp
    if pieced:
        return [((2, ndp // 4, rows, cols), b16)] * 2
    return [((D, cols), b16)]


def matrix_gradient(sets, pieced, ndp, vectors=None):
    widths = [s[2] for s in sets]
    total = sum(widths) + (LANES if vectors is not None else 0)
    outs = grad_outs(ndp, pieced, total)
    args, specs = [], []
    for left, right, _ in sets:
        for micro in range(MICRO):
            specs.append(VM)
            args.append(left[micro])
        for micro in range(MICRO):
            args.append(right[micro])
            specs.append(VM)
    plain = len(args)
    if vectors is not None:
        args += vectors
        specs += [VM] * len(vectors)
    n_in = len(args)
    step = 384

    def body(*refs):
        out_refs = refs[n_in : n_in + len(outs)]
        prod_ref = refs[n_in + len(outs)]
        at = 0
        for index, width in enumerate(widths):
            l0, l1, r0, r1 = refs[4 * index : 4 * index + 4]
            left = [r[m] if len(r.shape) == 3 else r[...] for m, r in enumerate((l0, l1))]
            r0, r1 = (r.at[m] if len(r.shape) == 3 else r for m, r in enumerate((r0, r1)))
            for col in range(0, width, step):
                prod_ref[...] = dot(left[0], r0[:, col : col + step], contract_first) + dot(
                    left[1], r1[:, col : col + step], contract_first
                )
                store_slots(prod_ref, out_refs, at, step)
                at += step
        if vectors is not None:
            pack_vectors(refs[plain:n_in], prod_ref)
            store_slots(prod_ref, out_refs, at, LANES)

    moved = sum(a.size * 2 for a in args[:plain]) + D * total * 2
    return call(
        body,
        outs,
        specs,
        [pltpu.VMEM((D, step), f32)],
        flops=2 * MICRO * SEQ * D * total,
        moved=moved,
    )(*args)


def pack_vectors(vec_refs, prod_ref):
    sums = []
    for layer in range(LAYERS):
        a0, a1, b0, b1 = vec_refs[4 * layer : 4 * layer + 4]
        sums.append((a0[...] + a1[...], b0[...] + b1[...]))
    rows = []
    for att, ffn in sums:
        rows += [att[0:1], att[1:2], att[2:3], ffn[0:1], ffn[1:2], ffn[2:3]]
    rows.append(jnp.zeros((4, D), f32))
    turned = jnp.concatenate(rows, axis=0)
    turned = jnp.concatenate([turned, jnp.zeros((LANES - 16, D), f32)], axis=0).T
    step = VCOL // 3
    phase = lax.rem(lax.broadcasted_iota(jnp.int32, (1, step), 1), 3)
    lane = lax.broadcasted_iota(jnp.int32, (1, LANES), 1)
    for i in range(3):
        picked = []
        for att, ffn in sums:
            line = (att[3:4], ffn[3:4], ffn[4:5])[i]
            for j in range(3):
                picked.append(jnp.where(phase == j, line, 0.0))
        picked = jnp.concatenate(
            [jnp.zeros((12, step), f32)] + picked + [jnp.zeros((LANES - 18, step), f32)], axis=0
        ).astype(b16)
        n_rows = D // 3
        mask = spread_mask(i * n_rows, n_rows, i * step, step)
        part = dot(mask, picked, contract_last)
        keep = turned[i * n_rows : (i + 1) * n_rows]
        prod_ref[i * n_rows : (i + 1) * n_rows, :LANES] = jnp.where(lane < 12, keep, part)


def meet(own, met, places):
    lo, hi = places[0], places[-1] + 1
    return (own[1, lo:hi].astype(f32) + met[1, lo:hi].astype(f32)).astype(b16)


def pass_on(own, met, got, places):
    lo, hi = places[0], places[-1] + 1
    total = own[0, lo:hi].astype(f32) + met[0, lo:hi].astype(f32) + got.astype(f32)
    return [total[i].astype(b16) for i in range(hi - lo)]


def pass_both(own, met, k, received=None):
    total = own[:, k].astype(f32) + met[:, k].astype(f32)
    if received is not None:
        total = total + received.astype(f32)
    return total.astype(b16)


def close(own, met, parts, vectors=False):
    _, _, rows, cols = own.shape
    mats = cols - LANES if vectors else cols
    parts = [p if isinstance(p, tuple) else (p, None) for p in parts]
    n = len(parts)

    def body(own_ref, met_ref, *refs):
        out_ref, sq_ref = refs[n:]
        total = jnp.zeros((rows, LANES), f32)
        for at in range(0, cols, LANES):
            s = slice(at, at + LANES)
            value = own_ref[0, 0, :, s].astype(f32) + met_ref[0, 0, :, s].astype(f32)
            for (_, index), ref in zip(parts, refs[:n]):
                value = value + (ref[:, s] if index is None else ref[index, :, s]).astype(f32)
            out_ref[:, s] = value
            square = value * value
            if at >= mats:
                lane = lax.broadcasted_iota(jnp.int32, (rows, LANES), 1)
                twice = (lane < 6 * LAYERS) & (lax.axis_index("tensor") != 0)
                square = jnp.where(twice, 0.0, square)
            total = total + square
        part = total[:8]
        for i in range(8, rows, 8):
            part = part + total[i : i + 8]
        sq_ref[...] = part

    return call(
        body,
        [((rows, cols), f32), ((8, LANES), f32)],
        [VM] * (2 + n),
        moved=rows * cols * 14,
    )(own, met, *[p[0] for p in parts])


def adamw(value, first, second, grad, rate, decay):
    first = 0.5 * first + 0.5 * grad
    second = 0.5 * second + 0.5 * grad * grad
    correct = 1.0 - 0.5**STEP
    direction = first / correct / (jnp.sqrt(second / correct) + 1e-08)
    return (value - rate * (direction + decay * value), first, second)


def clip_factor(squares):
    norm = jnp.sqrt(jnp.sum(squares, keepdims=True))
    return norm, jnp.minimum(1.0, clip_limit / (norm + 1e-06))


def ready(tiled, first, second):
    def body(w_ref, m_ref, v_ref, w_out, m_out, v_out):
        w_out[...] = w_ref[...] * (1.0 - weight_rate * weight_decay)
        m_out[...] = 0.5 * m_ref[...]
        v_out[...] = 0.5 * v_ref[...]

    return call(body, [(tiled.shape, f32)] * 3, [VM] * 3, moved=24 * tiled.size)(tiled, first, second)


def stepped(decayed, half_first, half_second, grad, rate):
    first = half_first + 0.5 * grad
    second = half_second + 0.5 * grad * grad
    correct = 1.0 - 0.5**STEP
    direction = first / correct / (jnp.sqrt(second / correct) + 1e-08)
    return decayed - rate * direction, first, second


def update_vectors(block, squares, reps, splits):
    rows = block.shape[0]
    per = splits[0].shape[2]

    def body(b_ref, q_ref, rw, rm, rv, sw, sm, sv, norm_ref, rwo, rmo, rvo, rlo, go, swo, smo, svo, slo):
        norm, scale = clip_factor(q_ref[...])
        norm_ref[...] = norm
        turned = jnp.concatenate([b_ref[...], jnp.zeros((LANES - rows, LANES), f32)], axis=0).T
        for layer in range(LAYERS):
            at = slice(layer, layer + 1)
            for kind in range(6):
                grad = turned[6 * layer + kind : 6 * layer + kind + 1, :rows] * scale
                new = adamw(rw[kind, at], rm[kind, at], rv[kind, at], grad, vector_rate, 0.0)
                rwo[kind, at], rmo[kind, at], rvo[kind, at] = new
                rlo[kind, at] = new[0].astype(b16)
                if kind == 0:
                    go[at] = grad
        row = lax.broadcasted_iota(jnp.int32, (rows, per), 0)
        col = lax.broadcasted_iota(jnp.int32, (rows, per), 1)
        gap = col - 3 * row
        mask = jnp.where((gap >= 0) & (gap < 3), 1.0, 0.0)
        wide = lax.dot_general(
            turned[6 * LAYERS : 6 * LAYERS + 8, :rows],
            mask,
            (((1,), (0,)), ((), ())),
            preferred_element_type=f32,
            precision=lax.Precision.HIGHEST,
        )
        phase = lax.rem(lax.broadcasted_iota(jnp.int32, (1, per), 1), 3)
        for layer in range(LAYERS):
            one, two, three = (wide[3 * layer + j : 3 * layer + j + 1] for j in range(3))
            grad = jnp.where(phase == 0, one, jnp.where(phase == 1, two, three)) * scale
            new = adamw(sw[layer], sm[layer], sv[layer], grad, vector_rate, 0.0)
            swo[layer], smo[layer], svo[layer] = new
            slo[layer] = new[0].astype(b16)

    rep, split = reps[0].shape, splits[0].shape
    return call(
        body,
        [((1, 1), f32)]
        + [(rep, f32)] * 3
        + [(rep, b16), ((LAYERS, rows), f32)]
        + [(split, f32)] * 3
        + [(split, b16)],
        [VM] * 8,
        moved=1 << 18,
    )(block, squares, *reps, *splits)


def update_matrices(decayed, first, second, grads, squares):
    rows = grads[0].shape[0]
    tiled = decayed
    step = 8 if rows % 8 == 0 else rows
    n_steps = rows // step
    block = (1, step * TILES, LANES)

    def body(f_ref, w_ref, m_ref, v_ref, a0, f0, a1, f1, nw, nm, nv, nl):
        scale = clip_factor(f_ref[...])[1]
        layer = pl.program_id(0)
        for c in range(TILES):
            if c < ATT // LANES:
                lo = c * LANES
                grad = jnp.where(layer == 0, a0[:, lo : lo + LANES], a1[:, lo : lo + LANES])
            else:
                lo = c * LANES - ATT
                grad = jnp.where(layer == 0, f0[:, lo : lo + LANES], f1[:, lo : lo + LANES])
            where = (0, pl.ds(c, step, stride=TILES), slice(None))
            new = stepped(w_ref[where], m_ref[where], v_ref[where], grad * scale, weight_rate)
            nw[where], nm[where], nv[where] = new
        nl[...] = nw[...].astype(b16)

    big = pl.BlockSpec(block, lambda l, i: (l, i, 0))
    shape = tiled.shape
    return pl.pallas_call(
        body,
        grid=(LAYERS, n_steps),
        out_shape=[jax.ShapeDtypeStruct(shape, f32)] * 3 + [jax.ShapeDtypeStruct(shape, b16)],
        in_specs=[pl.BlockSpec((8, LANES), lambda l, i: (0, 0)), big, big, big]
        + [pl.BlockSpec((step, g.shape[1]), lambda l, i: (i, 0)) for g in grads],
        out_specs=[big] * 4,
        compiler_params=pltpu.CompilerParams(vmem_limit_bytes=13 * 1024 * 1024),
        cost_estimate=pl.CostEstimate(
            flops=20 * tiled.size, bytes_accessed=30 * tiled.size, transcendentals=tiled.size
        ),
    )(squares, tiled, first, second, *grads)


def sum_everywhere(value):
    ndp = lax.axis_size("dp")
    if ndp & (ndp - 1) or ndp < 4:
        return lax.psum(value, ("dp", "tensor"))

    def level(a, first, second):
        one, two, both = ppermute_bits(a, first), ppermute_bits(a, second), ppermute_bits(a, first | second)
        return (a + one) + (two + both)

    value = value + ppermute_bits(value, 2)
    value = level(value, 4, 1)
    bit = 8
    while bit < 2 * ndp:
        if 2 * bit < 2 * ndp:
            value = level(value, bit, 2 * bit)
        else:
            value = value + ppermute_bits(value, bit)
        bit *= 4
    return value


def ppermute_bits(value, bits):
    n = 2 * lax.axis_size("dp")
    return lax.ppermute(value, ("dp", "tensor"), [(i, i ^ bits) for i in range(n)])


def per_device(
    block_in,
    out_grad,
    segments,
    weights,
    weights_first,
    weights_second,
    split_vectors,
    split_first,
    split_second,
    rep_vectors,
    rep_first,
    rep_second,
):
    ndp = lax.axis_size("dp")
    rows = D // ndp
    per = split_vectors.shape[2]
    pieced = ndp == 16 and rows % 16 == 0
    shard_shape = weights.shape
    tiled_shape = (LAYERS, -1, LANES)
    masters = [a.reshape(tiled_shape) for a in (weights, weights_first, weights_second)]
    weights_tiled = masters[0]
    rep_flat = rep_vectors.reshape(LAYERS * 6, -1)
    split_flat = split_vectors.reshape(LAYERS, per)
    both = range(MICRO)
    seg = segments.reshape(MICRO, 1, SEQ)
    if pieced:
        a0, f0, l1, every = prep(weights_tiled, rep_flat, split_flat)
        across = partial(move, kind="x")
        third = slice(COLS + LANES, COLS + LANES + ATT)
        fourth = slice(COLS + LANES + ATT, None)

        def finish(slots, cols):
            mine = [stack(half, rows, cols) for half in (slots[:4], slots[4:])]
            return settle(mine, [move(a, "core") for a in mine])

        def cut(array, cols):
            return (array, (slice(None), cols))

        x0 = across(every)
        a0_r1, a0_r2, a0_r3, f0 = tie(move(a0, 1), move(a0, 2), move(a0, 3), f0)
        a0_x = across(stack([a0_r1, a0_r2, a0_r3], rows, ATT + LANES))
        f0_r1, f0_r3 = move(f0, 1), move(f0, 3)
        near = stack([a0, a0_r1, a0_r2, a0_r3], rows, ATT + LANES)
        mine0 = stack(
            [cut(x0, slice(0, ATT + LANES)), (a0_x, 0), (a0_x, 1), (a0_x, 2)], rows, ATT + LANES
        )
        mine0, f0_r1, f0_r3, l1 = tie(mine0, f0_r1, f0_r3, l1)
        watt0 = settle([near, mine0], [move(near, "core"), move(mine0, "core")])
        f0_x13 = across(stack([f0_r1, f0_r3], rows, 2 * FFT))
        f0_r2 = move(f0_r1, 1)
        l1_r1, l1_r3 = move(l1, 1), move(l1, 3)
        f0_x2 = across(f0_r2)
    else:
        low = weights.astype(b16).reshape(LAYERS, rows, COLS)
        block = jnp.concatenate(
            [
                rep_flat.T,
                split_flat.reshape(LAYERS, rows, 3).transpose(1, 0, 2).reshape(rows, 6),
                jnp.zeros((rows, LANES - 18), f32),
            ],
            axis=1,
        ).astype(b16)
        gather = partial(lax.all_gather, axis_name="dp", axis=0, tiled=True)
        watt0 = gather(jnp.concatenate([low[0, :, :ATT], block], axis=1))
        watt1 = gather(low[1, :, :ATT])
        wffn0, wffn1 = (gather(low[layer, :, ATT:]) for layer in range(LAYERS))
    rep, split = unpack(watt0)

    done, qkv0, probs0, ctx0 = attention_first(block_in, seg, split, watt0)
    met = exchange(done)
    if pieced:
        head, tail = slice(0, ATT), slice(ATT, None)
        a1_r2 = move(stack([cut(l1_r1, head)], rows, ATT), 1)
        f0_x13, f0_x2, l1_r1, l1_r3, a1_r2, met = tie(f0_x13, f0_x2, l1_r1, l1_r3, a1_r2, met)
        a1_x = across(stack([cut(l1_r1, head), (a1_r2, 0), cut(l1_r3, head)], rows, ATT))
        f1_r2 = move(stack([cut(l1_r1, tail)], rows, 2 * FFT), 1)
        wffn0 = finish(
            [f0, f0_r1, f0_r2, f0_r3]
            + [cut(x0, slice(ATT + LANES, COLS + LANES)), (f0_x13, 0), f0_x2, (f0_x13, 1)],
            2 * FFT,
        )
    *done, n1_0, s1_0, low1_0, act0, slope0 = feed_first(block_in, done, met, rep, split, wffn0)
    if pieced:
        a1_x, f1_r2, *done = tie(a1_x, f1_r2, *done)
        f1_x = across(stack([cut(l1_r1, tail), (f1_r2, 0), cut(l1_r3, tail)], rows, 2 * FFT))
        watt1 = finish(
            [cut(l1, head), cut(l1_r1, head), (a1_r2, 0), cut(l1_r3, head), cut(x0, third)]
            + [(a1_x, k) for k in range(3)],
            ATT,
        )
    met = [exchange(a) for a in done]
    out = [
        attention_next(m, 1, n1_0, done[m], met[m], rep, seg, split, watt1) for m in both
    ]
    done = [o[0] for o in out]
    qkv1, probs1, ctx1, n2_0, s2_0, low_h1 = ([o[i] for o in out] for i in range(1, 7))
    if pieced:
        wffn1 = finish(
            [cut(l1, tail), cut(l1_r1, tail), (f1_r2, 0), cut(l1_r3, tail), cut(x0, fourth)]
            + [(f1_x, k) for k in range(3)],
            2 * FFT,
        )
    met = [exchange(a) for a in done]
    out = [feed_forward(m, 1, n2_0[m], done[m], met[m], rep, split, wffn1) for m in both]
    n1_1, s1_1, low1_1, act1, slope1 = ([o[i] for o in out] for i in range(1, 6))
    met = [exchange(o[0]) for o in out]

    out = [
        feed_back_top(m, 1, out_grad, n1_1[m], out[m][0], met[m], rep, slope1[m], wffn1)
        for m in both
    ]
    res, dffn, din, vec_f1 = ([o[i] for o in out] for i in range(1, 5))
    block_out = jnp.stack([o[5] for o in out])
    done = [o[0] for o in out]
    met = [exchange(o[0]) for o in out]
    plan = {"w_f1": 0, "f1_3": 1, "w_a1": 2, "f1_2": 3, "a1_s": 3, "w_f0": 4, "f1_1": 5, "a1_t": 6, "f0_s": 5}
    held, ends = {}, []

    def make(name):
        gate = ends[-1:] if 1 else []
        if name == "w_f1":
            g = matrix_gradient([(low1_1, din_1, FFT), (dffn_1, act1, FFT)], pieced, ndp)
        elif name == "w_a1":
            g = matrix_gradient(
                [(low_h1, dqkv_1, QKV), (datt_1, ctx1, HD)], pieced, ndp
            )
        elif name == "w_f0":
            g = matrix_gradient(
                [([low1_0] * 2, din_0, FFT), (dffn_0, [act0] * 2, FFT)], pieced, ndp
            )
        elif not pieced:
            return []
        if name.startswith("w_"):
            held[name[2:]] = g if not pieced else (g[0], move(g[1], "core"))
            return [g[0]]
        own, across_core = held[name[:2]]
        if name[:3] == "f1_":
            k = int(name[3])
            if k == 3:
                total = pass_both(own, after(across_core, *gate), k)
            else:
                total = pass_both(own, across_core, k, after(held["f1_rec"], *gate))
            held["f1_rec"] = move(total, 1)
            return [total]
        if name == "a1_t":
            parts = pass_on(own, across_core, after(held["a1_got"], *gate)[1:], (1, 2, 3))
            held["a1_r"] = [move(t, k + 1) for k, t in enumerate(parts)]
            return [parts[2]]
        places = (0, 1, 2, 3) if name == "a1_s" else (2, 3)
        total = meet(own, after(across_core, *gate), places)
        held[name[:2] + "_got"] = move(total, "x")
        return [total]

    def before(stage, value):
        needed = [a for name in plan if plan[name] == stage for a in make(name)]
        return after(value, *needed) if needed else value

    din_1, dffn_1 = din, dffn
    out = []
    for m in both:
        value = before(m, res[m])
        out.append(
            attention_back(
                m, 1, value, done[m], met[m], n1_1[m], s1_1[m], rep, qkv1[m], probs1[m], ctx1[m], watt1
            )
        )
        ends.append(out[m][0])
    mid, datt_1, dqkv_1, vec_a1 = ([o[i] for o in out] for i in range(1, 5))
    done = [o[0] for o in out]
    met = [exchange(o[0]) for o in out]
    out = []
    for m in both:
        value = before(2 + m, mid[m])
        out.append(feed_back(m, 0, value, done[m], met[m], n2_0[m], s2_0[m], rep, slope0, wffn0))
        ends.append(out[m][0])
    res, dffn_0, din_0, vec_f0 = ([o[i] for o in out] for i in range(1, 5))
    done = [o[0] for o in out]
    met = [exchange(o[0]) for o in out]
    out = []
    for m in both:
        value = before(4 + m, res[m])
        out.append(
            attention_back(
                m, 0, value, done[m], met[m], n1_0, s1_0, rep, qkv0, probs0, ctx0, watt0
            )
        )
        ends.append(out[m][0])
    mid, datt, dqkv, vec_a0 = ([o[i] for o in out] for i in range(1, 5))
    done = [o[0] for o in out]
    met = [exchange(o[0]) for o in out]
    dqkv[0] = before(6, dqkv[0])
    g_a0 = matrix_gradient(
        [([block_in] * MICRO, dqkv, QKV), (datt, [ctx0] * 2, HD)],
        pieced,
        ndp,
        vectors=vec_a0 + vec_f0 + vec_a1 + vec_f1,
    )
    ends.append(g_a0[0])
    before(7, g_a0[0])
    if pieced:
        (f1_own, f1_met), (a1_own, a1_met), (f0_own, f0_met) = (held[c] for c in ("f1", "a1", "f0"))
        f1_rec, a1_got, a1_r, f0_got_hi = (held[c] for c in ("f1_rec", "a1_got", "a1_r", "f0_got"))
    else:
        g_f1, g_a1, g_f0 = (held[c] for c in ("f1", "a1", "f0"))
    if pieced:
        masters = ready(*(after(a, g_a0[0]) for a in masters))
        input_grad = finish_input(mid, done, met)
        a0_own, a0_met = g_a0[0], move(g_a0[1], "core")
        a0_got = across(meet(a0_own, a0_met, (0, 1, 2, 3)))
        f1_last = pass_both(f1_own, f1_met, 0, f1_rec)
        f1_got = across(f1_last[1])
        f0_t2, f0_t3 = pass_on(f0_own, f0_met, f0_got_hi, (2, 3))
        f0_r3, f0_r2 = move(f0_t3, 3), move(f0_t2, 2)
        a0_got, f0_r3, f0_r2, *a1_r = tie(a0_got, f0_r3, f0_r2, *a1_r)
        f0_got_lo = across(meet(f0_own, f0_met, (0, 1)))
        a0_t = pass_on(a0_own, a0_met, a0_got[1:], (1, 2, 3))
        a0_r = [move(t, k + 1) for k, t in enumerate(a0_t)]
        grad_a1, sq_a1 = close(a1_own, a1_met, [(a1_got, 0)] + a1_r)
        grad_f1, sq_f1 = close(f1_own, f1_met, [f1_got, (f1_rec, 0)])
        f0_got_lo, grad_f1, grad_a1, block_out, input_grad, *rest = tie(
            f0_got_lo, grad_f1, grad_a1, block_out, input_grad, *a0_r, *masters
        )
        a0_r, masters = rest[:3], rest[3:]
        f0_r1 = move(pass_on(f0_own, f0_met, f0_got_lo[1:], (1,))[0], 1)
        grad_a0, sq_a0 = close(a0_own, a0_met, [(a0_got, 0)] + a0_r, vectors=True)
        grad_f0, sq_f0 = close(f0_own, f0_met, [(f0_got_lo, 0), f0_r1, f0_r2, f0_r3])
        squares = (sq_f1 + sq_a1) + (sq_f0 + sq_a0)
    else:
        input_grad = finish_input(mid, done, met)
        scatter = lambda g: lax.psum_scatter(g[0], "dp", scatter_dimension=0, tiled=True).astype(f32)
        grad_f1, grad_a1, grad_f0, grad_a0 = (scatter(g) for g in (g_f1, g_a1, g_f0, g_a0))
        once = jnp.where(lax.axis_index("tensor") == 0, 1.0, 0.0).astype(f32)
        square = lambda a: jnp.sum(a * a)
        squares = (
            square(grad_a0[:, :ATT])
            + square(grad_f0)
            + square(grad_a1)
            + square(grad_f1)
            + square(grad_a0[:, ATT + 12 :])
            + once * square(grad_a0[:, ATT : ATT + 12])
        )
        squares = jnp.full((8, LANES), squares / (8 * LANES), f32)

    squares = sum_everywhere(squares)
    if pieced:
        new = update_matrices(*masters, [grad_a0, grad_f0, grad_a1, grad_f1], squares)
        turn = lambda a: jnp.transpose(a, (1, 0, 2))
        vectors = update_vectors(
            grad_a0[:, ATT:],
            squares,
            [turn(a) for a in (rep_vectors, rep_first, rep_second)],
            (split_vectors, split_first, split_second),
        )
        grad_norm = vectors[0][0, 0]
        new_rep, rep_first_new, rep_second_new, rep_low = (turn(a) for a in vectors[1:5])
        bias_grad = vectors[5]
        new_split, split_first_new, split_second_new, split_low = vectors[6:]
    else:
        block = grad_a0[:, ATT:]
        grad_rep = block[:, :12].T.reshape(rep_vectors.shape)
        grad_split = (
            block[:, 12:18].reshape(rows, LAYERS, 3).transpose(1, 0, 2).reshape(split_vectors.shape)
        )
        grad_norm, factor = (a[0, 0] for a in clip_factor(squares))
        clipped_rep = grad_rep * factor
        grad = jnp.stack(
            [
                jnp.concatenate([grad_a0[:, :ATT], grad_f0], axis=1),
                jnp.concatenate([grad_a1, grad_f1], axis=1),
            ]
        ).reshape(tiled_shape)
        new = adamw(*masters, grad * factor, weight_rate, weight_decay)
        new = (*new, new[0].astype(b16))
        new_split, split_first_new, split_second_new = adamw(
            split_vectors, split_first, split_second, grad_split * factor, vector_rate, 0.0
        )
        new_rep, rep_first_new, rep_second_new = adamw(
            rep_vectors, rep_first, rep_second, clipped_rep, vector_rate, 0.0
        )
        split_low, rep_low = new_split.astype(b16), new_rep.astype(b16)
        bias_grad = clipped_rep[:, 0, :]
    new_weights, weights_first_new, weights_second_new, weights_low = (
        a.reshape(shard_shape) for a in new
    )
    return (
        block_out,
        input_grad,
        grad_norm,
        new_weights,
        weights_first_new,
        weights_second_new,
        weights_low,
        new_split,
        split_first_new,
        split_second_new,
        split_low,
        new_rep,
        rep_first_new,
        rep_second_new,
        rep_low,
        bias_grad,
    )


def solution(mesh):
    rows, packed, vector = P("dp", None, None), P(None, "tensor", "dp"), P(None, None, "dp")
    return jax.shard_map(
        per_device,
        mesh=mesh,
        in_specs=(rows, rows, P("dp", None)) + (packed,) * 6 + (vector,) * 3,
        out_specs=(rows, rows, P()) + (packed,) * 8 + (vector,) * 4 + (P(None, "dp"),),
        check_vma=False,
    )
```

```python
from functools import partial

import jax
import jax.numpy as jnp
from jax import lax
from jax.experimental import pallas as pl
from jax.experimental.pallas import tpu as pltpu
from jax.sharding import PartitionSpec as P

D = 768
HEAD_DIM = 64
LAYERS = 2
SEQ = 256
MICRO = 2
STEP = 3
HD = 384
FFT = 1536
QKV = 3 * HD
ATT = 4 * HD
COLS = ATT + 2 * FFT
VCOL = 2 * HD + FFT
LANES = 128
TILES = COLS // LANES

clip_limit = 1.0
weight_rate = 0.03
weight_decay = 0.01
vector_rate = 0.3
contract_last = (((1,), (1,)), ((), ()))
contract_first = (((0,), (0,)), ((), ()))
f32 = jnp.float32
b16 = jnp.bfloat16
VM = pl.BlockSpec(memory_space=pltpu.VMEM)


def call(body, outs, in_specs, scratch=(), flops=0, moved=0, out_specs=None, trans=0, limit=13):
    weight = 16 if flops else 1
    if out_specs is None:
        out_specs = [VM] * len(outs)
    return pl.pallas_call(
        body,
        out_shape=[jax.ShapeDtypeStruct(s, d) for s, d in outs],
        in_specs=in_specs,
        out_specs=out_specs,
        scratch_shapes=list(scratch),
        compiler_params=pltpu.CompilerParams(vmem_limit_bytes=limit * 1024 * 1024),
        cost_estimate=pl.CostEstimate(
            flops=int(flops * weight), bytes_accessed=int(moved * weight), transcendentals=trans
        ),
    )


def dot(a, b, dims=(((1,), (0,)), ((), ()))):
    return lax.dot_general(a, b, dims, preferred_element_type=f32)


def norm_rows(value):
    center = value - jnp.mean(value, axis=-1, keepdims=True)
    scale = lax.rsqrt(jnp.mean(center * center, axis=-1, keepdims=True) + 1e-12)
    return center * scale, scale


def norm_back(grad_out, normed, scale, gain):
    inner = grad_out * gain
    back = scale * (
        inner
        - jnp.mean(inner, axis=-1, keepdims=True)
        - normed * jnp.mean(inner * normed, axis=-1, keepdims=True)
    )
    return (
        back,
        jnp.sum(grad_out * normed, axis=0, keepdims=True),
        jnp.sum(grad_out, axis=0, keepdims=True),
    )


def places(ring):
    me = lax.axis_index("dp")
    return lax.div(me, 4), lax.rem(lax.div(me, 2), 2), lax.rem(me, 2)


def pairs_of(ndp, kind):
    if kind in (1, 2, 3):
        return [(i, (i + 4 * kind) % ndp) for i in range(ndp)]
    if kind == "x":
        return [(i, i ^ 2) for i in range(ndp)]
    return [(i, i ^ 1) for i in range(ndp)]


def move(a, kind):
    return lax.ppermute(a, "dp", pairs_of(lax.axis_size("dp"), kind))


def exchange(a):
    return lax.ppermute(a, "tensor", [(0, 1), (1, 0)])


def after(value, *others):
    return lax.optimization_barrier((value,) + others)[0]


def tie(*arrays):
    return lax.optimization_barrier(arrays)


def unique(entries):
    entries = [e if isinstance(e, tuple) else (e, Ellipsis) for e in entries]
    arrays, at = [], []
    for array, _ in entries:
        found = [i for i, a in enumerate(arrays) if a is array]
        if not found:
            found = [len(arrays)]
            arrays.append(array)
        at.append(found[0])
    return arrays, at, [where for _, where in entries]


def stack(entries, rows, cols, lead=None):
    arrays, at, where = unique(entries)
    lead = (len(entries),) if lead is None else lead

    def body(*refs):
        for i in range(len(entries)):
            place = (i,) if len(lead) == 1 else (i // lead[1], i % lead[1])
            refs[-1][place] = refs[at[i]][where[i]]

    size = len(entries) * rows * cols
    return call(body, [(lead + (rows, cols), b16)], [VM] * len(arrays), moved=4 * size)(*arrays)[0]


def settle(mine, met):
    ring, rows, cols = mine[0].shape

    def body(*refs):
        z, x, c = places(ring)
        for other in range(2):
            for xo in range(2):
                for k in range(ring):
                    zz = lax.rem(z - k + ring, ring)
                    xx = lax.rem(x + xo, 2)
                    cc = lax.rem(c + other, 2)
                    row = pl.multiple_of(((zz * 2 + xx) * 2 + cc) * rows, 16)
                    refs[4][pl.ds(row, rows), :] = refs[2 * other + xo][k]

    return call(
        body, [((4 * ring * rows, cols), b16)], [VM] * 4, moved=16 * ring * rows * cols
    )(*mine, *met)[0]


def prep(weights_tiled, rep, split):
    tiled_rows = weights_tiled.shape[1]
    rows = tiled_rows // TILES
    per = split.shape[1]

    def body(w_ref, rep_ref, split_ref, a0, f0, l1, every):
        a1, f1 = l1.at[:, :ATT], l1.at[:, ATT:]
        for layer, (a_ref, f_ref) in enumerate(((a0, f0), (a1, f1))):
            for c in range(TILES):
                piece = w_ref[layer, pl.ds(c, rows, stride=TILES), :].astype(b16)
                if c < ATT // LANES:
                    a_ref[:, c * LANES : (c + 1) * LANES] = piece
                else:
                    at = c * LANES - ATT
                    f_ref[:, at : at + LANES] = piece
        row = lax.broadcasted_iota(jnp.int32, (rows, rows), 0)
        col = lax.broadcasted_iota(jnp.int32, (rows, rows), 1)
        eye = (row == col).astype(b16)
        row3 = lax.broadcasted_iota(jnp.int32, (rows, per), 0)
        col3 = lax.broadcasted_iota(jnp.int32, (rows, per), 1)
        gap = col3 - 3 * row3
        block = jnp.zeros((rows, LANES), f32)
        lane = lax.broadcasted_iota(jnp.int32, (rows, LANES), 1)
        rep_cols = dot(eye, rep_ref[...].astype(b16), contract_last)
        rep_wide = jnp.concatenate(
            [rep_cols, jnp.zeros((rows, LANES - 6 * LAYERS), f32)], axis=1
        )
        block = rep_wide
        low = split_ref[...].astype(b16).astype(f32)
        for layer in range(LAYERS):
            for j in range(3):
                pick = jnp.where(gap == j, jnp.broadcast_to(low[layer : layer + 1], (rows, per)), 0.0)
                value = jnp.sum(pick, axis=1, keepdims=True)
                block = jnp.where(lane == 6 * LAYERS + 3 * layer + j, value, block)
        a0[:, ATT:] = block.astype(b16)
        every[:, : ATT + LANES] = a0[...]
        every[:, ATT + LANES : COLS + LANES] = f0[...]
        every[:, COLS + LANES :] = l1[...]

    return call(
        body,
        [
            ((rows, ATT + LANES), b16),
            ((rows, 2 * FFT), b16),
            ((rows, COLS), b16),
            ((rows, 2 * COLS + LANES), b16),
        ],
        [VM] * 3,
        moved=weights_tiled.size * 6,
    )(weights_tiled, rep, split)


def spread_mask(first_row, rows, first, cols):
    row = first_row + lax.broadcasted_iota(jnp.int32, (rows, cols), 0)
    col = first + lax.broadcasted_iota(jnp.int32, (rows, cols), 1)
    gap = col - 3 * row
    return jnp.where((gap >= 0) & (gap < 3), 1.0, 0.0).astype(b16)


def unpack(gathered):
    def body(w_ref, rep_ref, split_ref):
        flat = w_ref[:, ATT:]
        turned = flat.astype(f32).T
        rep_ref[...] = turned[:16]
        low = turned[:24].astype(b16)
        step = VCOL // 3
        for i in range(3):
            rows = D // 3
            mask = spread_mask(i * rows, rows, i * step, step)
            spread = dot(low[:, i * rows : (i + 1) * rows], mask)
            phase = lax.rem(lax.broadcasted_iota(jnp.int32, (1, step), 1), 3)
            for layer in range(LAYERS):
                at = 6 * LAYERS + 3 * layer
                value = jnp.where(
                    phase == 0,
                    spread[at : at + 1],
                    jnp.where(phase == 1, spread[at + 1 : at + 2], spread[at + 2 : at + 3]),
                )
                split_ref[layer : layer + 1, i * step : (i + 1) * step] = value

    return call(
        body,
        [((16, D), f32), ((8, VCOL), f32)],
        [VM],
        moved=D * LANES * 2,
        flops=24 * D * VCOL,
    )(gathered)


def gelu_parts(inner):
    cdf = 0.5 * (1.0 + lax.erf(inner * (0.5**0.5)))
    dens = jnp.exp(-0.5 * inner * inner) * 0.3989422804014327
    return inner * cdf, cdf + inner * dens


def attend(h_low, layer, w_ref, split_ref, seg_ref, part_ref, qkv_ref, probs_ref, ctx_ref):
    mixed = dot(h_low, w_ref[:, :QKV])
    qkv_ref[:, :HD] = (mixed[:, :HD] + split_ref[layer : layer + 1, :HD]).astype(b16)
    qkv_ref[:, HD : 2 * HD] = mixed[:, HD : 2 * HD].astype(b16)
    qkv_ref[:, 2 * HD :] = (
        mixed[:, 2 * HD :] + split_ref[layer : layer + 1, HD : 2 * HD]
    ).astype(b16)
    seg = jnp.broadcast_to(seg_ref[...].astype(f32), (SEQ, SEQ))
    same = seg == seg.T
    low_half = lax.broadcasted_iota(jnp.int32, (1, LANES), 1) < HEAD_DIM
    for pair in range(HD // LANES):
        at = pair * LANES
        query = qkv_ref[:, at : at + LANES].astype(f32) * HEAD_DIM ** (-0.5)
        keys = qkv_ref[:, HD + at : HD + at + LANES]
        values = qkv_ref[:, 2 * HD + at : 2 * HD + at + LANES].astype(f32)
        total = jnp.zeros((SEQ, LANES), f32)
        for half in range(2):
            mine = low_half if half == 0 else ~low_half
            scores = dot(jnp.where(mine, query, 0.0).astype(b16), keys, contract_last)
            scores = jnp.where(same, scores, -1000000000.0)
            raised = jnp.exp(scores - jnp.max(scores, axis=-1, keepdims=True))
            probs = (raised * (1.0 / jnp.sum(raised, axis=-1, keepdims=True))).astype(b16)
            probs_ref[2 * pair + half] = probs
            total = total + dot(probs, jnp.where(mine, values, 0.0).astype(b16))
        ctx_ref[:, at : at + LANES] = total.astype(b16)
    part_ref[...] = dot(ctx_ref[...], w_ref[:, QKV:ATT], contract_last).astype(b16)


ATT_FLOPS = 2 * SEQ * D * ATT + 4 * SEQ * SEQ * HD * 2
FFN_FLOPS = 2 * SEQ * D * 2 * FFT


ATT_OUTS = [((MICRO, SEQ, QKV), b16), ((MICRO, HD // HEAD_DIM, SEQ, SEQ), b16), ((MICRO, SEQ, HD), b16)]


def attention_first(block_in, segments, split, matrix):
    def body(h_ref, seg_ref, split_ref, w_ref, part_ref, qkv_ref, probs_ref, ctx_ref):
        for m in range(MICRO):
            views = [r.at[m] for r in (part_ref, qkv_ref, probs_ref, ctx_ref)]
            attend(h_ref[m], 0, w_ref, split_ref, seg_ref[m], *views)

    return call(
        body,
        [((MICRO, SEQ, D), b16)] + ATT_OUTS,
        [VM] * 4,
        flops=2 * ATT_FLOPS,
        moved=12 << 20,
        limit=16,
    )(block_in, segments, split, matrix)


def attention_next(micro, layer, normed, part_own, part_other, rep, segments, split, matrix):
    base = 6 * (layer - 1)

    def body(n_ref, own_ref, other_ref, rep_ref, seg_ref, split_ref, w_ref, *refs):
        part_ref, qkv_ref, probs_ref, ctx_ref, n2_ref, s2_ref, low_ref = refs
        first = n_ref[micro] * rep_ref[base + 1 : base + 2] + rep_ref[base + 2 : base + 3]
        added = own_ref[...].astype(f32) + other_ref[...].astype(f32)
        n2, s2 = norm_rows(first + added + rep_ref[base + 3 : base + 4])
        n2_ref[...] = n2
        s2_ref[...] = s2
        low = (n2 * rep_ref[base + 4 : base + 5] + rep_ref[base + 5 : base + 6]).astype(b16)
        low_ref[...] = low
        attend(
            low, layer, w_ref, split_ref, seg_ref[micro], part_ref, qkv_ref, probs_ref, ctx_ref
        )

    return call(
        body,
        [((SEQ, D), b16)]
        + [(shape[1:], kind) for shape, kind in ATT_OUTS]
        + [((SEQ, D), f32), ((SEQ, 1), f32), ((SEQ, D), b16)],
        [VM] * 7,
        flops=ATT_FLOPS,
        moved=8 << 20,
    )(normed, part_own, part_other, rep, segments, split, matrix)


def feed_step(hidden_in, added, layer, rep_ref, split_ref, w_ref, outs):
    base = 6 * layer
    part_ref, n1_ref, s1_ref, low_ref, act_ref, slope_ref = outs
    n1, s1 = norm_rows(hidden_in + added + rep_ref[base : base + 1])
    n1_ref[...] = n1
    s1_ref[...] = s1
    low_ref[...] = (n1 * rep_ref[base + 1 : base + 2] + rep_ref[base + 2 : base + 3]).astype(b16)
    step = 512
    for at in range(0, FFT, step):
        inner = (
            dot(low_ref[...], w_ref[:, at : at + step])
            + split_ref[layer : layer + 1, 2 * HD + at : 2 * HD + at + step]
        )
        active, slope = gelu_parts(inner)
        act_ref[:, at : at + step] = active.astype(b16)
        slope_ref[:, at : at + step] = slope.astype(b16)
    part_ref[...] = dot(act_ref[...], w_ref[:, FFT:], contract_last).astype(b16)


FEED_OUTS = [
    ((SEQ, D), b16),
    ((SEQ, D), f32),
    ((SEQ, 1), f32),
    ((SEQ, D), b16),
    ((SEQ, FFT), b16),
    ((SEQ, FFT), b16),
]


def feed_first(hidden, part_own, part_other, rep, split, matrix):
    def body(h_ref, own_ref, other_ref, rep_ref, split_ref, w_ref, *refs):
        parts, outs = refs[:MICRO], refs[MICRO:]
        for m in range(MICRO):
            added = own_ref[m].astype(f32) + other_ref[m].astype(f32)
            views = [parts[m]] + [r.at[m] for r in outs]
            feed_step(h_ref[m].astype(f32), added, 0, rep_ref, split_ref, w_ref, views)

    return call(
        body,
        [((SEQ, D), b16)] * MICRO + [((MICRO,) + shape, kind) for shape, kind in FEED_OUTS[1:]],
        [VM] * 6,
        flops=2 * FFN_FLOPS,
        moved=20 << 20,
        limit=22,
    )(hidden, part_own, part_other, rep, split, matrix)


def feed_forward(micro, layer, hidden, part_own, part_other, rep, split, matrix):
    base = 6 * layer

    def body(h_ref, own_ref, other_ref, rep_ref, split_ref, w_ref, *outs):
        hidden_in = h_ref[...] * rep_ref[base - 2 : base - 1] + rep_ref[base - 1 : base]
        added = own_ref[...].astype(f32) + other_ref[...].astype(f32)
        feed_step(hidden_in, added, layer, rep_ref, split_ref, w_ref, outs)

    return call(
        body,
        FEED_OUTS,
        [VM] * 6,
        flops=FFN_FLOPS,
        moved=10 << 20,
    )(hidden, part_own, part_other, rep, split, matrix)


def view(ref, micro):
    return ref.at[micro] if ref.shape[0] == MICRO else ref


def feed_back_tail(grad, n2, s2, layer, rep_ref, slope_ref, w_ref, outs):
    base = 6 * layer
    part_ref, res_ref, dffn_ref, din_ref, vec_ref = outs
    back, gain, shift = norm_back(grad, n2, s2, rep_ref[base + 4 : base + 5])
    res_ref[...] = back
    dffn_ref[...] = back.astype(b16)
    vec_ref[...] = jnp.zeros_like(vec_ref)
    vec_ref[0:1] = jnp.sum(back, axis=0, keepdims=True)
    vec_ref[1:2] = gain
    vec_ref[2:3] = shift
    step = 384
    for at in range(0, FFT, step):
        grad_act = dot(dffn_ref[...], w_ref[:, FFT + at : FFT + at + step])
        grad_in = (slope_ref[:, at : at + step].astype(f32) * grad_act).astype(b16)
        din_ref[:, at : at + step] = grad_in
        row, lane = 3 + at // D, at % D
        vec_ref[row : row + 1, lane : lane + step] = jnp.sum(
            grad_in.astype(f32), axis=0, keepdims=True
        )
    part_ref[...] = dot(din_ref[...], w_ref[:, :FFT], contract_last).astype(b16)


BACK_OUTS = [
    ((SEQ, D), b16),
    ((SEQ, D), f32),
    ((SEQ, D), b16),
    ((SEQ, FFT), b16),
    ((8, D), f32),
]


def feed_back_top(micro, layer, out_grad, n1, part_own, part_other, rep, slope, matrix):
    base = 6 * layer

    def body(g_ref, n_ref, own_ref, other_ref, rep_ref, slope_ref, w_ref, *refs):
        out_ref = refs[5]
        first = n_ref[...] * rep_ref[base + 1 : base + 2] + rep_ref[base + 2 : base + 3]
        added = own_ref[...].astype(f32) + other_ref[...].astype(f32)
        n2, s2 = norm_rows(first + added + rep_ref[base + 3 : base + 4])
        out_ref[...] = (n2 * rep_ref[base + 4 : base + 5] + rep_ref[base + 5 : base + 6]).astype(b16)
        feed_back_tail(
            g_ref[micro].astype(f32), n2, s2, layer, rep_ref, slope_ref, w_ref, refs[:5]
        )

    return call(
        body,
        BACK_OUTS + [((SEQ, D), b16)],
        [VM] * 6 + [VM],
        flops=FFN_FLOPS,
        moved=11 << 20,
    )(out_grad, n1, part_own, part_other, rep, slope, matrix)


def feed_back(micro, layer, mid, part_own, part_other, n2, s2, rep, slope, matrix):
    def body(mid_ref, own_ref, other_ref, n2_ref, s2_ref, rep_ref, slope_ref, w_ref, *refs):
        added = own_ref[...].astype(f32) + other_ref[...].astype(f32)
        feed_back_tail(
            mid_ref[...] + added,
            view(n2_ref, micro)[...],
            view(s2_ref, micro)[...],
            layer,
            rep_ref,
            view(slope_ref, micro),
            w_ref,
            refs[:5],
        )

    return call(
        body,
        BACK_OUTS,
        [VM] * 7 + [VM],
        flops=FFN_FLOPS,
        moved=11 << 20,
    )(mid, part_own, part_other, n2, s2, rep, slope, matrix)


def attention_back(micro, layer, res, part_own, part_other, n1, s1, rep, qkv, probs, ctx, matrix):
    base = 6 * layer

    def body(
        res_ref, own_ref, other_ref, n1_ref, s1_ref, rep_ref, qkv_ref, probs_ref, ctx_ref, w_ref, *refs
    ):
        part_ref, mid_ref, datt_ref, dqkv_ref, vec_ref = refs
        n1_ref, s1_ref, qkv_ref, probs_ref, ctx_ref = (
            view(r, micro) for r in (n1_ref, s1_ref, qkv_ref, probs_ref, ctx_ref)
        )
        grad = res_ref[...] + (own_ref[...].astype(f32) + other_ref[...].astype(f32))
        back, gain, shift = norm_back(grad, n1_ref[...], s1_ref[...], rep_ref[base + 1 : base + 2])
        mid_ref[...] = back
        datt_ref[...] = back.astype(b16)
        vec_ref[...] = jnp.zeros_like(vec_ref)
        vec_ref[0:1] = jnp.sum(back, axis=0, keepdims=True)
        vec_ref[1:2] = gain
        vec_ref[2:3] = shift
        dctx = dot(datt_ref[...], w_ref[:, QKV:ATT]).astype(b16).astype(f32)
        low_half = lax.broadcasted_iota(jnp.int32, (1, LANES), 1) < HEAD_DIM
        factor = HEAD_DIM ** (-0.5)
        for pair in range(HD // LANES):
            at = pair * LANES
            query = qkv_ref[:, at : at + LANES].astype(f32) * factor
            keys = qkv_ref[:, HD + at : HD + at + LANES].astype(f32) * factor
            values = qkv_ref[:, 2 * HD + at : 2 * HD + at + LANES]
            dc = dctx[:, at : at + LANES]
            weighed = dc * ctx_ref[:, at : at + LANES].astype(f32)
            dq = jnp.zeros((SEQ, LANES), f32)
            dk = jnp.zeros((SEQ, LANES), f32)
            dv = jnp.zeros((SEQ, LANES), f32)
            for half in range(2):
                mine = low_half if half == 0 else ~low_half
                dcm = jnp.where(mine, dc, 0.0).astype(b16)
                delta = jnp.sum(jnp.where(mine, weighed, 0.0), axis=-1, keepdims=True)
                probs = probs_ref[2 * pair + half]
                dprobs = dot(dcm, values, contract_last)
                dscores = (probs.astype(f32) * (dprobs - delta)).astype(b16)
                dq = dq + dot(dscores, jnp.where(mine, keys, 0.0).astype(b16))
                dk = dk + dot(dscores, jnp.where(mine, query, 0.0).astype(b16), contract_first)
                dv = dv + dot(probs, dcm, contract_first)
            dqkv_ref[:, at : at + LANES] = dq.astype(b16)
            dqkv_ref[:, HD + at : HD + at + LANES] = dk.astype(b16)
            dqkv_ref[:, 2 * HD + at : 2 * HD + at + LANES] = dv.astype(b16)
        vec_ref[3:4, :HD] = jnp.sum(dqkv_ref[:, :HD].astype(f32), axis=0, keepdims=True)
        vec_ref[3:4, HD:] = jnp.sum(dqkv_ref[:, 2 * HD :].astype(f32), axis=0, keepdims=True)
        part_ref[...] = dot(dqkv_ref[...], w_ref[:, :QKV], contract_last).astype(b16)

    return call(
        body,
        [
            ((SEQ, D), b16),
            ((SEQ, D), f32),
            ((SEQ, D), b16),
            ((SEQ, QKV), b16),
            ((8, D), f32),
        ],
        [VM] * 9 + [VM],
        flops=2 * ATT_FLOPS,
        moved=9 << 20,
    )(res, part_own, part_other, n1, s1, rep, qkv, probs, ctx, matrix)


def finish_input(mids, owns, others):
    def body(*refs):
        for micro in range(MICRO):
            m, a, b = refs[3 * micro : 3 * micro + 3]
            refs[-1][micro] = m[...] + (a[...].astype(f32) + b[...].astype(f32))

    args = []
    for micro in range(MICRO):
        args += [mids[micro], owns[micro], others[micro]]
    return call(body, [((MICRO, SEQ, D), f32)], [VM] * len(args), moved=7 << 20)(*args)[0]


def store_slots(product_ref, outs, at, width):
    if len(outs) == 1:
        outs[0][:, at : at + width] = product_ref[:, :width].astype(b16)
        return
    ring, rows = outs[0].shape[1], outs[0].shape[2]
    z, x, c = places(ring)
    for other in range(2):
        for xo in range(2):
            for k in range(ring):
                zz = lax.rem(z + k, ring)
                xx = lax.rem(x + xo, 2)
                cc = lax.rem(c + other, 2)
                row = pl.multiple_of(((zz * 2 + xx) * 2 + cc) * rows, 16)
                outs[other][xo, k, :, at : at + width] = product_ref[
                    pl.ds(row, rows), :width
                ].astype(b16)


def grad_outs(ndp, pieced, cols):
    rows = D // ndp
    if pieced:
        return [((2, ndp // 4, rows, cols), b16)] * 2
    return [((D, cols), b16)]


def matrix_gradient(sets, pieced, ndp, vectors=None):
    widths = [s[2] for s in sets]
    total = sum(widths) + (LANES if vectors is not None else 0)
    outs = grad_outs(ndp, pieced, total)
    args, specs = [], []
    for left, right, _ in sets:
        for micro in range(MICRO):
            specs.append(VM)
            args.append(left[micro])
        for micro in range(MICRO):
            args.append(right[micro])
            specs.append(VM)
    plain = len(args)
    if vectors is not None:
        args += vectors
        specs += [VM] * len(vectors)
    n_in = len(args)
    step = 384

    def body(*refs):
        out_refs = refs[n_in : n_in + len(outs)]
        prod_ref = refs[n_in + len(outs)]
        at = 0
        for index, width in enumerate(widths):
            l0, l1, r0, r1 = refs[4 * index : 4 * index + 4]
            left = [r[m] if len(r.shape) == 3 else r[...] for m, r in enumerate((l0, l1))]
            r0, r1 = (r.at[m] if len(r.shape) == 3 else r for m, r in enumerate((r0, r1)))
            for col in range(0, width, step):
                prod_ref[...] = dot(left[0], r0[:, col : col + step], contract_first) + dot(
                    left[1], r1[:, col : col + step], contract_first
                )
                store_slots(prod_ref, out_refs, at, step)
                at += step
        if vectors is not None:
            pack_vectors(refs[plain:n_in], prod_ref)
            store_slots(prod_ref, out_refs, at, LANES)

    moved = sum(a.size * 2 for a in args[:plain]) + D * total * 2
    return call(
        body,
        outs,
        specs,
        [pltpu.VMEM((D, step), f32)],
        flops=2 * MICRO * SEQ * D * total,
        moved=moved,
    )(*args)


def pack_vectors(vec_refs, prod_ref):
    sums = []
    for layer in range(LAYERS):
        a0, a1, b0, b1 = vec_refs[4 * layer : 4 * layer + 4]
        sums.append((a0[...] + a1[...], b0[...] + b1[...]))
    rows = []
    for att, ffn in sums:
        rows += [att[0:1], att[1:2], att[2:3], ffn[0:1], ffn[1:2], ffn[2:3]]
    rows.append(jnp.zeros((4, D), f32))
    turned = jnp.concatenate(rows, axis=0)
    turned = jnp.concatenate([turned, jnp.zeros((LANES - 16, D), f32)], axis=0).T
    step = VCOL // 3
    phase = lax.rem(lax.broadcasted_iota(jnp.int32, (1, step), 1), 3)
    lane = lax.broadcasted_iota(jnp.int32, (1, LANES), 1)
    for i in range(3):
        picked = []
        for att, ffn in sums:
            line = (att[3:4], ffn[3:4], ffn[4:5])[i]
            for j in range(3):
                picked.append(jnp.where(phase == j, line, 0.0))
        picked = jnp.concatenate(
            [jnp.zeros((12, step), f32)] + picked + [jnp.zeros((LANES - 18, step), f32)], axis=0
        ).astype(b16)
        n_rows = D // 3
        mask = spread_mask(i * n_rows, n_rows, i * step, step)
        part = dot(mask, picked, contract_last)
        keep = turned[i * n_rows : (i + 1) * n_rows]
        prod_ref[i * n_rows : (i + 1) * n_rows, :LANES] = jnp.where(lane < 12, keep, part)


def meet(own, met, places):
    lo, hi = places[0], places[-1] + 1
    return (own[1, lo:hi].astype(f32) + met[1, lo:hi].astype(f32)).astype(b16)


def pass_on(own, met, got, places):
    lo, hi = places[0], places[-1] + 1
    total = own[0, lo:hi].astype(f32) + met[0, lo:hi].astype(f32) + got.astype(f32)
    return [total[i].astype(b16) for i in range(hi - lo)]


def pass_both(own, met, k, received=None):
    total = own[:, k].astype(f32) + met[:, k].astype(f32)
    if received is not None:
        total = total + received.astype(f32)
    return total.astype(b16)


def close(own, met, parts, vectors=False):
    _, _, rows, cols = own.shape
    mats = cols - LANES if vectors else cols
    parts = [p if isinstance(p, tuple) else (p, None) for p in parts]
    n = len(parts)

    def body(own_ref, met_ref, *refs):
        out_ref, sq_ref = refs[n:]
        total = jnp.zeros((rows, LANES), f32)
        for at in range(0, cols, LANES):
            s = slice(at, at + LANES)
            value = own_ref[0, 0, :, s].astype(f32) + met_ref[0, 0, :, s].astype(f32)
            for (_, index), ref in zip(parts, refs[:n]):
                value = value + (ref[:, s] if index is None else ref[index, :, s]).astype(f32)
            out_ref[:, s] = value
            square = value * value
            if at >= mats:
                lane = lax.broadcasted_iota(jnp.int32, (rows, LANES), 1)
                twice = (lane < 6 * LAYERS) & (lax.axis_index("tensor") != 0)
                square = jnp.where(twice, 0.0, square)
            total = total + square
        part = total[:8]
        for i in range(8, rows, 8):
            part = part + total[i : i + 8]
        sq_ref[...] = part

    return call(
        body,
        [((rows, cols), f32), ((8, LANES), f32)],
        [VM] * (2 + n),
        moved=rows * cols * 14,
    )(own, met, *[p[0] for p in parts])


def adamw(value, first, second, grad, rate, decay):
    first = 0.5 * first + 0.5 * grad
    second = 0.5 * second + 0.5 * grad * grad
    correct = 1.0 - 0.5**STEP
    direction = first / correct / (jnp.sqrt(second / correct) + 1e-08)
    return (value - rate * (direction + decay * value), first, second)


def clip_factor(squares):
    norm = jnp.sqrt(jnp.sum(squares, keepdims=True))
    return norm, jnp.minimum(1.0, clip_limit / (norm + 1e-06))


def ready(tiled, first, second):
    def body(w_ref, m_ref, v_ref, w_out, m_out, v_out):
        w_out[...] = w_ref[...] * (1.0 - weight_rate * weight_decay)
        m_out[...] = 0.5 * m_ref[...]
        v_out[...] = 0.5 * v_ref[...]

    return call(body, [(tiled.shape, f32)] * 3, [VM] * 3, moved=24 * tiled.size)(tiled, first, second)


def stepped(decayed, half_first, half_second, grad, rate):
    first = half_first + 0.5 * grad
    second = half_second + 0.5 * grad * grad
    correct = 1.0 - 0.5**STEP
    direction = first / (correct * jnp.sqrt(second * (1.0 / correct)) + correct * 1e-08)
    return decayed - rate * direction, first, second


def update_vectors(block, squares, reps, splits):
    rows = block.shape[0]
    per = splits[0].shape[2]

    def body(b_ref, q_ref, rw, rm, rv, sw, sm, sv, norm_ref, rwo, rmo, rvo, rlo, go, swo, smo, svo, slo):
        norm, scale = clip_factor(q_ref[...])
        norm_ref[...] = norm
        turned = jnp.concatenate([b_ref[...], jnp.zeros((LANES - rows, LANES), f32)], axis=0).T
        for layer in range(LAYERS):
            at = slice(layer, layer + 1)
            for kind in range(6):
                grad = turned[6 * layer + kind : 6 * layer + kind + 1, :rows] * scale
                new = adamw(rw[kind, at], rm[kind, at], rv[kind, at], grad, vector_rate, 0.0)
                rwo[kind, at], rmo[kind, at], rvo[kind, at] = new
                rlo[kind, at] = new[0].astype(b16)
                if kind == 0:
                    go[at] = grad
        row = lax.broadcasted_iota(jnp.int32, (rows, per), 0)
        col = lax.broadcasted_iota(jnp.int32, (rows, per), 1)
        gap = col - 3 * row
        mask = jnp.where((gap >= 0) & (gap < 3), 1.0, 0.0)
        wide = lax.dot_general(
            turned[6 * LAYERS : 6 * LAYERS + 8, :rows],
            mask,
            (((1,), (0,)), ((), ())),
            preferred_element_type=f32,
            precision=lax.Precision.HIGHEST,
        )
        phase = lax.rem(lax.broadcasted_iota(jnp.int32, (1, per), 1), 3)
        for layer in range(LAYERS):
            one, two, three = (wide[3 * layer + j : 3 * layer + j + 1] for j in range(3))
            grad = jnp.where(phase == 0, one, jnp.where(phase == 1, two, three)) * scale
            new = adamw(sw[layer], sm[layer], sv[layer], grad, vector_rate, 0.0)
            swo[layer], smo[layer], svo[layer] = new
            slo[layer] = new[0].astype(b16)

    rep, split = reps[0].shape, splits[0].shape
    return call(
        body,
        [((1, 1), f32)]
        + [(rep, f32)] * 3
        + [(rep, b16), ((LAYERS, rows), f32)]
        + [(split, f32)] * 3
        + [(split, b16)],
        [VM] * 8,
        moved=1 << 18,
    )(block, squares, *reps, *splits)


def update_matrices(decayed, first, second, grads, squares):
    rows = grads[0].shape[0]
    tiled = decayed
    step = 24 if rows % 24 == 0 else rows
    n_steps = rows // step
    block = (1, step * TILES, LANES)

    def body(f_ref, w_ref, m_ref, v_ref, a0, f0, a1, f1, nw, nm, nv, nl):
        scale = clip_factor(f_ref[...])[1]

        def columns(a_ref, g_ref):
            for c in range(TILES):
                lo = c * LANES
                if lo < ATT:
                    grad = a_ref[:, lo : lo + LANES]
                else:
                    grad = g_ref[:, lo - ATT : lo - ATT + LANES]
                where = (0, pl.ds(c, step, stride=TILES), slice(None))
                new = stepped(w_ref[where], m_ref[where], v_ref[where], grad * scale, weight_rate)
                nw[where], nm[where], nv[where] = new

        for layer, pair in enumerate(((a0, f0), (a1, f1))):
            pl.when(pl.program_id(0) == layer)(partial(columns, *pair))
        nl[...] = nw[...].astype(b16)

    big = pl.BlockSpec(block, lambda l, i: (l, i, 0))
    shape = tiled.shape
    return pl.pallas_call(
        body,
        grid=(LAYERS, n_steps),
        out_shape=[jax.ShapeDtypeStruct(shape, f32)] * 3 + [jax.ShapeDtypeStruct(shape, b16)],
        in_specs=[pl.BlockSpec((8, LANES), lambda l, i: (0, 0)), big, big, big]
        + [pl.BlockSpec((step, g.shape[1]), lambda l, i: (i, 0)) for g in grads],
        out_specs=[big] * 4,
        compiler_params=pltpu.CompilerParams(vmem_limit_bytes=13 * 1024 * 1024),
        cost_estimate=pl.CostEstimate(
            flops=20 * tiled.size, bytes_accessed=30 * tiled.size, transcendentals=tiled.size
        ),
    )(squares, tiled, first, second, *grads)


def sum_everywhere(value):
    ndp = lax.axis_size("dp")
    if ndp & (ndp - 1) or ndp < 4:
        return lax.psum(value, ("dp", "tensor"))

    def level(a, first, second):
        one, two, both = ppermute_bits(a, first), ppermute_bits(a, second), ppermute_bits(a, first | second)
        return (a + one) + (two + both)

    value = value + ppermute_bits(value, 2)
    value = level(value, 4, 1)
    bit = 8
    while bit < 2 * ndp:
        if 2 * bit < 2 * ndp:
            value = level(value, bit, 2 * bit)
        else:
            value = value + ppermute_bits(value, bit)
        bit *= 4
    return value


def ppermute_bits(value, bits):
    n = 2 * lax.axis_size("dp")
    return lax.ppermute(value, ("dp", "tensor"), [(i, i ^ bits) for i in range(n)])


def per_device(
    block_in,
    out_grad,
    segments,
    weights,
    weights_first,
    weights_second,
    split_vectors,
    split_first,
    split_second,
    rep_vectors,
    rep_first,
    rep_second,
):
    ndp = lax.axis_size("dp")
    rows = D // ndp
    per = split_vectors.shape[2]
    pieced = ndp == 16 and rows % 16 == 0
    shard_shape = weights.shape
    tiled_shape = (LAYERS, -1, LANES)
    masters = [a.reshape(tiled_shape) for a in (weights, weights_first, weights_second)]
    weights_tiled = masters[0]
    rep_flat = rep_vectors.reshape(LAYERS * 6, -1)
    split_flat = split_vectors.reshape(LAYERS, per)
    both = range(MICRO)
    seg = segments.reshape(MICRO, 1, SEQ)
    if pieced:
        a0, f0, l1, every = prep(weights_tiled, rep_flat, split_flat)
        across = partial(move, kind="x")
        third = slice(COLS + LANES, COLS + LANES + ATT)
        fourth = slice(COLS + LANES + ATT, None)

        def finish(slots, cols):
            mine = [stack(half, rows, cols) for half in (slots[:4], slots[4:])]
            return settle(mine, [move(a, "core") for a in mine])

        def cut(array, cols):
            return (array, (slice(None), cols))

        x0 = across(every)
        a0_r1, a0_r2, a0_r3, f0 = tie(move(a0, 1), move(a0, 2), move(a0, 3), f0)
        a0_x = across(stack([a0_r1, a0_r2, a0_r3], rows, ATT + LANES))
        f0_r1, f0_r3 = move(f0, 1), move(f0, 3)
        near = stack([a0, a0_r1, a0_r2, a0_r3], rows, ATT + LANES)
        mine0 = stack(
            [cut(x0, slice(0, ATT + LANES)), (a0_x, 0), (a0_x, 1), (a0_x, 2)], rows, ATT + LANES
        )
        mine0, f0_r1, l1 = tie(mine0, f0_r1, l1)
        watt0 = settle([near, mine0], [move(near, "core"), move(mine0, "core")])
        f0_x13 = across(stack([f0_r1, f0_r3], rows, 2 * FFT))
        f0_r2 = move(f0_r1, 1)
        l1_r1, l1_r3 = move(l1, 1), move(l1, 3)
        f0_x2 = across(f0_r2)
    else:
        low = weights.astype(b16).reshape(LAYERS, rows, COLS)
        block = jnp.concatenate(
            [
                rep_flat.T,
                split_flat.reshape(LAYERS, rows, 3).transpose(1, 0, 2).reshape(rows, 6),
                jnp.zeros((rows, LANES - 18), f32),
            ],
            axis=1,
        ).astype(b16)
        gather = partial(lax.all_gather, axis_name="dp", axis=0, tiled=True)
        watt0 = gather(jnp.concatenate([low[0, :, :ATT], block], axis=1))
        watt1 = gather(low[1, :, :ATT])
        wffn0, wffn1 = (gather(low[layer, :, ATT:]) for layer in range(LAYERS))
    rep, split = unpack(watt0)

    done, qkv0, probs0, ctx0 = attention_first(block_in, seg, split, watt0)
    met = exchange(done)
    if pieced:
        head, tail = slice(0, ATT), slice(ATT, None)
        a1_r2 = move(stack([cut(l1_r1, head)], rows, ATT), 1)
        f0_x13, f0_x2, l1_r1, l1_r3, a1_r2, met = tie(f0_x13, f0_x2, l1_r1, l1_r3, a1_r2, met)
        a1_x = across(stack([cut(l1_r1, head), (a1_r2, 0), cut(l1_r3, head)], rows, ATT))
        f1_r2 = move(stack([cut(l1_r1, tail)], rows, 2 * FFT), 1)
        wffn0 = finish(
            [f0, f0_r1, f0_r2, f0_r3]
            + [cut(x0, slice(ATT + LANES, COLS + LANES)), (f0_x13, 0), f0_x2, (f0_x13, 1)],
            2 * FFT,
        )
    *done, n1_0, s1_0, low1_0, act0, slope0 = feed_first(block_in, done, met, rep, split, wffn0)
    if pieced:
        a1_x, f1_r2, *done = tie(a1_x, f1_r2, *done)
        f1_x = across(stack([cut(l1_r1, tail), (f1_r2, 0), cut(l1_r3, tail)], rows, 2 * FFT))
        watt1 = finish(
            [cut(l1, head), cut(l1_r1, head), (a1_r2, 0), cut(l1_r3, head), cut(x0, third)]
            + [(a1_x, k) for k in range(3)],
            ATT,
        )
    met = [exchange(a) for a in done]
    out = [
        attention_next(m, 1, n1_0, done[m], met[m], rep, seg, split, watt1) for m in both
    ]
    done = [o[0] for o in out]
    qkv1, probs1, ctx1, n2_0, s2_0, low_h1 = ([o[i] for o in out] for i in range(1, 7))
    if pieced:
        wffn1 = finish(
            [cut(l1, tail), cut(l1_r1, tail), (f1_r2, 0), cut(l1_r3, tail), cut(x0, fourth)]
            + [(f1_x, k) for k in range(3)],
            2 * FFT,
        )
    met = [exchange(a) for a in done]
    out = [feed_forward(m, 1, n2_0[m], done[m], met[m], rep, split, wffn1) for m in both]
    n1_1, s1_1, low1_1, act1, slope1 = ([o[i] for o in out] for i in range(1, 6))
    met = [exchange(o[0]) for o in out]

    out = [
        feed_back_top(m, 1, out_grad, n1_1[m], out[m][0], met[m], rep, slope1[m], wffn1)
        for m in both
    ]
    res, dffn, din, vec_f1 = ([o[i] for o in out] for i in range(1, 5))
    block_out = jnp.stack([o[5] for o in out])
    done = [o[0] for o in out]
    met = [exchange(o[0]) for o in out]
    plan = {"w_f1": 0, "f1_3": 1, "w_a1": 2, "f1_2": 3, "a1_s": 3, "w_f0": 4, "f1_1": 5, "a1_t": 6, "f0_s": 5}
    held, ends = {}, []

    def make(name):
        gate = ends[-1:] if 1 else []
        if name == "w_f1":
            g = matrix_gradient([(low1_1, din_1, FFT), (dffn_1, act1, FFT)], pieced, ndp)
        elif name == "w_a1":
            g = matrix_gradient(
                [(low_h1, dqkv_1, QKV), (datt_1, ctx1, HD)], pieced, ndp
            )
        elif name == "w_f0":
            g = matrix_gradient(
                [([low1_0] * 2, din_0, FFT), (dffn_0, [act0] * 2, FFT)], pieced, ndp
            )
        elif not pieced:
            return []
        if name.startswith("w_"):
            held[name[2:]] = g if not pieced else (g[0], move(g[1], "core"))
            return [g[0]]
        own, across_core = held[name[:2]]
        if name[:3] == "f1_":
            k = int(name[3])
            if k == 3:
                total = pass_both(own, after(across_core, *gate), k)
            else:
                total = pass_both(own, across_core, k, after(held["f1_rec"], *gate))
            held["f1_rec"] = move(total, 1)
            return [total]
        if name == "a1_t":
            parts = pass_on(own, across_core, after(held["a1_got"], *gate)[1:], (1, 2, 3))
            held["a1_r"] = [move(t, k + 1) for k, t in enumerate(parts)]
            return [parts[2]]
        places = (0, 1, 2, 3) if name == "a1_s" else (2, 3)
        total = meet(own, after(across_core, *gate), places)
        held[name[:2] + "_got"] = move(total, "x")
        return [total]

    def before(stage, value):
        needed = [a for name in plan if plan[name] == stage for a in make(name)]
        return after(value, *needed) if needed else value

    din_1, dffn_1 = din, dffn
    out = []
    for m in both:
        value = before(m, res[m])
        out.append(
            attention_back(
                m, 1, value, done[m], met[m], n1_1[m], s1_1[m], rep, qkv1[m], probs1[m], ctx1[m], watt1
            )
        )
        ends.append(out[m][0])
    mid, datt_1, dqkv_1, vec_a1 = ([o[i] for o in out] for i in range(1, 5))
    done = [o[0] for o in out]
    met = [exchange(o[0]) for o in out]
    out = []
    for m in both:
        value = before(2 + m, mid[m])
        out.append(feed_back(m, 0, value, done[m], met[m], n2_0[m], s2_0[m], rep, slope0, wffn0))
        ends.append(out[m][0])
    res, dffn_0, din_0, vec_f0 = ([o[i] for o in out] for i in range(1, 5))
    done = [o[0] for o in out]
    met = [exchange(o[0]) for o in out]
    out = []
    for m in both:
        value = before(4 + m, res[m])
        out.append(
            attention_back(
                m, 0, value, done[m], met[m], n1_0, s1_0, rep, qkv0, probs0, ctx0, watt0
            )
        )
        ends.append(out[m][0])
    mid, datt, dqkv, vec_a0 = ([o[i] for o in out] for i in range(1, 5))
    done = [o[0] for o in out]
    met = [exchange(o[0]) for o in out]
    dqkv[0] = before(6, dqkv[0])
    g_a0 = matrix_gradient(
        [([block_in] * MICRO, dqkv, QKV), (datt, [ctx0] * 2, HD)],
        pieced,
        ndp,
        vectors=vec_a0 + vec_f0 + vec_a1 + vec_f1,
    )
    ends.append(g_a0[0])
    before(7, g_a0[0])
    if pieced:
        (f1_own, f1_met), (a1_own, a1_met), (f0_own, f0_met) = (held[c] for c in ("f1", "a1", "f0"))
        f1_rec, a1_got, a1_r, f0_got_hi = (held[c] for c in ("f1_rec", "a1_got", "a1_r", "f0_got"))
    else:
        g_f1, g_a1, g_f0 = (held[c] for c in ("f1", "a1", "f0"))
    if pieced:
        masters = ready(*(after(a, g_a0[0]) for a in masters))
        input_grad = finish_input(mid, done, met)
        a0_own, a0_met = g_a0[0], move(g_a0[1], "core")
        a0_got = across(meet(a0_own, a0_met, (0, 1, 2, 3)))
        f1_last = pass_both(f1_own, f1_met, 0, f1_rec)
        f1_got = across(f1_last[1])
        f0_t2, f0_t3 = pass_on(f0_own, f0_met, f0_got_hi, (2, 3))
        f0_r3, f0_r2 = move(f0_t3, 3), move(f0_t2, 2)
        a0_got, f0_r3, f0_r2, *a1_r = tie(a0_got, f0_r3, f0_r2, *a1_r)
        f0_got_lo = across(meet(f0_own, f0_met, (0, 1)))
        a0_t = pass_on(a0_own, a0_met, a0_got[1:], (1, 2, 3))
        a0_r = [move(t, k + 1) for k, t in enumerate(a0_t)]
        grad_a1, sq_a1 = close(a1_own, a1_met, [(a1_got, 0)] + a1_r)
        grad_f1, sq_f1 = close(f1_own, f1_met, [f1_got, (f1_rec, 0)])
        f0_got_lo, grad_f1, grad_a1, block_out, input_grad, *rest = tie(
            f0_got_lo, grad_f1, grad_a1, block_out, input_grad, *a0_r, *masters
        )
        a0_r, masters = rest[:3], rest[3:]
        f0_r1 = move(pass_on(f0_own, f0_met, f0_got_lo[1:], (1,))[0], 1)
        grad_a0, sq_a0 = close(a0_own, a0_met, [(a0_got, 0)] + a0_r, vectors=True)
        grad_f0, sq_f0 = close(f0_own, f0_met, [(f0_got_lo, 0), f0_r1, f0_r2, f0_r3])
        squares = (sq_f1 + sq_a1) + (sq_f0 + sq_a0)
    else:
        input_grad = finish_input(mid, done, met)
        scatter = lambda g: lax.psum_scatter(g[0], "dp", scatter_dimension=0, tiled=True).astype(f32)
        grad_f1, grad_a1, grad_f0, grad_a0 = (scatter(g) for g in (g_f1, g_a1, g_f0, g_a0))
        once = jnp.where(lax.axis_index("tensor") == 0, 1.0, 0.0).astype(f32)
        square = lambda a: jnp.sum(a * a)
        squares = (
            square(grad_a0[:, :ATT])
            + square(grad_f0)
            + square(grad_a1)
            + square(grad_f1)
            + square(grad_a0[:, ATT + 12 :])
            + once * square(grad_a0[:, ATT : ATT + 12])
        )
        squares = jnp.full((8, LANES), squares / (8 * LANES), f32)

    squares = sum_everywhere(squares)
    if pieced:
        new = update_matrices(*masters, [grad_a0, grad_f0, grad_a1, grad_f1], squares)
        turn = lambda a: jnp.transpose(a, (1, 0, 2))
        vectors = update_vectors(
            grad_a0[:, ATT:],
            squares,
            [turn(a) for a in (rep_vectors, rep_first, rep_second)],
            (split_vectors, split_first, split_second),
        )
        grad_norm = vectors[0][0, 0]
        new_rep, rep_first_new, rep_second_new, rep_low = (turn(a) for a in vectors[1:5])
        bias_grad = vectors[5]
        new_split, split_first_new, split_second_new, split_low = vectors[6:]
    else:
        block = grad_a0[:, ATT:]
        grad_rep = block[:, :12].T.reshape(rep_vectors.shape)
        grad_split = (
            block[:, 12:18].reshape(rows, LAYERS, 3).transpose(1, 0, 2).reshape(split_vectors.shape)
        )
        grad_norm, factor = (a[0, 0] for a in clip_factor(squares))
        clipped_rep = grad_rep * factor
        grad = jnp.stack(
            [
                jnp.concatenate([grad_a0[:, :ATT], grad_f0], axis=1),
                jnp.concatenate([grad_a1, grad_f1], axis=1),
            ]
        ).reshape(tiled_shape)
        new = adamw(*masters, grad * factor, weight_rate, weight_decay)
        new = (*new, new[0].astype(b16))
        new_split, split_first_new, split_second_new = adamw(
            split_vectors, split_first, split_second, grad_split * factor, vector_rate, 0.0
        )
        new_rep, rep_first_new, rep_second_new = adamw(
            rep_vectors, rep_first, rep_second, clipped_rep, vector_rate, 0.0
        )
        split_low, rep_low = new_split.astype(b16), new_rep.astype(b16)
        bias_grad = clipped_rep[:, 0, :]
    new_weights, weights_first_new, weights_second_new, weights_low = (
        a.reshape(shard_shape) for a in new
    )
    return (
        block_out,
        input_grad,
        grad_norm,
        new_weights,
        weights_first_new,
        weights_second_new,
        weights_low,
        new_split,
        split_first_new,
        split_second_new,
        split_low,
        new_rep,
        rep_first_new,
        rep_second_new,
        rep_low,
        bias_grad,
    )


def solution(mesh):
    rows, packed, vector = P("dp", None, None), P(None, "tensor", "dp"), P(None, None, "dp")
    return jax.shard_map(
        per_device,
        mesh=mesh,
        in_specs=(rows, rows, P("dp", None)) + (packed,) * 6 + (vector,) * 3,
        out_specs=(rows, rows, P()) + (packed,) * 8 + (vector,) * 4 + (P(None, "dp"),),
        check_vma=False,
    )
```

```python
from functools import partial

import jax
import jax.numpy as jnp
from jax import lax
from jax.experimental import pallas as pl
from jax.experimental.pallas import tpu as pltpu
from jax.sharding import PartitionSpec as P

D = 768
HEAD_DIM = 64
LAYERS = 2
SEQ = 256
MICRO = 2
STEP = 3
HD = 384
FFT = 1536
QKV = 3 * HD
ATT = 4 * HD
COLS = ATT + 2 * FFT
VCOL = 2 * HD + FFT
LANES = 128
TILES = COLS // LANES

clip_limit = 1.0
weight_rate = 0.03
weight_decay = 0.01
vector_rate = 0.3
contract_last = (((1,), (1,)), ((), ()))
contract_first = (((0,), (0,)), ((), ()))
f32 = jnp.float32
b16 = jnp.bfloat16
VM = pl.BlockSpec(memory_space=pltpu.VMEM)


def call(body, outs, in_specs, scratch=(), flops=0, moved=0, out_specs=None, trans=0, limit=13):
    weight = 16 if flops else 1
    if out_specs is None:
        out_specs = [VM] * len(outs)
    return pl.pallas_call(
        body,
        out_shape=[jax.ShapeDtypeStruct(s, d) for s, d in outs],
        in_specs=in_specs,
        out_specs=out_specs,
        scratch_shapes=list(scratch),
        compiler_params=pltpu.CompilerParams(vmem_limit_bytes=limit * 1024 * 1024),
        cost_estimate=pl.CostEstimate(
            flops=int(flops * weight), bytes_accessed=int(moved * weight), transcendentals=trans
        ),
    )


def dot(a, b, dims=(((1,), (0,)), ((), ()))):
    return lax.dot_general(a, b, dims, preferred_element_type=f32)


def norm_rows(value):
    center = value - jnp.mean(value, axis=-1, keepdims=True)
    scale = lax.rsqrt(jnp.mean(center * center, axis=-1, keepdims=True) + 1e-12)
    return center * scale, scale


def norm_back(grad_out, normed, scale, gain):
    inner = grad_out * gain
    back = scale * (
        inner
        - jnp.mean(inner, axis=-1, keepdims=True)
        - normed * jnp.mean(inner * normed, axis=-1, keepdims=True)
    )
    return (
        back,
        jnp.sum(grad_out * normed, axis=0, keepdims=True),
        jnp.sum(grad_out, axis=0, keepdims=True),
    )


def places(ring):
    me = lax.axis_index("dp")
    return lax.div(me, 4), lax.rem(lax.div(me, 2), 2), lax.rem(me, 2)


def pairs_of(ndp, kind):
    if kind in (1, 2, 3):
        return [(i, (i + 4 * kind) % ndp) for i in range(ndp)]
    if kind == "x":
        return [(i, i ^ 2) for i in range(ndp)]
    return [(i, i ^ 1) for i in range(ndp)]


def move(a, kind):
    return lax.ppermute(a, "dp", pairs_of(lax.axis_size("dp"), kind))


def exchange(a):
    return lax.ppermute(a, "tensor", [(0, 1), (1, 0)])


def after(value, *others):
    return lax.optimization_barrier((value,) + others)[0]


def tie(*arrays):
    return lax.optimization_barrier(arrays)


def unique(entries):
    entries = [e if isinstance(e, tuple) else (e, Ellipsis) for e in entries]
    arrays, at = [], []
    for array, _ in entries:
        found = [i for i, a in enumerate(arrays) if a is array]
        if not found:
            found = [len(arrays)]
            arrays.append(array)
        at.append(found[0])
    return arrays, at, [where for _, where in entries]


def stack(entries, rows, cols, lead=None):
    arrays, at, where = unique(entries)
    lead = (len(entries),) if lead is None else lead

    def body(*refs):
        for i in range(len(entries)):
            place = (i,) if len(lead) == 1 else (i // lead[1], i % lead[1])
            refs[-1][place] = refs[at[i]][where[i]]

    size = len(entries) * rows * cols
    return call(body, [(lead + (rows, cols), b16)], [VM] * len(arrays), moved=4 * size)(*arrays)[0]


def settle(mine, met):
    ring, rows, cols = mine[0].shape

    def body(*refs):
        z, x, c = places(ring)
        for other in range(2):
            for xo in range(2):
                for k in range(ring):
                    zz = lax.rem(z - k + ring, ring)
                    xx = lax.rem(x + xo, 2)
                    cc = lax.rem(c + other, 2)
                    row = pl.multiple_of(((zz * 2 + xx) * 2 + cc) * rows, 16)
                    refs[4][pl.ds(row, rows), :] = refs[2 * other + xo][k]

    return call(
        body, [((4 * ring * rows, cols), b16)], [VM] * 4, moved=16 * ring * rows * cols
    )(*mine, *met)[0]


def prep(weights_tiled, rep, split):
    tiled_rows = weights_tiled.shape[1]
    rows = tiled_rows // TILES
    per = split.shape[1]

    def body(w_ref, rep_ref, split_ref, a0, f0, l1, every):
        a1, f1 = l1.at[:, :ATT], l1.at[:, ATT:]
        for layer, (a_ref, f_ref) in enumerate(((a0, f0), (a1, f1))):
            for c in range(TILES):
                piece = w_ref[layer, pl.ds(c, rows, stride=TILES), :].astype(b16)
                if c < ATT // LANES:
                    a_ref[:, c * LANES : (c + 1) * LANES] = piece
                else:
                    at = c * LANES - ATT
                    f_ref[:, at : at + LANES] = piece
        row = lax.broadcasted_iota(jnp.int32, (rows, rows), 0)
        col = lax.broadcasted_iota(jnp.int32, (rows, rows), 1)
        eye = (row == col).astype(b16)
        row3 = lax.broadcasted_iota(jnp.int32, (rows, per), 0)
        col3 = lax.broadcasted_iota(jnp.int32, (rows, per), 1)
        gap = col3 - 3 * row3
        block = jnp.zeros((rows, LANES), f32)
        lane = lax.broadcasted_iota(jnp.int32, (rows, LANES), 1)
        rep_cols = dot(eye, rep_ref[...].astype(b16), contract_last)
        rep_wide = jnp.concatenate(
            [rep_cols, jnp.zeros((rows, LANES - 6 * LAYERS), f32)], axis=1
        )
        block = rep_wide
        low = split_ref[...].astype(b16).astype(f32)
        for layer in range(LAYERS):
            for j in range(3):
                pick = jnp.where(gap == j, jnp.broadcast_to(low[layer : layer + 1], (rows, per)), 0.0)
                value = jnp.sum(pick, axis=1, keepdims=True)
                block = jnp.where(lane == 6 * LAYERS + 3 * layer + j, value, block)
        a0[:, ATT:] = block.astype(b16)
        every[:, : ATT + LANES] = a0[...]
        every[:, ATT + LANES : COLS + LANES] = f0[...]
        every[:, COLS + LANES :] = l1[...]

    return call(
        body,
        [
            ((rows, ATT + LANES), b16),
            ((rows, 2 * FFT), b16),
            ((rows, COLS), b16),
            ((rows, 2 * COLS + LANES), b16),
        ],
        [VM] * 3,
        moved=weights_tiled.size * 6,
    )(weights_tiled, rep, split)


def spread_mask(first_row, rows, first, cols):
    row = first_row + lax.broadcasted_iota(jnp.int32, (rows, cols), 0)
    col = first + lax.broadcasted_iota(jnp.int32, (rows, cols), 1)
    gap = col - 3 * row
    return jnp.where((gap >= 0) & (gap < 3), 1.0, 0.0).astype(b16)


def unpack(gathered):
    def body(w_ref, rep_ref, split_ref):
        flat = w_ref[:, ATT:]
        turned = flat.astype(f32).T
        rep_ref[...] = turned[:16]
        low = turned[:24].astype(b16)
        step = VCOL // 3
        for i in range(3):
            rows = D // 3
            mask = spread_mask(i * rows, rows, i * step, step)
            spread = dot(low[:, i * rows : (i + 1) * rows], mask)
            phase = lax.rem(lax.broadcasted_iota(jnp.int32, (1, step), 1), 3)
            for layer in range(LAYERS):
                at = 6 * LAYERS + 3 * layer
                value = jnp.where(
                    phase == 0,
                    spread[at : at + 1],
                    jnp.where(phase == 1, spread[at + 1 : at + 2], spread[at + 2 : at + 3]),
                )
                split_ref[layer : layer + 1, i * step : (i + 1) * step] = value

    return call(
        body,
        [((16, D), f32), ((8, VCOL), f32)],
        [VM],
        moved=D * LANES * 2,
        flops=24 * D * VCOL,
    )(gathered)


def gelu_parts(inner):
    cdf = 0.5 * (1.0 + lax.erf(inner * (0.5**0.5)))
    dens = jnp.exp(-0.5 * inner * inner) * 0.3989422804014327
    return inner * cdf, cdf + inner * dens


def attend(h_low, layer, w_ref, split_ref, seg_ref, part_ref, qkv_ref, probs_ref, ctx_ref):
    mixed = dot(h_low, w_ref[:, :QKV])
    qkv_ref[:, :HD] = (mixed[:, :HD] + split_ref[layer : layer + 1, :HD]).astype(b16)
    qkv_ref[:, HD : 2 * HD] = mixed[:, HD : 2 * HD].astype(b16)
    qkv_ref[:, 2 * HD :] = (
        mixed[:, 2 * HD :] + split_ref[layer : layer + 1, HD : 2 * HD]
    ).astype(b16)
    seg = jnp.broadcast_to(seg_ref[...].astype(f32), (SEQ, SEQ))
    same = seg == seg.T
    low_half = lax.broadcasted_iota(jnp.int32, (1, LANES), 1) < HEAD_DIM
    for pair in range(HD // LANES):
        at = pair * LANES
        query = qkv_ref[:, at : at + LANES].astype(f32) * HEAD_DIM ** (-0.5)
        keys = qkv_ref[:, HD + at : HD + at + LANES]
        values = qkv_ref[:, 2 * HD + at : 2 * HD + at + LANES].astype(f32)
        total = jnp.zeros((SEQ, LANES), f32)
        for half in range(2):
            mine = low_half if half == 0 else ~low_half
            scores = dot(jnp.where(mine, query, 0.0).astype(b16), keys, contract_last)
            scores = jnp.where(same, scores, -1000000000.0)
            raised = jnp.exp(scores - jnp.max(scores, axis=-1, keepdims=True))
            probs = (raised * (1.0 / jnp.sum(raised, axis=-1, keepdims=True))).astype(b16)
            probs_ref[2 * pair + half] = probs
            total = total + dot(probs, jnp.where(mine, values, 0.0).astype(b16))
        ctx_ref[:, at : at + LANES] = total.astype(b16)
    part_ref[...] = dot(ctx_ref[...], w_ref[:, QKV:ATT], contract_last).astype(b16)


ATT_FLOPS = 2 * SEQ * D * ATT + 4 * SEQ * SEQ * HD * 2
FFN_FLOPS = 2 * SEQ * D * 2 * FFT


ATT_OUTS = [((MICRO, SEQ, QKV), b16), ((MICRO, HD // HEAD_DIM, SEQ, SEQ), b16), ((MICRO, SEQ, HD), b16)]


def attention_first(block_in, segments, split, matrix):
    def body(h_ref, seg_ref, split_ref, w_ref, part_ref, qkv_ref, probs_ref, ctx_ref):
        for m in range(MICRO):
            views = [r.at[m] for r in (part_ref, qkv_ref, probs_ref, ctx_ref)]
            attend(h_ref[m], 0, w_ref, split_ref, seg_ref[m], *views)

    return call(
        body,
        [((MICRO, SEQ, D), b16)] + ATT_OUTS,
        [VM] * 4,
        flops=2 * ATT_FLOPS,
        moved=12 << 20,
        limit=16,
    )(block_in, segments, split, matrix)


def attention_next(micro, layer, normed, part_own, part_other, rep, segments, split, matrix):
    base = 6 * (layer - 1)

    def body(n_ref, own_ref, other_ref, rep_ref, seg_ref, split_ref, w_ref, *refs):
        part_ref, qkv_ref, probs_ref, ctx_ref, n2_ref, s2_ref, low_ref = refs
        first = n_ref[micro] * rep_ref[base + 1 : base + 2] + rep_ref[base + 2 : base + 3]
        added = own_ref[...].astype(f32) + other_ref[...].astype(f32)
        n2, s2 = norm_rows(first + added + rep_ref[base + 3 : base + 4])
        n2_ref[...] = n2
        s2_ref[...] = s2
        low = (n2 * rep_ref[base + 4 : base + 5] + rep_ref[base + 5 : base + 6]).astype(b16)
        low_ref[...] = low
        attend(
            low, layer, w_ref, split_ref, seg_ref[micro], part_ref, qkv_ref, probs_ref, ctx_ref
        )

    return call(
        body,
        [((SEQ, D), b16)]
        + [(shape[1:], kind) for shape, kind in ATT_OUTS]
        + [((SEQ, D), f32), ((SEQ, 1), f32), ((SEQ, D), b16)],
        [VM] * 7,
        flops=ATT_FLOPS,
        moved=8 << 20,
    )(normed, part_own, part_other, rep, segments, split, matrix)


def feed_step(hidden_in, added, layer, rep_ref, split_ref, w_ref, outs):
    base = 6 * layer
    part_ref, n1_ref, s1_ref, low_ref, act_ref, slope_ref = outs
    n1, s1 = norm_rows(hidden_in + added + rep_ref[base : base + 1])
    n1_ref[...] = n1
    s1_ref[...] = s1
    low_ref[...] = (n1 * rep_ref[base + 1 : base + 2] + rep_ref[base + 2 : base + 3]).astype(b16)
    step = 512
    for at in range(0, FFT, step):
        inner = (
            dot(low_ref[...], w_ref[:, at : at + step])
            + split_ref[layer : layer + 1, 2 * HD + at : 2 * HD + at + step]
        )
        active, slope = gelu_parts(inner)
        act_ref[:, at : at + step] = active.astype(b16)
        slope_ref[:, at : at + step] = slope.astype(b16)
    part_ref[...] = dot(act_ref[...], w_ref[:, FFT:], contract_last).astype(b16)


FEED_OUTS = [
    ((SEQ, D), b16),
    ((SEQ, D), f32),
    ((SEQ, 1), f32),
    ((SEQ, D), b16),
    ((SEQ, FFT), b16),
    ((SEQ, FFT), b16),
]


def feed_first(hidden, part_own, part_other, rep, split, matrix):
    def body(h_ref, own_ref, other_ref, rep_ref, split_ref, w_ref, *refs):
        parts, outs = refs[:MICRO], refs[MICRO:]
        for m in range(MICRO):
            added = own_ref[m].astype(f32) + other_ref[m].astype(f32)
            views = [parts[m]] + [r.at[m] for r in outs]
            feed_step(h_ref[m].astype(f32), added, 0, rep_ref, split_ref, w_ref, views)

    return call(
        body,
        [((SEQ, D), b16)] * MICRO + [((MICRO,) + shape, kind) for shape, kind in FEED_OUTS[1:]],
        [VM] * 6,
        flops=2 * FFN_FLOPS,
        moved=20 << 20,
        limit=22,
    )(hidden, part_own, part_other, rep, split, matrix)


def feed_forward(micro, layer, hidden, part_own, part_other, rep, split, matrix):
    base = 6 * layer

    def body(h_ref, own_ref, other_ref, rep_ref, split_ref, w_ref, *outs):
        hidden_in = h_ref[...] * rep_ref[base - 2 : base - 1] + rep_ref[base - 1 : base]
        added = own_ref[...].astype(f32) + other_ref[...].astype(f32)
        feed_step(hidden_in, added, layer, rep_ref, split_ref, w_ref, outs)

    return call(
        body,
        FEED_OUTS,
        [VM] * 6,
        flops=FFN_FLOPS,
        moved=10 << 20,
    )(hidden, part_own, part_other, rep, split, matrix)


def view(ref, micro):
    return ref.at[micro] if ref.shape[0] == MICRO else ref


def feed_back_tail(grad, n2, s2, layer, rep_ref, slope_ref, w_ref, outs):
    base = 6 * layer
    part_ref, res_ref, dffn_ref, din_ref, vec_ref = outs
    back, gain, shift = norm_back(grad, n2, s2, rep_ref[base + 4 : base + 5])
    res_ref[...] = back
    dffn_ref[...] = back.astype(b16)
    vec_ref[...] = jnp.zeros_like(vec_ref)
    vec_ref[0:1] = jnp.sum(back, axis=0, keepdims=True)
    vec_ref[1:2] = gain
    vec_ref[2:3] = shift
    step = 384
    for at in range(0, FFT, step):
        grad_act = dot(dffn_ref[...], w_ref[:, FFT + at : FFT + at + step])
        grad_in = (slope_ref[:, at : at + step].astype(f32) * grad_act).astype(b16)
        din_ref[:, at : at + step] = grad_in
        row, lane = 3 + at // D, at % D
        vec_ref[row : row + 1, lane : lane + step] = jnp.sum(
            grad_in.astype(f32), axis=0, keepdims=True
        )
    part_ref[...] = dot(din_ref[...], w_ref[:, :FFT], contract_last).astype(b16)


BACK_OUTS = [
    ((SEQ, D), b16),
    ((SEQ, D), f32),
    ((SEQ, D), b16),
    ((SEQ, FFT), b16),
    ((8, D), f32),
]


def feed_back_top(micro, layer, out_grad, n1, part_own, part_other, rep, slope, matrix):
    base = 6 * layer

    def body(g_ref, n_ref, own_ref, other_ref, rep_ref, slope_ref, w_ref, *refs):
        out_ref = refs[5]
        first = n_ref[...] * rep_ref[base + 1 : base + 2] + rep_ref[base + 2 : base + 3]
        added = own_ref[...].astype(f32) + other_ref[...].astype(f32)
        n2, s2 = norm_rows(first + added + rep_ref[base + 3 : base + 4])
        out_ref[...] = (n2 * rep_ref[base + 4 : base + 5] + rep_ref[base + 5 : base + 6]).astype(b16)
        feed_back_tail(
            g_ref[micro].astype(f32), n2, s2, layer, rep_ref, slope_ref, w_ref, refs[:5]
        )

    return call(
        body,
        BACK_OUTS + [((SEQ, D), b16)],
        [VM] * 6 + [VM],
        flops=FFN_FLOPS,
        moved=11 << 20,
    )(out_grad, n1, part_own, part_other, rep, slope, matrix)


def feed_back(micro, layer, mid, part_own, part_other, n2, s2, rep, slope, matrix):
    def body(mid_ref, own_ref, other_ref, n2_ref, s2_ref, rep_ref, slope_ref, w_ref, *refs):
        added = own_ref[...].astype(f32) + other_ref[...].astype(f32)
        feed_back_tail(
            mid_ref[...] + added,
            view(n2_ref, micro)[...],
            view(s2_ref, micro)[...],
            layer,
            rep_ref,
            view(slope_ref, micro),
            w_ref,
            refs[:5],
        )

    return call(
        body,
        BACK_OUTS,
        [VM] * 7 + [VM],
        flops=FFN_FLOPS,
        moved=11 << 20,
    )(mid, part_own, part_other, n2, s2, rep, slope, matrix)


def attention_back(micro, layer, res, part_own, part_other, n1, s1, rep, qkv, probs, ctx, matrix):
    base = 6 * layer

    def body(
        res_ref, own_ref, other_ref, n1_ref, s1_ref, rep_ref, qkv_ref, probs_ref, ctx_ref, w_ref, *refs
    ):
        part_ref, mid_ref, datt_ref, dqkv_ref, vec_ref = refs
        n1_ref, s1_ref, qkv_ref, probs_ref, ctx_ref = (
            view(r, micro) for r in (n1_ref, s1_ref, qkv_ref, probs_ref, ctx_ref)
        )
        grad = res_ref[...] + (own_ref[...].astype(f32) + other_ref[...].astype(f32))
        back, gain, shift = norm_back(grad, n1_ref[...], s1_ref[...], rep_ref[base + 1 : base + 2])
        mid_ref[...] = back
        datt_ref[...] = back.astype(b16)
        vec_ref[...] = jnp.zeros_like(vec_ref)
        vec_ref[0:1] = jnp.sum(back, axis=0, keepdims=True)
        vec_ref[1:2] = gain
        vec_ref[2:3] = shift
        dctx = dot(datt_ref[...], w_ref[:, QKV:ATT]).astype(b16).astype(f32)
        low_half = lax.broadcasted_iota(jnp.int32, (1, LANES), 1) < HEAD_DIM
        factor = HEAD_DIM ** (-0.5)
        for pair in range(HD // LANES):
            at = pair * LANES
            query = qkv_ref[:, at : at + LANES].astype(f32) * factor
            keys = qkv_ref[:, HD + at : HD + at + LANES].astype(f32) * factor
            values = qkv_ref[:, 2 * HD + at : 2 * HD + at + LANES]
            dc = dctx[:, at : at + LANES]
            weighed = dc * ctx_ref[:, at : at + LANES].astype(f32)
            dq = jnp.zeros((SEQ, LANES), f32)
            dk = jnp.zeros((SEQ, LANES), f32)
            dv = jnp.zeros((SEQ, LANES), f32)
            for half in range(2):
                mine = low_half if half == 0 else ~low_half
                dcm = jnp.where(mine, dc, 0.0).astype(b16)
                delta = jnp.sum(jnp.where(mine, weighed, 0.0), axis=-1, keepdims=True)
                probs = probs_ref[2 * pair + half]
                dprobs = dot(dcm, values, contract_last)
                dscores = (probs.astype(f32) * (dprobs - delta)).astype(b16)
                dq = dq + dot(dscores, jnp.where(mine, keys, 0.0).astype(b16))
                dk = dk + dot(dscores, jnp.where(mine, query, 0.0).astype(b16), contract_first)
                dv = dv + dot(probs, dcm, contract_first)
            dqkv_ref[:, at : at + LANES] = dq.astype(b16)
            dqkv_ref[:, HD + at : HD + at + LANES] = dk.astype(b16)
            dqkv_ref[:, 2 * HD + at : 2 * HD + at + LANES] = dv.astype(b16)
        vec_ref[3:4, :HD] = jnp.sum(dqkv_ref[:, :HD].astype(f32), axis=0, keepdims=True)
        vec_ref[3:4, HD:] = jnp.sum(dqkv_ref[:, 2 * HD :].astype(f32), axis=0, keepdims=True)
        part_ref[...] = dot(dqkv_ref[...], w_ref[:, :QKV], contract_last).astype(b16)

    return call(
        body,
        [
            ((SEQ, D), b16),
            ((SEQ, D), f32),
            ((SEQ, D), b16),
            ((SEQ, QKV), b16),
            ((8, D), f32),
        ],
        [VM] * 9 + [VM],
        flops=2 * ATT_FLOPS,
        moved=9 << 20,
    )(res, part_own, part_other, n1, s1, rep, qkv, probs, ctx, matrix)


def finish_input(mids, owns, others):
    def body(*refs):
        for micro in range(MICRO):
            m, a, b = refs[3 * micro : 3 * micro + 3]
            refs[-1][micro] = m[...] + (a[...].astype(f32) + b[...].astype(f32))

    args = []
    for micro in range(MICRO):
        args += [mids[micro], owns[micro], others[micro]]
    return call(body, [((MICRO, SEQ, D), f32)], [VM] * len(args), moved=7 << 20)(*args)[0]


def store_slots(product_ref, outs, at, width):
    if len(outs) == 1:
        outs[0][:, at : at + width] = product_ref[:, :width].astype(b16)
        return
    ring, rows = outs[0].shape[1], outs[0].shape[2]
    z, x, c = places(ring)
    for other in range(2):
        for xo in range(2):
            for k in range(ring):
                zz = lax.rem(z + k, ring)
                xx = lax.rem(x + xo, 2)
                cc = lax.rem(c + other, 2)
                row = pl.multiple_of(((zz * 2 + xx) * 2 + cc) * rows, 16)
                outs[other][xo, k, :, at : at + width] = product_ref[
                    pl.ds(row, rows), :width
                ].astype(b16)


def grad_outs(ndp, pieced, cols):
    rows = D // ndp
    if pieced:
        return [((2, ndp // 4, rows, cols), b16)] * 2
    return [((D, cols), b16)]


def matrix_gradient(sets, pieced, ndp, vectors=None):
    widths = [s[2] for s in sets]
    total = sum(widths) + (LANES if vectors is not None else 0)
    outs = grad_outs(ndp, pieced, total)
    args, specs = [], []
    for left, right, _ in sets:
        for micro in range(MICRO):
            specs.append(VM)
            args.append(left[micro])
        for micro in range(MICRO):
            args.append(right[micro])
            specs.append(VM)
    plain = len(args)
    if vectors is not None:
        args += vectors
        specs += [VM] * len(vectors)
    n_in = len(args)
    step = 384

    def body(*refs):
        out_refs = refs[n_in : n_in + len(outs)]
        prod_ref = refs[n_in + len(outs)]
        at = 0
        for index, width in enumerate(widths):
            l0, l1, r0, r1 = refs[4 * index : 4 * index + 4]
            left = [r[m] if len(r.shape) == 3 else r[...] for m, r in enumerate((l0, l1))]
            r0, r1 = (r.at[m] if len(r.shape) == 3 else r for m, r in enumerate((r0, r1)))
            for col in range(0, width, step):
                prod_ref[...] = dot(left[0], r0[:, col : col + step], contract_first) + dot(
                    left[1], r1[:, col : col + step], contract_first
                )
                store_slots(prod_ref, out_refs, at, step)
                at += step
        if vectors is not None:
            pack_vectors(refs[plain:n_in], prod_ref)
            store_slots(prod_ref, out_refs, at, LANES)

    moved = sum(a.size * 2 for a in args[:plain]) + D * total * 2
    return call(
        body,
        outs,
        specs,
        [pltpu.VMEM((D, step), f32)],
        flops=2 * MICRO * SEQ * D * total,
        moved=moved,
    )(*args)


def pack_vectors(vec_refs, prod_ref):
    sums = []
    for layer in range(LAYERS):
        a0, a1, b0, b1 = vec_refs[4 * layer : 4 * layer + 4]
        sums.append((a0[...] + a1[...], b0[...] + b1[...]))
    rows = []
    for att, ffn in sums:
        rows += [att[0:1], att[1:2], att[2:3], ffn[0:1], ffn[1:2], ffn[2:3]]
    rows.append(jnp.zeros((4, D), f32))
    turned = jnp.concatenate(rows, axis=0)
    turned = jnp.concatenate([turned, jnp.zeros((LANES - 16, D), f32)], axis=0).T
    step = VCOL // 3
    phase = lax.rem(lax.broadcasted_iota(jnp.int32, (1, step), 1), 3)
    lane = lax.broadcasted_iota(jnp.int32, (1, LANES), 1)
    for i in range(3):
        picked = []
        for att, ffn in sums:
            line = (att[3:4], ffn[3:4], ffn[4:5])[i]
            for j in range(3):
                picked.append(jnp.where(phase == j, line, 0.0))
        picked = jnp.concatenate(
            [jnp.zeros((12, step), f32)] + picked + [jnp.zeros((LANES - 18, step), f32)], axis=0
        ).astype(b16)
        n_rows = D // 3
        mask = spread_mask(i * n_rows, n_rows, i * step, step)
        part = dot(mask, picked, contract_last)
        keep = turned[i * n_rows : (i + 1) * n_rows]
        prod_ref[i * n_rows : (i + 1) * n_rows, :LANES] = jnp.where(lane < 12, keep, part)


def meet(own, met, places):
    lo, hi = places[0], places[-1] + 1
    return (own[1, lo:hi].astype(f32) + met[1, lo:hi].astype(f32)).astype(b16)


def pass_on(own, met, got, places):
    lo, hi = places[0], places[-1] + 1
    total = own[0, lo:hi].astype(f32) + met[0, lo:hi].astype(f32) + got.astype(f32)
    return [total[i].astype(b16) for i in range(hi - lo)]


def pass_both(own, met, k, received=None):
    total = own[:, k].astype(f32) + met[:, k].astype(f32)
    if received is not None:
        total = total + received.astype(f32)
    return total.astype(b16)


def close(own, met, parts, vectors=False):
    _, _, rows, cols = own.shape
    mats = cols - LANES if vectors else cols
    parts = [p if isinstance(p, tuple) else (p, None) for p in parts]
    n = len(parts)

    def body(own_ref, met_ref, *refs):
        out_ref, sq_ref = refs[n:]
        total = jnp.zeros((rows, LANES), f32)
        for at in range(0, cols, LANES):
            s = slice(at, at + LANES)
            value = own_ref[0, 0, :, s].astype(f32) + met_ref[0, 0, :, s].astype(f32)
            for (_, index), ref in zip(parts, refs[:n]):
                value = value + (ref[:, s] if index is None else ref[index, :, s]).astype(f32)
            out_ref[:, s] = value
            square = value * value
            if at >= mats:
                lane = lax.broadcasted_iota(jnp.int32, (rows, LANES), 1)
                twice = (lane < 6 * LAYERS) & (lax.axis_index("tensor") != 0)
                square = jnp.where(twice, 0.0, square)
            total = total + square
        part = total[:8]
        for i in range(8, rows, 8):
            part = part + total[i : i + 8]
        sq_ref[...] = part

    return call(
        body,
        [((rows, cols), f32), ((8, LANES), f32)],
        [VM] * (2 + n),
        moved=rows * cols * 14,
    )(own, met, *[p[0] for p in parts])


def adamw(value, first, second, grad, rate, decay):
    first = 0.5 * first + 0.5 * grad
    second = 0.5 * second + 0.5 * grad * grad
    correct = 1.0 - 0.5**STEP
    direction = first / correct / (jnp.sqrt(second / correct) + 1e-08)
    return (value - rate * (direction + decay * value), first, second)


def clip_factor(squares):
    norm = jnp.sqrt(jnp.sum(squares, keepdims=True))
    return norm, jnp.minimum(1.0, clip_limit / (norm + 1e-06))


def ready(tiled, first, second):
    def body(w_ref, m_ref, v_ref, w_out, m_out, v_out):
        w_out[...] = w_ref[...] * (1.0 - weight_rate * weight_decay)
        m_out[...] = 0.5 * m_ref[...]
        v_out[...] = 0.5 * v_ref[...]

    return call(body, [(tiled.shape, f32)] * 3, [VM] * 3, moved=24 * tiled.size)(tiled, first, second)


def stepped(decayed, half_first, half_second, grad, rate):
    first = half_first + 0.5 * grad
    second = half_second + 0.5 * grad * grad
    correct = 1.0 - 0.5**STEP
    direction = first / (correct * jnp.sqrt(second * (1.0 / correct)) + correct * 1e-08)
    return decayed - rate * direction, first, second


def update_vectors(block, squares, reps, splits):
    rows = block.shape[0]
    per = splits[0].shape[2]

    def body(b_ref, q_ref, rw, rm, rv, sw, sm, sv, norm_ref, rwo, rmo, rvo, rlo, go, swo, smo, svo, slo):
        norm, scale = clip_factor(q_ref[...])
        norm_ref[...] = norm
        turned = jnp.concatenate([b_ref[...], jnp.zeros((LANES - rows, LANES), f32)], axis=0).T
        for layer in range(LAYERS):
            at = slice(layer, layer + 1)
            for kind in range(6):
                grad = turned[6 * layer + kind : 6 * layer + kind + 1, :rows] * scale
                new = adamw(rw[kind, at], rm[kind, at], rv[kind, at], grad, vector_rate, 0.0)
                rwo[kind, at], rmo[kind, at], rvo[kind, at] = new
                if kind == 0:
                    go[at] = grad
        row = lax.broadcasted_iota(jnp.int32, (rows, per), 0)
        col = lax.broadcasted_iota(jnp.int32, (rows, per), 1)
        gap = col - 3 * row
        mask = jnp.where((gap >= 0) & (gap < 3), 1.0, 0.0)
        wide = lax.dot_general(
            turned[6 * LAYERS : 6 * LAYERS + 8, :rows],
            mask,
            (((1,), (0,)), ((), ())),
            preferred_element_type=f32,
            precision=lax.Precision.HIGHEST,
        )
        phase = lax.rem(lax.broadcasted_iota(jnp.int32, (1, per), 1), 3)
        for layer in range(LAYERS):
            one, two, three = (wide[3 * layer + j : 3 * layer + j + 1] for j in range(3))
            grad = jnp.where(phase == 0, one, jnp.where(phase == 1, two, three)) * scale
            new = adamw(sw[layer], sm[layer], sv[layer], grad, vector_rate, 0.0)
            swo[layer], smo[layer], svo[layer] = new
        rlo[...] = rwo[...].astype(b16)
        slo[...] = swo[...].astype(b16)

    rep, split = reps[0].shape, splits[0].shape
    return call(
        body,
        [((1, 1), f32)]
        + [(rep, f32)] * 3
        + [(rep, b16), ((LAYERS, rows), f32)]
        + [(split, f32)] * 3
        + [(split, b16)],
        [VM] * 8,
        moved=1 << 18,
    )(block, squares, *reps, *splits)


def update_matrices(decayed, first, second, grads, squares):
    rows = grads[0].shape[0]
    tiled = decayed
    step = 24 if rows % 24 == 0 else rows
    n_steps = rows // step
    block = (1, step * TILES, LANES)

    def body(f_ref, w_ref, m_ref, v_ref, a0, f0, a1, f1, nw, nm, nv, nl):
        scale = clip_factor(f_ref[...])[1]

        def columns(a_ref, g_ref):
            for c in range(TILES):
                lo = c * LANES
                if lo < ATT:
                    grad = a_ref[:, lo : lo + LANES]
                else:
                    grad = g_ref[:, lo - ATT : lo - ATT + LANES]
                where = (0, pl.ds(c, step, stride=TILES), slice(None))
                new = stepped(w_ref[where], m_ref[where], v_ref[where], grad * scale, weight_rate)
                nw[where], nm[where], nv[where] = new

        for layer, pair in enumerate(((a0, f0), (a1, f1))):
            pl.when(pl.program_id(0) == layer)(partial(columns, *pair))
        nl[...] = nw[...].astype(b16)

    big = pl.BlockSpec(block, lambda l, i: (l, i, 0))
    shape = tiled.shape
    return pl.pallas_call(
        body,
        grid=(LAYERS, n_steps),
        out_shape=[jax.ShapeDtypeStruct(shape, f32)] * 3 + [jax.ShapeDtypeStruct(shape, b16)],
        in_specs=[pl.BlockSpec((8, LANES), lambda l, i: (0, 0)), big, big, big]
        + [pl.BlockSpec((step, g.shape[1]), lambda l, i: (i, 0)) for g in grads],
        out_specs=[big] * 4,
        compiler_params=pltpu.CompilerParams(vmem_limit_bytes=13 * 1024 * 1024),
        cost_estimate=pl.CostEstimate(
            flops=20 * tiled.size, bytes_accessed=30 * tiled.size, transcendentals=tiled.size
        ),
    )(squares, tiled, first, second, *grads)


def sum_everywhere(value):
    ndp = lax.axis_size("dp")
    if ndp & (ndp - 1) or ndp < 4:
        return lax.psum(value, ("dp", "tensor"))

    def level(a, first, second):
        one, two, both = ppermute_bits(a, first), ppermute_bits(a, second), ppermute_bits(a, first | second)
        return (a + one) + (two + both)

    value = value + ppermute_bits(value, 2)
    value = level(value, 4, 1)
    bit = 8
    while bit < 2 * ndp:
        if 2 * bit < 2 * ndp:
            value = level(value, bit, 2 * bit)
        else:
            value = value + ppermute_bits(value, bit)
        bit *= 4
    return value


def ppermute_bits(value, bits):
    n = 2 * lax.axis_size("dp")
    return lax.ppermute(value, ("dp", "tensor"), [(i, i ^ bits) for i in range(n)])


def per_device(
    block_in,
    out_grad,
    segments,
    weights,
    weights_first,
    weights_second,
    split_vectors,
    split_first,
    split_second,
    rep_vectors,
    rep_first,
    rep_second,
):
    ndp = lax.axis_size("dp")
    rows = D // ndp
    per = split_vectors.shape[2]
    pieced = ndp == 16 and rows % 16 == 0
    shard_shape = weights.shape
    tiled_shape = (LAYERS, -1, LANES)
    masters = [a.reshape(tiled_shape) for a in (weights, weights_first, weights_second)]
    weights_tiled = masters[0]
    rep_flat = rep_vectors.reshape(LAYERS * 6, -1)
    split_flat = split_vectors.reshape(LAYERS, per)
    both = range(MICRO)
    seg = segments.reshape(MICRO, 1, SEQ)
    if pieced:
        a0, f0, l1, every = prep(weights_tiled, rep_flat, split_flat)
        across = partial(move, kind="x")
        third = slice(COLS + LANES, COLS + LANES + ATT)
        fourth = slice(COLS + LANES + ATT, None)

        def finish(slots, cols):
            mine = [stack(half, rows, cols) for half in (slots[:4], slots[4:])]
            return settle(mine, [move(a, "core") for a in mine])

        def cut(array, cols):
            return (array, (slice(None), cols))

        x0 = across(every)
        a0_r1, a0_r2, a0_r3, f0 = tie(move(a0, 1), move(a0, 2), move(a0, 3), f0)
        a0_x = across(stack([a0_r1, a0_r2, a0_r3], rows, ATT + LANES))
        f0_r1, f0_r3 = move(f0, 1), move(f0, 3)
        near = stack([a0, a0_r1, a0_r2, a0_r3], rows, ATT + LANES)
        mine0 = stack(
            [cut(x0, slice(0, ATT + LANES)), (a0_x, 0), (a0_x, 1), (a0_x, 2)], rows, ATT + LANES
        )
        mine0, f0_r1, l1 = tie(mine0, f0_r1, l1)
        watt0 = settle([near, mine0], [move(near, "core"), move(mine0, "core")])
        f0_x13 = across(stack([f0_r1, f0_r3], rows, 2 * FFT))
        f0_r2 = move(f0_r1, 1)
        l1_r1, l1_r3 = move(l1, 1), move(l1, 3)
        f0_x2 = across(f0_r2)
    else:
        low = weights.astype(b16).reshape(LAYERS, rows, COLS)
        block = jnp.concatenate(
            [
                rep_flat.T,
                split_flat.reshape(LAYERS, rows, 3).transpose(1, 0, 2).reshape(rows, 6),
                jnp.zeros((rows, LANES - 18), f32),
            ],
            axis=1,
        ).astype(b16)
        gather = partial(lax.all_gather, axis_name="dp", axis=0, tiled=True)
        watt0 = gather(jnp.concatenate([low[0, :, :ATT], block], axis=1))
        watt1 = gather(low[1, :, :ATT])
        wffn0, wffn1 = (gather(low[layer, :, ATT:]) for layer in range(LAYERS))
    rep, split = unpack(watt0)

    done, qkv0, probs0, ctx0 = attention_first(block_in, seg, split, watt0)
    met = exchange(done)
    if pieced:
        head, tail = slice(0, ATT), slice(ATT, None)
        a1_r2 = move(stack([cut(l1_r1, head)], rows, ATT), 1)
        f0_x13, f0_x2, l1_r1, l1_r3, a1_r2, met = tie(f0_x13, f0_x2, l1_r1, l1_r3, a1_r2, met)
        a1_x = across(stack([cut(l1_r1, head), (a1_r2, 0), cut(l1_r3, head)], rows, ATT))
        f1_r2 = move(stack([cut(l1_r1, tail)], rows, 2 * FFT), 1)
        wffn0 = finish(
            [f0, f0_r1, f0_r2, f0_r3]
            + [cut(x0, slice(ATT + LANES, COLS + LANES)), (f0_x13, 0), f0_x2, (f0_x13, 1)],
            2 * FFT,
        )
    *done, n1_0, s1_0, low1_0, act0, slope0 = feed_first(block_in, done, met, rep, split, wffn0)
    if pieced:
        a1_x, f1_r2, *done = tie(a1_x, f1_r2, *done)
        f1_x = across(stack([cut(l1_r1, tail), (f1_r2, 0), cut(l1_r3, tail)], rows, 2 * FFT))
        watt1 = finish(
            [cut(l1, head), cut(l1_r1, head), (a1_r2, 0), cut(l1_r3, head), cut(x0, third)]
            + [(a1_x, k) for k in range(3)],
            ATT,
        )
    met = [exchange(a) for a in done]
    out = [
        attention_next(m, 1, n1_0, done[m], met[m], rep, seg, split, watt1) for m in both
    ]
    done = [o[0] for o in out]
    qkv1, probs1, ctx1, n2_0, s2_0, low_h1 = ([o[i] for o in out] for i in range(1, 7))
    if pieced:
        wffn1 = finish(
            [cut(l1, tail), cut(l1_r1, tail), (f1_r2, 0), cut(l1_r3, tail), cut(x0, fourth)]
            + [(f1_x, k) for k in range(3)],
            2 * FFT,
        )
    met = [exchange(a) for a in done]
    out = [feed_forward(m, 1, n2_0[m], done[m], met[m], rep, split, wffn1) for m in both]
    n1_1, s1_1, low1_1, act1, slope1 = ([o[i] for o in out] for i in range(1, 6))
    met = [exchange(o[0]) for o in out]

    out = [
        feed_back_top(m, 1, out_grad, n1_1[m], out[m][0], met[m], rep, slope1[m], wffn1)
        for m in both
    ]
    res, dffn, din, vec_f1 = ([o[i] for o in out] for i in range(1, 5))
    block_out = jnp.stack([o[5] for o in out])
    done = [o[0] for o in out]
    met = [exchange(o[0]) for o in out]
    plan = {"w_f1": 0, "f1_3": 1, "w_a1": 2, "f1_2": 3, "a1_s": 3, "w_f0": 4, "f1_1": 5, "a1_t": 6, "f0_s": 5}
    held, ends = {}, []

    def make(name):
        gate = ends[-1:] if 1 else []
        if name == "w_f1":
            g = matrix_gradient([(low1_1, din_1, FFT), (dffn_1, act1, FFT)], pieced, ndp)
        elif name == "w_a1":
            g = matrix_gradient(
                [(low_h1, dqkv_1, QKV), (datt_1, ctx1, HD)], pieced, ndp
            )
        elif name == "w_f0":
            g = matrix_gradient(
                [([low1_0] * 2, din_0, FFT), (dffn_0, [act0] * 2, FFT)], pieced, ndp
            )
        elif not pieced:
            return []
        if name.startswith("w_"):
            held[name[2:]] = g if not pieced else (g[0], move(g[1], "core"))
            return [g[0]]
        own, across_core = held[name[:2]]
        if name[:3] == "f1_":
            k = int(name[3])
            if k == 3:
                total = pass_both(own, after(across_core, *gate), k)
            else:
                total = pass_both(own, across_core, k, after(held["f1_rec"], *gate))
            held["f1_rec"] = move(total, 1)
            return [total]
        if name == "a1_t":
            parts = pass_on(own, across_core, after(held["a1_got"], *gate)[1:], (1, 2, 3))
            held["a1_r"] = [move(t, k + 1) for k, t in enumerate(parts)]
            return [parts[2]]
        places = (0, 1, 2, 3) if name == "a1_s" else (2, 3)
        total = meet(own, after(across_core, *gate), places)
        held[name[:2] + "_got"] = move(total, "x")
        return [total]

    def before(stage, value):
        needed = [a for name in plan if plan[name] == stage for a in make(name)]
        return after(value, *needed) if needed else value

    din_1, dffn_1 = din, dffn
    out = []
    for m in both:
        value = before(m, res[m])
        out.append(
            attention_back(
                m, 1, value, done[m], met[m], n1_1[m], s1_1[m], rep, qkv1[m], probs1[m], ctx1[m], watt1
            )
        )
        ends.append(out[m][0])
    mid, datt_1, dqkv_1, vec_a1 = ([o[i] for o in out] for i in range(1, 5))
    done = [o[0] for o in out]
    met = [exchange(o[0]) for o in out]
    out = []
    for m in both:
        value = before(2 + m, mid[m])
        out.append(feed_back(m, 0, value, done[m], met[m], n2_0[m], s2_0[m], rep, slope0, wffn0))
        ends.append(out[m][0])
    res, dffn_0, din_0, vec_f0 = ([o[i] for o in out] for i in range(1, 5))
    done = [o[0] for o in out]
    met = [exchange(o[0]) for o in out]
    out = []
    for m in both:
        value = before(4 + m, res[m])
        out.append(
            attention_back(
                m, 0, value, done[m], met[m], n1_0, s1_0, rep, qkv0, probs0, ctx0, watt0
            )
        )
        ends.append(out[m][0])
    mid, datt, dqkv, vec_a0 = ([o[i] for o in out] for i in range(1, 5))
    done = [o[0] for o in out]
    met = [exchange(o[0]) for o in out]
    dqkv[0] = before(6, dqkv[0])
    g_a0 = matrix_gradient(
        [([block_in] * MICRO, dqkv, QKV), (datt, [ctx0] * 2, HD)],
        pieced,
        ndp,
        vectors=vec_a0 + vec_f0 + vec_a1 + vec_f1,
    )
    ends.append(g_a0[0])
    before(7, g_a0[0])
    if pieced:
        (f1_own, f1_met), (a1_own, a1_met), (f0_own, f0_met) = (held[c] for c in ("f1", "a1", "f0"))
        f1_rec, a1_got, a1_r, f0_got_hi = (held[c] for c in ("f1_rec", "a1_got", "a1_r", "f0_got"))
    else:
        g_f1, g_a1, g_f0 = (held[c] for c in ("f1", "a1", "f0"))
    if pieced:
        masters = ready(*(after(a, g_a0[0]) for a in masters))
        input_grad = finish_input(mid, done, met)
        a0_own, a0_met = g_a0[0], move(g_a0[1], "core")
        a0_got = across(meet(a0_own, a0_met, (0, 1, 2, 3)))
        f1_last = pass_both(f1_own, f1_met, 0, f1_rec)
        f1_got = across(f1_last[1])
        f0_t2, f0_t3 = pass_on(f0_own, f0_met, f0_got_hi, (2, 3))
        f0_r3, f0_r2 = move(f0_t3, 3), move(f0_t2, 2)
        a0_got, f0_r3, f0_r2, *a1_r = tie(a0_got, f0_r3, f0_r2, *a1_r)
        f0_got_lo = across(meet(f0_own, f0_met, (0, 1)))
        a0_t = pass_on(a0_own, a0_met, a0_got[1:], (1, 2, 3))
        a0_r = [move(t, k + 1) for k, t in enumerate(a0_t)]
        grad_a1, sq_a1 = close(a1_own, a1_met, [(a1_got, 0)] + a1_r)
        grad_f1, sq_f1 = close(f1_own, f1_met, [f1_got, (f1_rec, 0)])
        f0_got_lo, grad_f1, grad_a1, block_out, input_grad, *rest = tie(
            f0_got_lo, grad_f1, grad_a1, block_out, input_grad, *a0_r, *masters
        )
        a0_r, masters = rest[:3], rest[3:]
        f0_r1 = move(pass_on(f0_own, f0_met, f0_got_lo[1:], (1,))[0], 1)
        grad_a0, sq_a0 = close(a0_own, a0_met, [(a0_got, 0)] + a0_r, vectors=True)
        grad_f0, sq_f0 = close(f0_own, f0_met, [(f0_got_lo, 0), f0_r1, f0_r2, f0_r3])
        squares = (sq_f1 + sq_a1) + (sq_f0 + sq_a0)
    else:
        input_grad = finish_input(mid, done, met)
        scatter = lambda g: lax.psum_scatter(g[0], "dp", scatter_dimension=0, tiled=True).astype(f32)
        grad_f1, grad_a1, grad_f0, grad_a0 = (scatter(g) for g in (g_f1, g_a1, g_f0, g_a0))
        once = jnp.where(lax.axis_index("tensor") == 0, 1.0, 0.0).astype(f32)
        square = lambda a: jnp.sum(a * a)
        squares = (
            square(grad_a0[:, :ATT])
            + square(grad_f0)
            + square(grad_a1)
            + square(grad_f1)
            + square(grad_a0[:, ATT + 12 :])
            + once * square(grad_a0[:, ATT : ATT + 12])
        )
        squares = jnp.full((8, LANES), squares / (8 * LANES), f32)

    squares = sum_everywhere(squares)
    if pieced:
        new = update_matrices(*masters, [grad_a0, grad_f0, grad_a1, grad_f1], squares)
        turn = lambda a: jnp.transpose(a, (1, 0, 2))
        vectors = update_vectors(
            grad_a0[:, ATT:],
            squares,
            [turn(a) for a in (rep_vectors, rep_first, rep_second)],
            (split_vectors, split_first, split_second),
        )
        grad_norm = vectors[0][0, 0]
        new_rep, rep_first_new, rep_second_new, rep_low = (turn(a) for a in vectors[1:5])
        bias_grad = vectors[5]
        new_split, split_first_new, split_second_new, split_low = vectors[6:]
    else:
        block = grad_a0[:, ATT:]
        grad_rep = block[:, :12].T.reshape(rep_vectors.shape)
        grad_split = (
            block[:, 12:18].reshape(rows, LAYERS, 3).transpose(1, 0, 2).reshape(split_vectors.shape)
        )
        grad_norm, factor = (a[0, 0] for a in clip_factor(squares))
        clipped_rep = grad_rep * factor
        grad = jnp.stack(
            [
                jnp.concatenate([grad_a0[:, :ATT], grad_f0], axis=1),
                jnp.concatenate([grad_a1, grad_f1], axis=1),
            ]
        ).reshape(tiled_shape)
        new = adamw(*masters, grad * factor, weight_rate, weight_decay)
        new = (*new, new[0].astype(b16))
        new_split, split_first_new, split_second_new = adamw(
            split_vectors, split_first, split_second, grad_split * factor, vector_rate, 0.0
        )
        new_rep, rep_first_new, rep_second_new = adamw(
            rep_vectors, rep_first, rep_second, clipped_rep, vector_rate, 0.0
        )
        split_low, rep_low = new_split.astype(b16), new_rep.astype(b16)
        bias_grad = clipped_rep[:, 0, :]
    new_weights, weights_first_new, weights_second_new, weights_low = (
        a.reshape(shard_shape) for a in new
    )
    return (
        block_out,
        input_grad,
        grad_norm,
        new_weights,
        weights_first_new,
        weights_second_new,
        weights_low,
        new_split,
        split_first_new,
        split_second_new,
        split_low,
        new_rep,
        rep_first_new,
        rep_second_new,
        rep_low,
        bias_grad,
    )


def solution(mesh):
    rows, packed, vector = P("dp", None, None), P(None, "tensor", "dp"), P(None, None, "dp")
    return jax.shard_map(
        per_device,
        mesh=mesh,
        in_specs=(rows, rows, P("dp", None)) + (packed,) * 6 + (vector,) * 3,
        out_specs=(rows, rows, P()) + (packed,) * 8 + (vector,) * 4 + (P(None, "dp"),),
        check_vma=False,
    )
```
